256 devices in a mesh: mesh: 2 (over core), patch: 128 (over z, y, x).
Axes of the slice: x: 4, y: 4, z: 8, core: 2. Of those that a mesh axis runs over, the one named last changes fastest.
Arguments:
- nodes: bfloat16 [2, 65536, 512], P('mesh', 'patch'), may hold values from -6 to 6
- edges: bfloat16 [2, 131072, 512], P('mesh', 'patch'), may hold values from -6 to 6
- cot_nodes: bfloat16 [2, 65536, 512], P('mesh', 'patch'), may hold values from -6 to 6
- weights: bfloat16 [3584, 512], replicated, may hold values from -0.1875 to 0.1875
- edge_src: int32 [2, 131072], P('mesh', 'patch'), may hold values from 0 to 639, as said below
- edge_dst: int32 [2, 131072], P('mesh', 'patch'), may hold values from 0 to 511
- halo_rows: int32 [2, 16384], P('mesh', 'patch'), may hold values from 0 to 511
- couple_rows: int32 [2, 128, 1024], P('mesh', 'patch'), may hold values from 0 to 511
- couple_count: int32 [2, 128, 128], P('mesh', 'patch'), may hold values from 0 to 8, as said below
- couple_target: int32 [2, 128, 1024], P('mesh', 'patch'), may hold values from 0 to 511
- couple_weight: float32 [2, 128, 1024], P('mesh', 'patch'), may hold values from 0.25 to 1
Outputs:
- new_nodes: bfloat16 [2, 65536, 512], P('mesh', 'patch')
- node_grads: bfloat16 [2, 65536, 512], P('mesh', 'patch')
- edge_grads: bfloat16 [2, 131072, 512], P('mesh', 'patch')
- weight_grads: float32 [7, 262144], P(None, 'patch')
The draws below stay inside these ranges and needn't reach their ends.
Inputs may be any that keep to these rules, and one draw needn't show every extreme that they name: `edge_src`: in each patch the first 768 entries name own rows (below 512), the last 256 name rows received from neighbouring patches. `couple_count`: A sending patch has up to 4 live slots to any receiving patch, more to receiving patches within cyclic distance 3 of it; every sending patch fills all 8 slots for one receiver near it, and one receiving patch of each half gets 8 live slots from every sender. Loads of receiving patches differ.
All inputs are finite; a program needn't handle non-finite values.
Results may differ from the reference program's by a relative error of at most 0.011.
Values may be sent and summed in bfloat16 or wider, within the bound.
No kernel may reach another device: no remote copies, remote signals or barrier semaphores. Data moves between devices by JAX's collectives and lax.ppermute only.
A program may use at most 128 MiB of HBM per device.

```python
import math
import jax
import jax.numpy as jnp
from jax import lax

D = 512
NODE_DEV = 512
SLOT = 8
EDGE_DEV = 1024
HALO = 64
NODES = 65536
EDGES = 131072
N_PATCH = 128


def draw_edge_src(key, part):
    key = jax.random.fold_in(key, 1)
    key_inner, key_border = jax.random.split(key, 2)
    inner = EDGE_DEV - EDGE_DEV // 4
    local_rows = jax.random.randint(key_inner, (2, N_PATCH, inner), 0, NODE_DEV)
    border_rows = jax.random.randint(key_border, (2, N_PATCH, EDGE_DEV // 4), NODE_DEV, NODE_DEV + 2 * HALO)
    return jnp.concatenate([local_rows, border_rows], axis=2).reshape(2, N_PATCH * EDGE_DEV).astype(jnp.int32)


def draw_couple_count(key, part):
    key = jax.random.fold_in(key, 2)
    key_far, key_counts, key_pick, key_busy = jax.random.split(key, 4)
    sender = jnp.arange(N_PATCH, dtype=jnp.int32)[None, :, None]
    column = jnp.arange(N_PATCH, dtype=jnp.int32)[None, None, :]
    offset = jnp.mod(column - sender, N_PATCH)
    distance = jnp.minimum(offset, N_PATCH - offset)
    far_counts = jax.random.randint(key_far, (2, N_PATCH, N_PATCH), 0, SLOT // 2 + 1)
    near_counts = jax.random.randint(key_counts, (2, N_PATCH, N_PATCH), 1, SLOT + 1)
    counts = jnp.where(distance <= 3, near_counts, far_counts)
    shift = jax.random.randint(key_pick, (2, N_PATCH, 1), -1, 2)
    chosen = jnp.mod(sender + shift, N_PATCH)
    counts = jnp.where(column == chosen, SLOT, counts)
    busiest = jax.random.randint(key_busy, (2, 1, 1), 0, N_PATCH)
    counts = jnp.where(column == busiest, SLOT, counts)
    return counts.astype(jnp.int32)


def touch_ends(values, own_key, low, top_value):
    longest = values.shape.index(max(values.shape))
    spots = []
    for shift in (0, 1):
        where = [jax.random.randint(jax.random.fold_in(own_key, axis), (), 0, length) for axis, length in enumerate(values.shape)]
        where[longest] = (where[longest] + shift) % values.shape[longest]
        spots.append(tuple(where))
    return values.at[spots[0]].set(low).at[spots[1]].set(top_value)


def level_of(own_key, dims, pieces, smallest, high):
    factor_of, own = 1.0, jax.random.fold_in(own_key, 6)
    for dim, shards_of in pieces:
        draws = jnp.exp(jax.random.uniform(jax.random.fold_in(own, dim), (shards_of,), jnp.float32, smallest / len(pieces), high / len(pieces)))
        factor_of = factor_of * jnp.repeat(draws, dims[dim] // shards_of).reshape([-1 if axis == dim else 1 for axis in range(len(dims))])
    return factor_of


def normal_values(stream_key, extent, scale, limit, cuts=(), held_as=jnp.bfloat16):
    drawn = scale * jax.random.normal(stream_key, extent, jnp.float32)
    if cuts:
        drawn = drawn * level_of(stream_key, extent, cuts, -0.22, 0.18)
    return jnp.clip(drawn, -limit, limit).astype(held_as)


def setup_inputs(seed: int = 0) -> dict:
    seeds = jax.random.split(jax.random.key(seed), 12)
    nodes = normal_values(seeds[0], (2, NODES, D), 1.0, 6.0, ((0, 2), (1, 128)))
    edges = normal_values(seeds[1], (2, EDGES, D), 1.0, 6.0, ((0, 2), (1, 128)))
    cot_nodes = normal_values(seeds[2], (2, NODES, D), 1.0, 6.0, ((0, 2), (1, 128)))
    weights = normal_values(seeds[3], (7 * D, D), (2 * D) ** -0.5, 0.1875)
    edge_src = draw_edge_src(jax.random.fold_in(seeds[11], 71), 0)
    edge_dst = touch_ends(jax.random.randint(seeds[5], (2, EDGES), 0, NODE_DEV), jax.random.fold_in(seeds[5], 1), 0, NODE_DEV - 1).astype(jnp.int32)
    halo_rows = touch_ends(jax.random.randint(seeds[6], (2, N_PATCH * 2 * HALO), 0, NODE_DEV), jax.random.fold_in(seeds[6], 1), 0, NODE_DEV - 1).astype(jnp.int32)
    couple_rows = touch_ends(jax.random.randint(seeds[7], (2, N_PATCH, N_PATCH * SLOT), 0, NODE_DEV), jax.random.fold_in(seeds[7], 1), 0, NODE_DEV - 1).astype(jnp.int32)
    couple_count = draw_couple_count(jax.random.fold_in(seeds[11], 71), 0)
    couple_target = touch_ends(jax.random.randint(seeds[9], (2, N_PATCH, N_PATCH * SLOT), 0, NODE_DEV), jax.random.fold_in(seeds[9], 1), 0, NODE_DEV - 1).astype(jnp.int32)
    couple_weight = jnp.clip(jnp.exp(math.log(1.0) - 1.3862944 * jax.random.uniform(seeds[10], (2, N_PATCH, N_PATCH * SLOT), jnp.float32) ** level_of(seeds[10], (2, N_PATCH, N_PATCH * SLOT), ((0, 2), (1, 128)), -0.2, 0.2)), 0.25, 1.0)
    return {"nodes": nodes, "edges": edges, "cot_nodes": cot_nodes, "weights": weights, "edge_src": edge_src, "edge_dst": edge_dst, "halo_rows": halo_rows, "couple_rows": couple_rows, "couple_count": couple_count, "couple_target": couple_target, "couple_weight": couple_weight}


def silu_slope(value):
    sigma = jax.nn.sigmoid(value)
    return sigma * (1.0 + value * (1.0 - sigma))

def process_layer(nodes_own, edges_own, cotangent, source_feat, targets_edge, received, target, margin, weights):
    count, width = nodes_own.shape
    edge_first = weights[:3 * width]
    edge_second = weights[3 * width:4 * width]
    node_first = weights[4 * width:6 * width]
    node_second = weights[6 * width:]
    edge_input = jnp.concatenate([source_feat, nodes_own[targets_edge], edges_own], axis=1)
    edge_pre = jnp.dot(edge_input, edge_first, preferred_element_type=jnp.float32)
    edge_hidden = jax.nn.silu(edge_pre).astype(jnp.bfloat16)
    message = jnp.dot(edge_hidden, edge_second, preferred_element_type=jnp.float32)
    flat_received = received.reshape(-1, width).astype(jnp.float32)
    flat_target = target.reshape(-1)
    flat_margin = margin.reshape(-1)
    coupled = jax.ops.segment_sum(flat_received * flat_margin[:, None], flat_target, num_segments=count)
    pooled = (jax.ops.segment_sum(message, targets_edge, num_segments=count) + coupled).astype(jnp.bfloat16)
    node_input = jnp.concatenate([nodes_own, pooled], axis=1)
    node_pre = jnp.dot(node_input, node_first, preferred_element_type=jnp.float32)
    node_hidden = jax.nn.silu(node_pre).astype(jnp.bfloat16)
    update = jnp.dot(node_hidden, node_second, preferred_element_type=jnp.float32)
    new_nodes = (nodes_own.astype(jnp.float32) + update).astype(jnp.bfloat16)
    grad_node_second = jnp.dot(node_hidden.T, cotangent, preferred_element_type=jnp.float32)
    grad_node_pre = (jnp.dot(cotangent, node_second.T, preferred_element_type=jnp.float32) * silu_slope(node_pre)).astype(jnp.bfloat16)
    grad_node_first = jnp.dot(node_input.T, grad_node_pre, preferred_element_type=jnp.float32)
    grad_node_input = jnp.dot(grad_node_pre, node_first.T, preferred_element_type=jnp.float32)
    grad_pooled = grad_node_input[:, width:].astype(jnp.bfloat16)
    grad_message = grad_pooled[targets_edge]
    grad_edge_second = jnp.dot(edge_hidden.T, grad_message, preferred_element_type=jnp.float32)
    grad_edge_pre = (jnp.dot(grad_message, edge_second.T, preferred_element_type=jnp.float32) * silu_slope(edge_pre)).astype(jnp.bfloat16)
    grad_edge_first = jnp.dot(edge_input.T, grad_edge_pre, preferred_element_type=jnp.float32)
    grad_edge_input = jnp.dot(grad_edge_pre, edge_first.T, preferred_element_type=jnp.float32)
    edge_grads = grad_edge_input[:, 2 * width:].astype(jnp.bfloat16)
    node_part = cotangent.astype(jnp.float32) + grad_node_input[:, :width]
    node_part = node_part + jax.ops.segment_sum(grad_edge_input[:, width:2 * width], targets_edge, num_segments=count)
    source_grad = grad_edge_input[:, :width]
    returned = (grad_pooled[flat_target].astype(jnp.float32) * flat_margin[:, None]).astype(jnp.bfloat16).reshape(received.shape)
    weight_grad = jnp.concatenate([grad_edge_first, grad_edge_second, grad_node_first, grad_node_second], axis=0)
    return (new_nodes, node_part, source_grad, returned, edge_grads, weight_grad)

def reference(nodes, edges, cot_nodes, weights, edge_src, edge_dst, halo_rows, couple_rows, couple_count, couple_target, couple_weight):
    devices = 2 * N_PATCH
    node_blocks = nodes.reshape(2, N_PATCH, NODE_DEV, D)
    halo_index = halo_rows.reshape(2, N_PATCH, 2 * HALO)
    sent = jnp.take_along_axis(node_blocks, halo_index[..., None], axis=2)
    from_prev = jnp.roll(sent[:, :, HALO:], 1, axis=1)
    from_next = jnp.roll(sent[:, :, :HALO], -1, axis=1)
    extended = jnp.concatenate([node_blocks, from_prev, from_next], axis=2)
    slot_rows = couple_rows.reshape(2, N_PATCH, N_PATCH * SLOT)
    live = jnp.arange(SLOT, dtype=jnp.int32)[None, None, None, :] < couple_count[..., None]
    outgoing = jnp.take_along_axis(node_blocks, slot_rows[..., None], axis=2).reshape(2, N_PATCH, N_PATCH, SLOT, D)
    outgoing = jnp.where(live[..., None], outgoing, jnp.zeros((), outgoing.dtype))
    received = jnp.transpose(outgoing[::-1], (0, 2, 1, 3, 4))
    scale = 1.0 / math.sqrt(2 * N_PATCH * EDGE_DEV)

    def step(total, item):
        ext_rows, edge_rows, cot_rows, src_rows, dst_rows, recv_rows, target_rows, margin_rows = item
        new_nodes, node_part, source_grad, returned, edge_grads, weight_grad = process_layer(ext_rows[:NODE_DEV], edge_rows, cot_rows, ext_rows[src_rows], dst_rows, recv_rows, target_rows, margin_rows, weights)
        spread = jax.ops.segment_sum(source_grad, src_rows, num_segments=NODE_DEV + 2 * HALO)
        node_part = node_part + spread[:NODE_DEV]
        halo_grad = spread[NODE_DEV:].astype(jnp.bfloat16)
        return (total + weight_grad * scale, (new_nodes, node_part, halo_grad, returned, edge_grads))
    items = (extended.reshape(devices, NODE_DEV + 2 * HALO, D), edges.reshape(devices, EDGE_DEV, D), cot_nodes.reshape(devices, NODE_DEV, D), edge_src.reshape(devices, EDGE_DEV), edge_dst.reshape(devices, EDGE_DEV), received.reshape(devices, N_PATCH, SLOT, D), couple_target.reshape(devices, N_PATCH, SLOT), couple_weight.reshape(devices, N_PATCH, SLOT))
    total, results = lax.scan(step, jnp.zeros((7 * D, D), jnp.float32), items)
    new_nodes, node_part, halo_grad, returned, edge_grads = results
    halo_grad = halo_grad.reshape(2, N_PATCH, 2 * HALO, D)
    back_prev = jnp.roll(halo_grad[:, :, HALO:], 1, axis=1)
    back_next = jnp.roll(halo_grad[:, :, :HALO], -1, axis=1)
    halo_back = jnp.concatenate([back_prev, back_next], axis=2).astype(jnp.float32).reshape(devices, 2 * HALO, D)
    couple_back = returned.reshape(2, N_PATCH, N_PATCH, SLOT, D)
    couple_back = jnp.transpose(couple_back[::-1], (0, 2, 1, 3, 4))
    couple_back = jnp.where(live[..., None], couple_back, jnp.zeros((), couple_back.dtype))
    couple_back = couple_back.astype(jnp.float32).reshape(devices, N_PATCH * SLOT, D)
    scatter_rows = jax.vmap(lambda values, index: jax.ops.segment_sum(values, index, num_segments=NODE_DEV))
    node_grads = node_part + scatter_rows(halo_back, halo_rows.reshape(devices, 2 * HALO))
    node_grads = node_grads + scatter_rows(couple_back, couple_rows.reshape(devices, N_PATCH * SLOT))
    return (new_nodes.reshape(2, N_PATCH * NODE_DEV, D), node_grads.astype(jnp.bfloat16).reshape(2, N_PATCH * NODE_DEV, D), edge_grads.reshape(2, N_PATCH * EDGE_DEV, D), total.reshape(7, D * D))
```

```python
import math

import jax
import jax.numpy as jnp
from jax import lax
from jax.sharding import PartitionSpec as P

SLOT = 8
PLANE = 16
BF = jnp.bfloat16
F32 = jnp.float32


def from_partner(value):
    return lax.ppermute(value, "mesh", [(0, 1), (1, 0)])


def shift(value, step):
    count = lax.axis_size("patch")
    return lax.ppermute(value, "patch", [(i, (i + step) % count) for i in range(count)])


def border(low_out, high_out):
    return jnp.concatenate([shift(high_out, 1), shift(low_out, -1)], axis=0)


def route(buffer):
    return lax.all_to_all(from_partner(buffer), "patch", split_axis=0, concat_axis=0, tiled=True)


def dot(a, b):
    return jnp.dot(a, b, preferred_element_type=F32)


def dot_tn(a, b):
    return lax.dot_general(a, b, (((0,), (0,)), ((), ())), preferred_element_type=F32)


def dot_nt(a, b):
    return lax.dot_general(a, b, (((1,), (1,)), ((), ())), preferred_element_type=F32)


def onehot(index, count, value=1.0):
    columns = lax.broadcasted_iota(jnp.int32, (index.shape[0], count), 1)
    return jnp.where(index[:, None] == columns, value, 0.0).astype(BF)


def row_order(width, patches):
    depth = patches // PLANE
    fine = width // patches
    row = lax.broadcasted_iota(jnp.int32, (width, width), 0)
    column = lax.broadcasted_iota(jnp.int32, (width, width), 1)
    plane, rest = row // (depth * fine), row % (depth * fine)
    source = ((rest // fine) * PLANE + plane) * fine + rest % fine
    return (column == source).astype(BF)


def reduce_blocks(blocks, order):
    count, width = len(blocks), blocks[0].shape[1]
    half = width // 2
    patches = lax.axis_size("patch")
    depth = patches // PLANE
    fine = width // patches
    first = lax.axis_index("mesh") == 0
    stacked = jnp.stack([dot(order, block.astype(BF)).astype(BF) for block in blocks])
    left, right = stacked[:, :, :half], stacked[:, :, half:]
    own = jnp.where(first, left, right)
    crossed = from_partner(jnp.where(first, right, left))
    paired = (own.astype(F32) + crossed.astype(F32)).astype(BF)
    paired = paired.reshape(count, PLANE, depth * fine, half).transpose(1, 0, 2, 3)
    planes = [[z * PLANE + i for i in range(PLANE)] for z in range(depth)]
    spread = lax.all_to_all(
        paired, "patch", split_axis=0, concat_axis=0, axis_index_groups=planes, tiled=True
    )
    part = jnp.sum(spread.astype(F32), axis=0).astype(BF)
    part = part.reshape(count, depth, fine, half).transpose(1, 0, 2, 3)
    columns = [
        [m * patches + z * PLANE + i for m in range(2) for z in range(depth)] for i in range(PLANE)
    ]
    both = lax.all_to_all(
        jnp.concatenate([part, part], axis=0),
        ("mesh", "patch"),
        split_axis=0,
        concat_axis=0,
        axis_index_groups=columns,
        tiled=True,
    )
    total = jnp.sum(both.reshape(2, depth, count, fine, half).astype(F32), axis=1)
    return total.transpose(1, 2, 0, 3).reshape(count, fine * width)


def silu_slope(value):
    sigma = jax.nn.sigmoid(value)
    return sigma * (1.0 + value * (1.0 - sigma))


def shards(
    nodes,
    edges,
    cot_nodes,
    weights,
    edge_src,
    edge_dst,
    halo_rows,
    couple_rows,
    couple_count,
    couple_target,
    couple_weight,
):
    nodes_own = nodes[0]
    edges_own = edges[0]
    cotangent = cot_nodes[0]
    count, width = nodes_own.shape
    halo_index = halo_rows[0]
    depth = halo_index.shape[0] // 2
    patches = lax.axis_size("patch")
    scale = 1.0 / math.sqrt(2 * patches * edges_own.shape[0])
    edge_a, edge_b, edge_c = (weights[i * width : (i + 1) * width] for i in range(3))
    edge_second = weights[3 * width : 4 * width]
    node_a = weights[4 * width : 5 * width]
    node_b = weights[5 * width : 6 * width]
    node_second = weights[6 * width :]

    slot_rows = couple_rows[0, 0].reshape(patches, SLOT)
    live = lax.broadcasted_iota(jnp.int32, (patches, SLOT), 1) < couple_count[0, 0][:, None]
    live_rows = jnp.where(live, slot_rows, -1).reshape(-1)
    out_pick = onehot(live_rows, count)
    outgoing = dot(out_pick, nodes_own).astype(BF).reshape(patches, SLOT, width)
    received = route(outgoing).reshape(-1, width)
    halo_pick = onehot(halo_index, count)
    halo_out = dot(halo_pick, nodes_own).astype(BF)
    extended = jnp.concatenate([nodes_own, border(halo_out[:depth], halo_out[depth:])], axis=0)

    src_pick = onehot(edge_src[0], count + 2 * depth)
    dst_pick = onehot(edge_dst[0], count)
    source_feat = dot(src_pick, extended).astype(BF)
    target_feat = dot(dst_pick, nodes_own).astype(BF)
    edge_pre = dot(source_feat, edge_a) + dot(target_feat, edge_b) + dot(edges_own, edge_c)
    edge_hidden = (edge_pre * jax.nn.sigmoid(edge_pre)).astype(BF)
    edge_slope = silu_slope(edge_pre)
    gathered = dot_tn(dst_pick, edge_hidden).astype(BF)
    message = dot(gathered, edge_second)

    couple_pick = onehot(couple_target[0, 0], count, couple_weight[0, 0][:, None])
    pooled = (message + dot_tn(couple_pick, received)).astype(BF)
    node_pre = dot(nodes_own, node_a) + dot(pooled, node_b)
    node_hidden = (node_pre * jax.nn.sigmoid(node_pre)).astype(BF)
    new_nodes = (nodes_own.astype(F32) + dot(node_hidden, node_second)).astype(BF)
    grad_node_pre = (dot_nt(cotangent, node_second) * silu_slope(node_pre)).astype(BF)
    grad_pooled = dot_nt(grad_node_pre, node_b).astype(BF)
    node_part = cotangent.astype(F32) + dot_nt(grad_node_pre, node_a)
    returned = dot(couple_pick, grad_pooled).astype(BF).reshape(patches, SLOT, width)
    couple_back = route(returned).reshape(-1, width)

    order = row_order(width, patches)
    late = [
        dot_tn(gathered, grad_pooled) * scale,
        dot_tn(nodes_own, grad_node_pre) * scale,
        dot_tn(pooled, grad_node_pre) * scale,
        dot_tn(node_hidden, cotangent) * scale,
    ]
    late = reduce_blocks(late, order)

    grad_message = dot(dst_pick, grad_pooled).astype(BF)
    grad_edge_pre = (dot_nt(grad_message, edge_second) * edge_slope).astype(BF)
    edge_grads = dot_nt(grad_edge_pre, edge_c).astype(BF)
    by_source = dot_tn(src_pick, grad_edge_pre).astype(BF)
    by_target = dot_tn(dst_pick, grad_edge_pre).astype(BF)
    early = [
        dot_tn(extended, by_source) * scale,
        dot_tn(nodes_own, by_target) * scale,
        dot_tn(edges_own, grad_edge_pre) * scale,
    ]
    early = reduce_blocks(early, order)
    spread = dot_nt(by_source, edge_a)
    halo_grad = spread[count:].astype(BF)
    halo_back = border(halo_grad[:depth], halo_grad[depth:])
    node_total = node_part + dot_nt(by_target, edge_b) + spread[:count]
    node_total = node_total + dot_tn(halo_pick, halo_back) + dot_tn(out_pick, couple_back)
    summed = jnp.concatenate([early, late], axis=0)
    return (new_nodes[None], node_total.astype(BF)[None], edge_grads[None], summed)


def solution(mesh):
    return jax.shard_map(
        shards,
        mesh=mesh,
        in_specs=(
            P("mesh", "patch", None),
            P("mesh", "patch", None),
            P("mesh", "patch", None),
            P(),
            P("mesh", "patch"),
            P("mesh", "patch"),
            P("mesh", "patch"),
            P("mesh", "patch", None),
            P("mesh", "patch", None),
            P("mesh", "patch", None),
            P("mesh", "patch", None),
        ),
        out_specs=(
            P("mesh", "patch", None),
            P("mesh", "patch", None),
            P("mesh", "patch", None),
            P(None, "patch"),
        ),
        check_vma=False,
    )
```

```python
import math

import jax
import jax.numpy as jnp
from jax import lax
from jax.experimental import pallas as pl
from jax.experimental.pallas import tpu as pltpu
from jax.sharding import PartitionSpec as P

SLOT = 8
PLANE = 16
TILE = 256
BF = jnp.bfloat16
F32 = jnp.float32
I32 = jnp.int32
VMEM = pl.BlockSpec(memory_space=pltpu.VMEM)
SMEM = pl.BlockSpec(memory_space=pltpu.SMEM)


def dot(a, b):
    return jnp.dot(a, b, preferred_element_type=F32)


def dot_nt(a, b):
    return lax.dot_general(a, b, (((1,), (1,)), ((), ())), preferred_element_type=F32)


def column(row):
    return jnp.transpose(jnp.broadcast_to(row.astype(F32), (128, row.shape[1])))


def pick(col, count, value=None):
    base = lax.broadcasted_iota(I32, (col.shape[0], 128), 1).astype(F32)
    one = jnp.ones_like(base) if value is None else value
    parts = [jnp.where(col == base + float(k), one, 0.0).astype(BF) for k in range(0, count, 128)]
    return parts[0] if len(parts) == 1 else jnp.concatenate(parts, axis=1)


def pick_t(row, start, size, value=None):
    base = lax.broadcasted_iota(I32, (size, row.shape[1]), 0) + start
    one = jnp.ones(base.shape, F32) if value is None else jnp.broadcast_to(value, base.shape)
    return jnp.where(base == row, one, 0.0).astype(BF)


def row_order(width, patches):
    fine = width // patches
    depth = patches // PLANE
    row = lax.broadcasted_iota(I32, (width, width), 0)
    col = lax.broadcasted_iota(I32, (width, width), 1)
    plane, rest = row // (depth * fine), row % (depth * fine)
    source = ((rest // fine) * PLANE + plane) * fine + rest % fine
    return jnp.where(col == source, 1.0, 0.0).astype(BF)


def tiles(count):
    return [slice(i, i + TILE) for i in range(0, count, TILE)]


def call(kernel, args, outs, scratch=(), specs=None, flops=0):
    size = sum(math.prod(a.shape) * a.dtype.itemsize for a in list(args) + list(outs))
    return pl.pallas_call(
        kernel,
        out_shape=tuple(outs),
        in_specs=specs or [VMEM] * len(args),
        out_specs=tuple([VMEM] * len(outs)),
        scratch_shapes=list(scratch),
        compiler_params=pltpu.CompilerParams(vmem_limit_bytes=40 * 2**20),
        cost_estimate=pl.CostEstimate(flops=flops, bytes_accessed=size, transcendentals=0),
    )(*args)


def shape(dtype, *dims):
    return jax.ShapeDtypeStruct(dims, dtype)


def send_kernel(rows_ref, count_ref, halo_ref, nodes_ref, out_ref, low_ref, high_ref, live_ref):
    slots = rows_ref.shape[1]
    patches = count_ref.shape[1]
    width = nodes_ref.shape[0]
    owner = lax.broadcasted_iota(I32, (patches, slots), 0)
    place = lax.broadcasted_iota(I32, (patches, slots), 1)
    repeat = jnp.where(place // SLOT == owner, 1.0, 0.0).astype(BF)
    counts = jnp.broadcast_to(count_ref[...].astype(F32), (8, patches)).astype(BF)
    spread = dot(counts, repeat)[:1].astype(I32)
    slot = lax.broadcasted_iota(I32, (1, slots), 1) % SLOT
    live = jnp.where(slot < spread, rows_ref[...], -1)
    live_ref[...] = live
    nodes = nodes_ref[...]
    depth = low_ref.shape[0]
    halo = dot(pick(column(halo_ref[...]), width), nodes).astype(BF)
    low_ref[...] = halo[:depth]
    high_ref[...] = halo[depth:]
    col = column(live)
    for r in tiles(slots):
        out_ref[r] = dot(pick(col[r], width), nodes).astype(BF)


def edge_kernel(
    src_ref, dst_ref, nodes_ref, low_ref, high_ref, edges_ref, w_ref, slope_ref, agg_ref, msg_ref, hid_ref
):
    count, width = nodes_ref.shape
    inner = edges_ref.shape[0] - edges_ref.shape[0] // 4
    src = column(src_ref[...])
    dst = column(dst_ref[...])
    nodes = nodes_ref[...]
    halo = jnp.concatenate([low_ref[...], high_ref[...]], axis=0)
    for r in tiles(edges_ref.shape[0]):
        if r.stop <= inner:
            feat = dot(pick(src[r], count), nodes).astype(BF)
        else:
            feat = dot(pick(src[r] - float(count), halo.shape[0]), halo).astype(BF)
        own = dot(pick(dst[r], count), nodes).astype(BF)
        pre = (
            dot(feat, w_ref[:width])
            + dot(own, w_ref[width : 2 * width])
            + dot(edges_ref[r], w_ref[2 * width : 3 * width])
        )
        sigma = jax.nn.sigmoid(pre)
        hid_ref[r] = (pre * sigma).astype(BF)
        slope_ref[r] = (sigma * (1.0 + pre * (1.0 - sigma))).astype(BF)
    for r in tiles(count):
        agg = dot(pick_t(dst_ref[...], r.start, TILE), hid_ref[...]).astype(BF)
        agg_ref[r] = agg
        msg_ref[r] = dot(agg, w_ref[3 * width : 4 * width])


def node_kernel(
    target_ref, margin_ref, nodes_ref, cot_ref, msg_ref, recv_ref, w_ref,
    new_ref, pooled_ref, hid_ref, gpre_ref, gpool_ref, part_ref, ret_ref,
):
    count, width = nodes_ref.shape
    node_a = w_ref[4 * width : 5 * width]
    node_b = w_ref[5 * width : 6 * width]
    second = w_ref[6 * width :]
    target, margin = target_ref[...], margin_ref[...]
    for r in tiles(count):
        coupled = dot(pick_t(target, r.start, TILE, margin), recv_ref[...])
        pooled = (msg_ref[r] + coupled).astype(BF)
        pooled_ref[r] = pooled
        nodes = nodes_ref[r]
        pre = dot(nodes, node_a) + dot(pooled, node_b)
        sigma = jax.nn.sigmoid(pre)
        hidden = (pre * sigma).astype(BF)
        hid_ref[r] = hidden
        slope = sigma * (1.0 + pre * (1.0 - sigma))
        cot = cot_ref[r]
        gpre = (dot_nt(cot, second) * slope).astype(BF)
        gpre_ref[r] = gpre
        gpool_ref[r] = dot_nt(gpre, node_b).astype(BF)
        new_ref[r] = (nodes.astype(F32) + dot(hidden, second)).astype(BF)
        part_ref[r] = cot.astype(F32) + dot_nt(gpre, node_a)
    col, weight = column(target), column(margin)
    gpool = gpool_ref[...]
    for r in tiles(recv_ref.shape[0]):
        ret_ref[r] = dot(pick(col[r], count, weight[r]), gpool).astype(BF)


def put(own_ref, send_ref, index, value, first):
    half = value.shape[1] // 2
    planes, fine = own_ref.shape[0], own_ref.shape[2]
    value = value.reshape(planes, fine, 2 * half)
    left, right = value[:, :, :half], value[:, :, half:]
    own_ref[:, index] = jnp.where(first, left, right).astype(BF)
    send_ref[:, index] = jnp.where(first, right, left).astype(BF)


def node_grad_kernel(
    side_ref, agg_ref, nodes_ref, pooled_ref, hid_ref, gpre_ref, gpool_ref, cot_ref, own_ref, send_ref,
    *, patches, scale
):
    order = row_order(nodes_ref.shape[1], patches)
    first = side_ref[0] == 0
    pairs = [(agg_ref, gpool_ref), (nodes_ref, gpre_ref), (pooled_ref, gpre_ref), (hid_ref, cot_ref)]
    for index, (left, right) in enumerate(pairs):
        turned = dot_nt(order, left[...]).astype(BF)
        put(own_ref, send_ref, index, dot(turned, right[...]) * scale, first)


def edge_grad_kernel(
    side_ref, src_ref, dst_ref, nodes_ref, low_ref, high_ref, edges_ref, slope_ref, gpool_ref, w_ref,
    own_ref, send_ref, gpre_ref, bysrc_ref, bydst_ref, glow_ref, ghigh_ref,
    *, patches, scale
):
    count, width = nodes_ref.shape
    inner = edges_ref.shape[0] - edges_ref.shape[0] // 4
    depth = low_ref.shape[0]
    first = side_ref[0] == 0
    gpool = gpool_ref[...]
    second = w_ref[3 * width : 4 * width]
    dst_row, src_row = dst_ref[...], src_ref[...]
    dst = column(dst_row)
    for r in tiles(edges_ref.shape[0]):
        message = dot(pick(dst[r], count), gpool).astype(BF)
        gpre_ref[r] = (dot_nt(message, second) * slope_ref[r].astype(F32)).astype(BF)
    order = row_order(width, patches)
    turned = dot_nt(order, edges_ref[...]).astype(BF)
    put(own_ref, send_ref, 2, dot(turned, gpre_ref[...]) * scale, first)
    for r in tiles(count):
        bydst_ref[r] = dot(pick_t(dst_row, r.start, TILE), gpre_ref[...]).astype(BF)
        bysrc_ref[r] = dot(pick_t(src_row[:, :inner], r.start, TILE), gpre_ref[:inner]).astype(BF)
    halo = dot(pick_t(src_row[:, inner:], count, 2 * depth), gpre_ref[inner:]).astype(BF)
    turned = dot_nt(order, nodes_ref[...]).astype(BF)
    put(own_ref, send_ref, 1, dot(turned, bydst_ref[...]) * scale, first)
    rim = dot_nt(order, jnp.concatenate([low_ref[...], high_ref[...]], axis=0)).astype(BF)
    put(own_ref, send_ref, 0, (dot(turned, bysrc_ref[...]) + dot(rim, halo)) * scale, first)
    back = dot_nt(halo, w_ref[:width]).astype(BF)
    glow_ref[...] = back[:depth]
    ghigh_ref[...] = back[depth:]


def edge_rest_kernel(gpre_ref, bysrc_ref, bydst_ref, part_ref, w_ref, edge_ref, total_ref):
    count, width = bysrc_ref.shape
    for r in tiles(gpre_ref.shape[0]):
        edge_ref[r] = dot_nt(gpre_ref[r], w_ref[2 * width : 3 * width]).astype(BF)
    for r in tiles(count):
        total_ref[r] = (
            part_ref[r]
            + dot_nt(bysrc_ref[r], w_ref[:width])
            + dot_nt(bydst_ref[r], w_ref[width : 2 * width])
        )


def last_kernel(live_ref, halo_ref, total_ref, low_ref, high_ref, back_ref, out_ref):
    halo_back = jnp.concatenate([low_ref[...], high_ref[...]], axis=0)
    for r in tiles(total_ref.shape[0]):
        out_ref[r] = (
            total_ref[r]
            + dot(pick_t(halo_ref[...], r.start, TILE), halo_back)
            + dot(pick_t(live_ref[...], r.start, TILE), back_ref[...])
        ).astype(BF)


def from_partner(value):
    return lax.ppermute(value, "mesh", [(0, 1), (1, 0)])


def shift(value, step):
    count = lax.axis_size("patch")
    return lax.ppermute(value, "patch", [(i, (i + step) % count) for i in range(count)])


def route(buffer):
    rows, width = buffer.shape
    patches = lax.axis_size("patch")
    crossed = from_partner(buffer).reshape(patches, rows // patches, width)
    routed = lax.all_to_all(crossed, "patch", split_axis=0, concat_axis=0, tiled=True)
    return routed.reshape(rows, width)


def reduce_blocks(own, send):
    planes, count, rest, half = own.shape
    patches = lax.axis_size("patch")
    depth = patches // PLANE
    fine = rest // depth
    paired = (own.astype(F32) + from_partner(send).astype(F32)).astype(BF)
    groups = [[z * PLANE + i for i in range(PLANE)] for z in range(depth)]
    spread = lax.all_to_all(
        paired, "patch", split_axis=0, concat_axis=0, axis_index_groups=groups, tiled=True
    )
    part = jnp.sum(spread.astype(F32), axis=0).astype(BF)
    part = part.reshape(count, depth, fine, half).transpose(1, 0, 2, 3)
    columns = [
        [m * patches + z * PLANE + i for m in range(2) for z in range(depth)] for i in range(PLANE)
    ]
    both = lax.all_to_all(
        jnp.concatenate([part, part], axis=0),
        ("mesh", "patch"),
        split_axis=0,
        concat_axis=0,
        axis_index_groups=columns,
        tiled=True,
    )
    total = jnp.sum(both.reshape(2, depth, count, fine, half).astype(F32), axis=1)
    return total.transpose(1, 2, 0, 3).reshape(count, fine * 2 * half)


def shards(
    nodes,
    edges,
    cot_nodes,
    weights,
    edge_src,
    edge_dst,
    halo_rows,
    couple_rows,
    couple_count,
    couple_target,
    couple_weight,
):
    nodes_own = nodes[0]
    edges_own = edges[0]
    cotangent = cot_nodes[0]
    count, width = nodes_own.shape
    edge_count = edges_own.shape[0]
    depth = halo_rows.shape[1] // 2
    patches = lax.axis_size("patch")
    slots = couple_rows.shape[2]
    scale = 1.0 / math.sqrt(2 * patches * edge_count)
    side = lax.axis_index("mesh").astype(I32).reshape(1)
    target, margin = couple_target[0], couple_weight[0]
    unit = 2 * width * width

    outgoing, low_out, high_out, live = call(
        send_kernel,
        (couple_rows[0], couple_count[0], halo_rows, nodes_own),
        (shape(BF, slots, width), shape(BF, depth, width), shape(BF, depth, width), shape(I32, 1, slots)),
        flops=(slots + 2 * depth) * unit,
    )
    low, high = shift(high_out, 1), shift(low_out, -1)
    received = route(outgoing)
    slope, agg, message = call(
        edge_kernel,
        (edge_src, edge_dst, nodes_own, low, high, edges_own, weights),
        (shape(BF, edge_count, width), shape(BF, count, width), shape(F32, count, width)),
        scratch=(pltpu.VMEM((edge_count, width), BF),),
        flops=edge_count * 6 * unit,
    )
    square = shape(BF, count, width)
    new_nodes, pooled, hidden, grad_pre, grad_pooled, part, returned = call(
        node_kernel,
        (target, margin, nodes_own, cotangent, message, received, weights),
        (square, square, square, square, square, shape(F32, count, width), shape(BF, slots, width)),
        flops=count * 10 * unit,
    )
    couple_back = route(returned)
    grad_shape = lambda blocks: shape(BF, PLANE, blocks, width // PLANE, width // 2)
    own, send = call(
        lambda *refs: node_grad_kernel(*refs, patches=patches, scale=scale),
        (side, agg, nodes_own, pooled, hidden, grad_pre, grad_pooled, cotangent),
        (grad_shape(4), grad_shape(4)),
        specs=[SMEM] + [VMEM] * 7,
        flops=count * 8 * unit,
    )
    late = reduce_blocks(own, send)
    own, send, grad_edge_pre, by_source, by_target, grad_low, grad_high = call(
        lambda *refs: edge_grad_kernel(*refs, patches=patches, scale=scale),
        (side, edge_src, edge_dst, nodes_own, low, high, edges_own, slope, grad_pooled, weights),
        (
            grad_shape(3), grad_shape(3), shape(BF, edge_count, width), square, square,
            shape(BF, depth, width), shape(BF, depth, width),
        ),
        specs=[SMEM] + [VMEM] * 9,
        flops=edge_count * 8 * unit,
    )
    early = reduce_blocks(own, send)
    back_low, back_high = shift(grad_high, 1), shift(grad_low, -1)
    edge_grads, total = call(
        edge_rest_kernel,
        (grad_edge_pre, by_source, by_target, part, weights),
        (shape(BF, edge_count, width), shape(F32, count, width)),
        flops=edge_count * 2 * unit,
    )
    (node_grads,) = call(
        last_kernel,
        (live, halo_rows, total, back_low, back_high, couple_back),
        (square,),
        flops=count * 2 * unit,
    )
    summed = jnp.concatenate([early, late], axis=0)
    return (new_nodes[None], node_grads[None], edge_grads[None], summed)


def solution(mesh):
    return jax.shard_map(
        shards,
        mesh=mesh,
        in_specs=(
            P("mesh", "patch", None),
            P("mesh", "patch", None),
            P("mesh", "patch", None),
            P(),
            P("mesh", "patch"),
            P("mesh", "patch"),
            P("mesh", "patch"),
            P("mesh", "patch", None),
            P("mesh", "patch", None),
            P("mesh", "patch", None),
            P("mesh", "patch", None),
        ),
        out_specs=(
            P("mesh", "patch", None),
            P("mesh", "patch", None),
            P("mesh", "patch", None),
            P(None, "patch"),
        ),
        check_vma=False,
    )
```

```python
import math

import jax
import jax.numpy as jnp
from jax import lax
from jax.experimental import pallas as pl
from jax.experimental.pallas import tpu as pltpu
from jax.sharding import PartitionSpec as P

SLOT = 8
RING = 4
PLANE = RING * RING
TILE = 256
BF = jnp.bfloat16
F32 = jnp.float32
I32 = jnp.int32
VMEM = pl.BlockSpec(memory_space=pltpu.VMEM)
SMEM = pl.BlockSpec(memory_space=pltpu.SMEM)


def dot(a, b):
    return jnp.dot(a, b, preferred_element_type=F32)


def dot_nt(a, b):
    return lax.dot_general(a, b, (((1,), (1,)), ((), ())), preferred_element_type=F32)


def column(row):
    return jnp.transpose(jnp.broadcast_to(row.astype(F32), (128, row.shape[1])))


def pick(col, count, value=None):
    base = lax.broadcasted_iota(I32, (col.shape[0], 128), 1).astype(F32)
    one = jnp.ones_like(base) if value is None else value
    parts = [jnp.where(col == base + float(k), one, 0.0).astype(BF) for k in range(0, count, 128)]
    return parts[0] if len(parts) == 1 else jnp.concatenate(parts, axis=1)


def pick_t(row, start, size, value=None):
    base = lax.broadcasted_iota(I32, (size, row.shape[1]), 0) + start
    one = jnp.ones(base.shape, F32) if value is None else jnp.broadcast_to(value, base.shape)
    return jnp.where(base == row, one, 0.0).astype(BF)


def row_order(place, width, patches):
    fine = width // patches
    depth = patches // PLANE
    row = lax.broadcasted_iota(I32, (width, width), 0)
    col = lax.broadcasted_iota(I32, (width, width), 1)
    dx, dy = row // (width // RING), (row // (width // PLANE)) % RING
    dz, offset = (row // fine) % depth, row % fine
    x, y = place % RING, (place // RING) % RING
    patch = dz * PLANE + (y + dy) % RING * RING + (x + dx) % RING
    return jnp.where(col == patch * fine + offset, 1.0, 0.0).astype(BF)


def tiles(count):
    return [slice(i, i + TILE) for i in range(0, count, TILE)]


class Far:
    def __init__(self, array, start=0, size=None):
        self.array = array
        self.start = start
        self.size = array.shape[0] if size is None else size


class Fetched:
    def __init__(self, copy, buffer):
        self.copy, self.buffer, self.waited = copy, buffer, False
        self.shape = buffer.shape

    def __getitem__(self, index):
        if not self.waited:
            self.copy.wait()
            self.waited = True
        return self.buffer[index]


def call(kernel, args, outs, scratch=(), flops=0):
    far = [i for i, a in enumerate(args) if isinstance(a, Far)]
    arrays = [a.array if isinstance(a, Far) else a for a in args]
    buffers = [
        pltpu.VMEM((args[i].size,) + args[i].array.shape[1:], args[i].array.dtype) for i in far
    ]
    specs = [
        pl.BlockSpec(memory_space=pl.ANY)
        if isinstance(a, Far)
        else (SMEM if a.dtype == I32 and a.ndim == 1 else VMEM)
        for a in args
    ]
    ins, made = len(args), len(args) + len(outs)

    def body(*refs):
        held = refs[made : made + len(far)]
        refs_in = list(refs[:ins])
        if far:
            sems = refs[made + len(far)]
        for k, i in enumerate(far):
            source = refs_in[i].at[args[i].start : args[i].start + args[i].size]
            copy = pltpu.make_async_copy(source, held[k], sems.at[k])
            copy.start()
            refs_in[i] = Fetched(copy, held[k])
        kernel(*refs_in, *refs[ins:made], *refs[made + len(far) + (1 if far else 0) :])
        for i in far:
            if not refs_in[i].waited:
                refs_in[i].copy.wait()

    size = sum(math.prod(a.shape) * a.dtype.itemsize for a in arrays + list(outs))
    extra = buffers + ([pltpu.SemaphoreType.DMA((len(far),))] if far else [])
    return pl.pallas_call(
        body,
        out_shape=tuple(outs),
        in_specs=specs,
        out_specs=tuple([VMEM] * len(outs)),
        scratch_shapes=extra + list(scratch),
        compiler_params=pltpu.CompilerParams(vmem_limit_bytes=16 * 2**20),
        cost_estimate=pl.CostEstimate(flops=flops, bytes_accessed=size, transcendentals=0),
    )(*arrays)


def shape(dtype, *dims):
    return jax.ShapeDtypeStruct(dims, dtype)


def send_kernel(rows_ref, count_ref, halo_ref, nodes_ref, out_ref, low_ref, high_ref, live_ref):
    slots = rows_ref.shape[1]
    patches = count_ref.shape[1]
    width = nodes_ref.shape[0]
    owner = lax.broadcasted_iota(I32, (patches, slots), 0)
    place = lax.broadcasted_iota(I32, (patches, slots), 1)
    repeat = jnp.where(place // SLOT == owner, 1.0, 0.0).astype(BF)
    counts = jnp.broadcast_to(count_ref[...].astype(F32), (8, patches)).astype(BF)
    spread = dot(counts, repeat)[:1].astype(I32)
    slot = lax.broadcasted_iota(I32, (1, slots), 1) % SLOT
    live = jnp.where(slot < spread, rows_ref[...], -1)
    live_ref[...] = live
    nodes = nodes_ref[...]
    depth = low_ref.shape[0]
    halo = dot(pick(column(halo_ref[...]), width), nodes).astype(BF)
    low_ref[...] = halo[:depth]
    high_ref[...] = halo[depth:]
    col = column(live)
    for r in tiles(slots):
        out_ref[r] = dot(pick(col[r], width), nodes).astype(BF)


def edge_kernel(
    dst_ref, nodes_ref, wb_ref, src_ref, low_ref, high_ref, wa_ref, edges_ref, wc_ref, second_ref,
    slope_ref, agg_ref, msg_ref, hid_ref,
):
    count, width = nodes_ref.shape
    inner = edges_ref.shape[0] - edges_ref.shape[0] // 4
    dst = column(dst_ref[...])
    nodes = nodes_ref[...]
    src = column(src_ref[...])
    halo = jnp.concatenate([low_ref[...], high_ref[...]], axis=0)
    for r in tiles(edges_ref.shape[0]):
        if r.stop <= inner:
            feat = dot(pick(src[r], count), nodes).astype(BF)
        else:
            feat = dot(pick(src[r] - float(count), halo.shape[0]), halo).astype(BF)
        own = dot(pick(dst[r], count), nodes).astype(BF)
        pre = dot(own, wb_ref[...]) + dot(feat, wa_ref[...]) + dot(edges_ref[r], wc_ref[...])
        sigma = jax.nn.sigmoid(pre)
        hid_ref[r] = (pre * sigma).astype(BF)
        slope_ref[r] = (sigma * (1.0 + pre * (1.0 - sigma))).astype(BF)
    for r in tiles(count):
        agg = dot(pick_t(dst_ref[...], r.start, TILE), hid_ref[...]).astype(BF)
        agg_ref[r] = agg
        msg_ref[r] = dot(agg, second_ref[...])


def node_kernel(
    target_ref, margin_ref, nodes_ref, a_ref, b_ref, cot_ref, second_ref, msg_ref, recv_ref,
    new_ref, pooled_ref, hid_ref, gpre_ref, gpool_ref, part_ref, ret_ref,
):
    count, width = nodes_ref.shape
    target, margin = target_ref[...], margin_ref[...]
    for r in tiles(count):
        coupled = dot(pick_t(target, r.start, TILE, margin), recv_ref[...])
        pooled = (msg_ref[r] + coupled).astype(BF)
        pooled_ref[r] = pooled
        nodes = nodes_ref[r]
        pre = dot(nodes, a_ref[...]) + dot(pooled, b_ref[...])
        sigma = jax.nn.sigmoid(pre)
        hidden = (pre * sigma).astype(BF)
        hid_ref[r] = hidden
        slope = sigma * (1.0 + pre * (1.0 - sigma))
        cot = cot_ref[r]
        gpre = (dot_nt(cot, second_ref[...]) * slope).astype(BF)
        gpre_ref[r] = gpre
        gpool_ref[r] = dot_nt(gpre, b_ref[...]).astype(BF)
        new_ref[r] = (nodes.astype(F32) + dot(hidden, second_ref[...])).astype(BF)
        part_ref[r] = cot.astype(F32) + dot_nt(gpre, a_ref[...])
    col, weight = column(target), column(margin)
    gpool = gpool_ref[...]
    for r in tiles(recv_ref.shape[0]):
        ret_ref[r] = dot(pick(col[r], count, weight[r]), gpool).astype(BF)


def put(own_ref, send_ref, index, value, first):
    half = value.shape[1] // 2
    lane = half // 2
    step = value.shape[0] // RING
    fine = step // RING
    own = jnp.where(first, value[:, :half], value[:, half:]).astype(BF)
    send = jnp.where(first, value[:, half:], value[:, :half]).astype(BF)
    for ref, part in ((own_ref, own), (send_ref, send)):
        for i in range(RING):
            ref[0, i, index] = part[i * step : (i + 1) * step, :lane]
            for j in range(RING):
                start = i * step + j * fine
                ref[1, j, index, i * fine : (i + 1) * fine] = part[start : start + fine, lane:]


def node_grad_kernel(
    side_ref, agg_ref, nodes_ref, pooled_ref, hid_ref, gpre_ref, gpool_ref, cot_ref, own_ref, send_ref,
    *, patches, scale
):
    order = row_order(side_ref[1], nodes_ref.shape[1], patches)
    first = side_ref[0] == 0
    pairs = [(agg_ref, gpool_ref), (nodes_ref, gpre_ref), (pooled_ref, gpre_ref), (hid_ref, cot_ref)]
    for index, (left, right) in enumerate(pairs):
        turned = dot_nt(order, left[...]).astype(BF)
        put(own_ref, send_ref, index, dot(turned, right[...]) * scale, first)


def edge_grad_kernel(
    side_ref, dst_ref, second_ref, edges_ref, src_ref, nodes_ref, wa_ref, low_ref, high_ref, slope_ref, gpool_ref,
    own_ref, send_ref, gpre_ref, bysrc_ref, bydst_ref, glow_ref, ghigh_ref,
    *, patches, scale
):
    count, width = nodes_ref.shape
    inner = edges_ref.shape[0] - edges_ref.shape[0] // 4
    depth = low_ref.shape[0]
    first = side_ref[0] == 0
    gpool = gpool_ref[...]
    second = second_ref[...]
    dst_row, src_row = dst_ref[...], src_ref[...]
    dst = column(dst_row)
    for r in tiles(edges_ref.shape[0]):
        message = dot(pick(dst[r], count), gpool).astype(BF)
        gpre_ref[r] = (dot_nt(message, second) * slope_ref[r].astype(F32)).astype(BF)
    order = row_order(side_ref[1], width, patches)
    turned = dot_nt(order, edges_ref[...]).astype(BF)
    put(own_ref, send_ref, 2, dot(turned, gpre_ref[...]) * scale, first)
    for r in tiles(count):
        bydst_ref[r] = dot(pick_t(dst_row, r.start, TILE), gpre_ref[...]).astype(BF)
        bysrc_ref[r] = dot(pick_t(src_row[:, :inner], r.start, TILE), gpre_ref[:inner]).astype(BF)
    halo = dot(pick_t(src_row[:, inner:], count, 2 * depth), gpre_ref[inner:]).astype(BF)
    turned = dot_nt(order, nodes_ref[...]).astype(BF)
    put(own_ref, send_ref, 1, dot(turned, bydst_ref[...]) * scale, first)
    rim = dot_nt(order, jnp.concatenate([low_ref[...], high_ref[...]], axis=0)).astype(BF)
    put(own_ref, send_ref, 0, (dot(turned, bysrc_ref[...]) + dot(rim, halo)) * scale, first)
    back = dot_nt(halo, wa_ref[...]).astype(BF)
    glow_ref[...] = back[:depth]
    ghigh_ref[...] = back[depth:]


def edge_rest_kernel(
    wc_ref, wa_ref, wb_ref, gpre_ref, bysrc_ref, bydst_ref, part_ref, edge_ref, total_ref
):
    count, width = bysrc_ref.shape
    for r in tiles(gpre_ref.shape[0]):
        edge_ref[r] = dot_nt(gpre_ref[r], wc_ref[...]).astype(BF)
    for r in tiles(count):
        total_ref[r] = (
            part_ref[r]
            + dot_nt(bysrc_ref[r], wa_ref[...])
            + dot_nt(bydst_ref[r], wb_ref[...])
        )


def last_kernel(live_ref, halo_ref, total_ref, low_ref, high_ref, back_ref, out_ref):
    halo_back = jnp.concatenate([low_ref[...], high_ref[...]], axis=0)
    for r in tiles(total_ref.shape[0]):
        out_ref[r] = (
            total_ref[r]
            + dot(pick_t(halo_ref[...], r.start, TILE), halo_back)
            + dot(pick_t(live_ref[...], r.start, TILE), back_ref[...])
        ).astype(BF)


def from_partner(value):
    return lax.ppermute(value, "mesh", [(0, 1), (1, 0)])


def shift(value, step):
    count = lax.axis_size("patch")
    return lax.ppermute(value, "patch", [(i, (i + step) % count) for i in range(count)])


def route(crossed):
    rows, width = crossed.shape
    patches = lax.axis_size("patch")
    crossed = crossed.reshape(patches, rows // patches, width)
    routed = lax.all_to_all(crossed, "patch", split_axis=0, concat_axis=0, tiled=True)
    return routed.reshape(rows, width)


def hop(value, dy=0, dx=0):
    pairs = []
    for p in range(lax.axis_size("patch")):
        z, y, x = p // PLANE, p // RING % RING, p % RING
        pairs.append((p, z * PLANE + (y + dy) % RING * RING + (x + dx) % RING))
    return lax.ppermute(value, "patch", pairs)


def join_kernel(own_a, other_a, own_b, other_b, *outs):
    for index, out in enumerate(outs):
        c, d = index // RING, index % RING
        base = 0
        for own, other in ((own_a, other_a), (own_b, other_b)):
            blocks = own.shape[2]
            joined = own[c, d].astype(F32) + other[c, d].astype(F32)
            out[base : base + blocks] = joined.astype(BF)
            base += blocks


def total_of(refs):
    total = refs[0][...].astype(F32)
    for ref in refs[1:]:
        total = total + ref[...].astype(F32)
    return total


def plane_kernel(*refs):
    for c in range(2):
        total = total_of(refs[c * RING : (c + 1) * RING])
        fine = total.shape[1] // RING
        for d in range(RING):
            refs[(2 + c) * RING + d][...] = total[:, d * fine : (d + 1) * fine].astype(BF)


def depth_kernel(*refs):
    ins, (out, hold) = refs[: 2 * RING], refs[2 * RING :]
    depth = hold.shape[0]
    hold[...] = jnp.zeros(hold.shape, F32)
    for c in range(2):
        total = total_of(ins[c * RING : (c + 1) * RING])
        blocks, rows, lane = total.shape
        fine = rows // depth
        for block in range(blocks):
            for d in range(depth):
                hold[d, block * fine : (block + 1) * fine, c * lane : (c + 1) * lane] = total[
                    block, d * fine : (d + 1) * fine
                ]
    value = hold[...].astype(BF)
    out[:depth] = value
    out[depth:] = value


def finish_kernel(in_ref, out_ref):
    count, _, lane = in_ref.shape
    depth = count // 2
    for side in range(2):
        total = in_ref[side * depth].astype(F32)
        for d in range(1, depth):
            total = total + in_ref[side * depth + d].astype(F32)
        out_ref[:, side * lane : (side + 1) * lane] = total[: out_ref.shape[0]]


def weight_sums(own_a, other_a, own_b, other_b):
    patches = lax.axis_size("patch")
    depth = patches // PLANE
    rows, lane = own_a.shape[3:]
    blocks = own_a.shape[2] + own_b.shape[2]
    fine = rows // RING // depth
    piece = shape(BF, blocks, rows, lane)
    small = shape(BF, blocks, rows // RING, lane)
    pieces = call(join_kernel, (own_a, other_a, own_b, other_b), (piece,) * (2 * RING))
    for kernel, axes in ((plane_kernel, ("dx", "dy")), (None, ("dy", "dx"))):
        pieces = [
            pieces[c * RING + d] if d == 0 else hop(pieces[c * RING + d], **{axis: d})
            for c, axis in enumerate(axes)
            for d in range(RING)
        ]
        if kernel is not None:
            pieces = call(kernel, pieces, (small,) * (2 * RING))
    padded = (blocks * fine + 15) // 16 * 16
    (part,) = call(
        depth_kernel,
        pieces,
        (shape(BF, 2 * depth, padded, 2 * lane),),
        scratch=(pltpu.VMEM((depth, padded, 2 * lane), F32),),
    )
    columns = [
        [m * patches + z * PLANE + i for m in range(2) for z in range(depth)] for i in range(PLANE)
    ]
    both = lax.all_to_all(
        part, ("mesh", "patch"), split_axis=0, concat_axis=0, axis_index_groups=columns, tiled=True
    )
    (total,) = call(finish_kernel, (both,), (shape(F32, blocks * fine, 4 * lane),))
    return total.reshape(blocks, fine * 4 * lane)


def shards(
    nodes,
    edges,
    cot_nodes,
    weights,
    edge_src,
    edge_dst,
    halo_rows,
    couple_rows,
    couple_count,
    couple_target,
    couple_weight,
):
    nodes_own = nodes[0]
    edges_own = edges[0]
    cotangent = cot_nodes[0]
    count, width = nodes_own.shape
    edge_count = edges_own.shape[0]
    depth = halo_rows.shape[1] // 2
    patches = lax.axis_size("patch")
    slots = couple_rows.shape[2]
    scale = 1.0 / math.sqrt(2 * patches * edge_count)
    side = jnp.stack([lax.axis_index("mesh"), lax.axis_index("patch")]).astype(I32)
    target, margin = couple_target[0], couple_weight[0]
    unit = 2 * width * width

    def weight(block):
        return Far(weights, block * width, width)

    outgoing, low_out, high_out, live = call(
        send_kernel,
        (Far(couple_rows[0]), Far(couple_count[0]), Far(halo_rows), Far(nodes_own)),
        (shape(BF, slots, width), shape(BF, depth, width), shape(BF, depth, width), shape(I32, 1, slots)),
        flops=(slots + 2 * depth) * unit,
    )
    crossed = from_partner(outgoing)
    low, high = shift(high_out, 1), shift(low_out, -1)
    crossed, low, high = lax.optimization_barrier((crossed, low, high))
    received = route(crossed)
    slope, agg, message = call(
        edge_kernel,
        (
            Far(edge_dst), Far(nodes_own), weight(1), Far(edge_src), low, high, weight(0),
            Far(edges_own), weight(2), weight(3),
        ),
        (shape(BF, edge_count, width), shape(BF, count, width), shape(F32, count, width)),
        scratch=(pltpu.VMEM((edge_count, width), BF),),
        flops=edge_count * 6 * unit,
    )
    square = shape(BF, count, width)
    new_nodes, pooled, hidden, grad_pre, grad_pooled, part, returned = call(
        node_kernel,
        (
            Far(target), Far(margin), Far(nodes_own), weight(4), weight(5), Far(cotangent), weight(6),
            message, received,
        ),
        (square, square, square, square, square, shape(F32, count, width), shape(BF, slots, width)),
        flops=count * 10 * unit,
    )
    crossed_back = from_partner(returned)
    couple_back = route(crossed_back)
    grad_shape = lambda blocks: shape(BF, 2, RING, blocks, width // RING, width // 4)
    own_b, send_b = call(
        lambda *refs: node_grad_kernel(*refs, patches=patches, scale=scale),
        (side, agg, Far(nodes_own), pooled, hidden, grad_pre, grad_pooled, Far(cotangent)),
        (grad_shape(4), grad_shape(4)),
        flops=count * 8 * unit,
    )
    other_b = from_partner(send_b)
    grad_pooled, other_b = lax.optimization_barrier((grad_pooled, other_b))
    own_a, send_a, grad_edge_pre, by_source, by_target, grad_low, grad_high = call(
        lambda *refs: edge_grad_kernel(*refs, patches=patches, scale=scale),
        (
            side, Far(edge_dst), weight(3), Far(edges_own), Far(edge_src), Far(nodes_own), weight(0),
            low, high, slope, grad_pooled,
        ),
        (
            grad_shape(3), grad_shape(3), shape(BF, edge_count, width), square, square,
            shape(BF, depth, width), shape(BF, depth, width),
        ),
        flops=edge_count * 8 * unit,
    )
    summed = weight_sums(own_a, from_partner(send_a), own_b, other_b)
    back_low, back_high = shift(grad_high, 1), shift(grad_low, -1)
    edge_grads, total = call(
        edge_rest_kernel,
        (weight(2), weight(0), weight(1), grad_edge_pre, by_source, by_target, part),
        (shape(BF, edge_count, width), shape(F32, count, width)),
        flops=edge_count * 2 * unit,
    )
    (node_grads,) = call(
        last_kernel,
        (live, Far(halo_rows), total, back_low, back_high, couple_back),
        (square,),
        flops=count * 2 * unit,
    )
    return (new_nodes[None], node_grads[None], edge_grads[None], summed)


def solution(mesh):
    return jax.shard_map(
        shards,
        mesh=mesh,
        in_specs=(
            P("mesh", "patch", None),
            P("mesh", "patch", None),
            P("mesh", "patch", None),
            P(),
            P("mesh", "patch"),
            P("mesh", "patch"),
            P("mesh", "patch"),
            P("mesh", "patch", None),
            P("mesh", "patch", None),
            P("mesh", "patch", None),
            P("mesh", "patch", None),
        ),
        out_specs=(
            P("mesh", "patch", None),
            P("mesh", "patch", None),
            P("mesh", "patch", None),
            P(None, "patch"),
        ),
        check_vma=False,
    )
```

```python
import math

import jax
import jax.numpy as jnp
from jax import lax
from jax.experimental import pallas as pl
from jax.experimental.pallas import tpu as pltpu
from jax.sharding import PartitionSpec as P

SLOT = 8
RING = 4
PLANE = RING * RING
TILE = 256
BF = jnp.bfloat16
F32 = jnp.float32
I32 = jnp.int32
VMEM = pl.BlockSpec(memory_space=pltpu.VMEM)
SMEM = pl.BlockSpec(memory_space=pltpu.SMEM)


def dot(a, b):
    return jnp.dot(a, b, preferred_element_type=F32)


def dot_nt(a, b):
    return lax.dot_general(a, b, (((1,), (1,)), ((), ())), preferred_element_type=F32)


def column(row):
    return jnp.transpose(jnp.broadcast_to(row.astype(F32), (128, row.shape[1])))


def pick(col, count, value=None):
    base = lax.broadcasted_iota(I32, (col.shape[0], 128), 1).astype(F32)
    one = jnp.ones_like(base) if value is None else value
    parts = [jnp.where(col == base + float(k), one, 0.0).astype(BF) for k in range(0, count, 128)]
    return parts[0] if len(parts) == 1 else jnp.concatenate(parts, axis=1)


def pick_t(row, start, size, value=None):
    base = lax.broadcasted_iota(I32, (size, row.shape[1]), 0) + start
    one = jnp.ones(base.shape, F32) if value is None else jnp.broadcast_to(value, base.shape)
    return jnp.where(base == row, one, 0.0).astype(BF)


def row_order(place, width, patches):
    fine = width // patches
    depth = patches // PLANE
    row = lax.broadcasted_iota(I32, (width, width), 0)
    col = lax.broadcasted_iota(I32, (width, width), 1)
    dx, dy = row // (width // RING), (row // (width // PLANE)) % RING
    dz, offset = (row // fine) % depth, row % fine
    x, y, z = place % RING, (place // RING) % RING, place // PLANE
    patch = (z + dz) % depth * PLANE + (y + dy) % RING * RING + (x + dx) % RING
    return jnp.where(col == patch * fine + offset, 1.0, 0.0).astype(BF)


def tiles(count):
    return [slice(i, i + TILE) for i in range(0, count, TILE)]


class Far:
    def __init__(self, array, start=0, size=None):
        self.array = array
        self.start = start
        self.size = array.shape[0] if size is None else size


class Fetched:
    def __init__(self, copy, buffer):
        self.copy, self.buffer, self.waited = copy, buffer, False
        self.shape = buffer.shape

    def __getitem__(self, index):
        if not self.waited:
            self.copy.wait()
            self.waited = True
        return self.buffer[index]


def call(kernel, args, outs, scratch=(), flops=0):
    far = [i for i, a in enumerate(args) if isinstance(a, Far)]
    arrays = [a.array if isinstance(a, Far) else a for a in args]
    buffers = [
        pltpu.VMEM((args[i].size,) + args[i].array.shape[1:], args[i].array.dtype) for i in far
    ]
    specs = [
        pl.BlockSpec(memory_space=pltpu.HBM)
        if isinstance(a, Far)
        else (SMEM if a.dtype == I32 and a.ndim == 1 else VMEM)
        for a in args
    ]
    ins, made = len(args), len(args) + len(outs)

    def body(*refs):
        held = refs[made : made + len(far)]
        refs_in = list(refs[:ins])
        if far:
            sems = refs[made + len(far)]
        for k, i in enumerate(far):
            source = refs_in[i].at[args[i].start : args[i].start + args[i].size]
            copy = pltpu.make_async_copy(source, held[k], sems.at[k])
            copy.start()
            refs_in[i] = Fetched(copy, held[k])
        kernel(*refs_in, *refs[ins:made], *refs[made + len(far) + (1 if far else 0) :])
        for i in far:
            if not refs_in[i].waited:
                refs_in[i].copy.wait()

    size = sum(math.prod(a.shape) * a.dtype.itemsize for a in arrays + list(outs))
    extra = buffers + ([pltpu.SemaphoreType.DMA((len(far),))] if far else [])
    return pl.pallas_call(
        body,
        out_shape=tuple(outs),
        in_specs=specs,
        out_specs=tuple([VMEM] * len(outs)),
        scratch_shapes=extra + list(scratch),
        compiler_params=pltpu.CompilerParams(vmem_limit_bytes=14 * 2**20),
        cost_estimate=pl.CostEstimate(flops=flops, bytes_accessed=size, transcendentals=0),
    )(*arrays)


def shape(dtype, *dims):
    return jax.ShapeDtypeStruct(dims, dtype)


def send_kernel(rows_ref, count_ref, halo_ref, nodes_ref, out_ref, low_ref, high_ref, live_ref):
    slots = rows_ref.shape[1]
    patches = count_ref.shape[1]
    width = nodes_ref.shape[0]
    owner = lax.broadcasted_iota(I32, (patches, slots), 0)
    place = lax.broadcasted_iota(I32, (patches, slots), 1)
    repeat = jnp.where(place // SLOT == owner, 1.0, 0.0).astype(BF)
    counts = jnp.broadcast_to(count_ref[...].astype(F32), (8, patches)).astype(BF)
    spread = dot(counts, repeat)[:1].astype(I32)
    slot = lax.broadcasted_iota(I32, (1, slots), 1) % SLOT
    live = jnp.where(slot < spread, rows_ref[...], -1)
    live_ref[...] = live
    nodes = nodes_ref[...]
    depth = low_ref.shape[0]
    halo = dot(pick(column(halo_ref[...]), width), nodes).astype(BF)
    low_ref[...] = halo[:depth]
    high_ref[...] = halo[depth:]
    col = column(live)
    for r in tiles(slots):
        out_ref[r] = dot(pick(col[r], width), nodes).astype(BF)


def edge_kernel(
    dst_ref, nodes_ref, wb_ref, src_ref, low_ref, high_ref, wa_ref, edges_ref, wc_ref, second_ref,
    slope_ref, agg_ref, msg_ref, hid_ref,
):
    count, width = nodes_ref.shape
    inner = edges_ref.shape[0] - edges_ref.shape[0] // 4
    dst = column(dst_ref[...])
    nodes = nodes_ref[...]
    src = column(src_ref[...])
    halo = jnp.concatenate([low_ref[...], high_ref[...]], axis=0)
    for r in tiles(edges_ref.shape[0]):
        if r.stop <= inner:
            feat = dot(pick(src[r], count), nodes).astype(BF)
        else:
            feat = dot(pick(src[r] - float(count), halo.shape[0]), halo).astype(BF)
        own = dot(pick(dst[r], count), nodes).astype(BF)
        pre = dot(own, wb_ref[...]) + dot(feat, wa_ref[...]) + dot(edges_ref[r], wc_ref[...])
        sigma = jax.nn.sigmoid(pre)
        hid_ref[r] = (pre * sigma).astype(BF)
        slope_ref[r] = (sigma * (1.0 + pre * (1.0 - sigma))).astype(BF)
    for r in tiles(count):
        agg = dot(pick_t(dst_ref[...], r.start, TILE), hid_ref[...]).astype(BF)
        agg_ref[r] = agg
        msg_ref[r] = dot(agg, second_ref[...])


def node_kernel(
    target_ref, margin_ref, nodes_ref, a_ref, b_ref, cot_ref, second_ref, msg_ref, recv_ref,
    new_ref, pooled_ref, hid_ref, gpre_ref, gpool_ref, part_ref, ret_ref,
):
    count, width = nodes_ref.shape
    target, margin = target_ref[...], margin_ref[...]
    for r in tiles(count):
        coupled = dot(pick_t(target, r.start, TILE, margin), recv_ref[...])
        pooled = (msg_ref[r] + coupled).astype(BF)
        pooled_ref[r] = pooled
        nodes = nodes_ref[r]
        pre = dot(nodes, a_ref[...]) + dot(pooled, b_ref[...])
        sigma = jax.nn.sigmoid(pre)
        hidden = (pre * sigma).astype(BF)
        hid_ref[r] = hidden
        slope = sigma * (1.0 + pre * (1.0 - sigma))
        cot = cot_ref[r]
        gpre = (dot_nt(cot, second_ref[...]) * slope).astype(BF)
        gpre_ref[r] = gpre
        gpool_ref[r] = dot_nt(gpre, b_ref[...]).astype(BF)
        new_ref[r] = (nodes.astype(F32) + dot(hidden, second_ref[...])).astype(BF)
        part_ref[r] = cot.astype(F32) + dot_nt(gpre, a_ref[...])
    col, weight = column(target), column(margin)
    gpool = gpool_ref[...]
    for r in tiles(recv_ref.shape[0]):
        ret_ref[r] = dot(pick(col[r], count, weight[r]), gpool).astype(BF)


def put(own_ref, send_ref, index, value, first):
    half = value.shape[1] // 2
    lane = half // 2
    step = value.shape[0] // RING
    fine = step // RING
    own = jnp.where(first, value[:, :half], value[:, half:]).astype(BF)
    send = jnp.where(first, value[:, half:], value[:, :half]).astype(BF)
    for ref, part in ((own_ref, own), (send_ref, send)):
        for i in range(RING):
            ref[0, i, index] = part[i * step : (i + 1) * step, :lane]
            for j in range(RING):
                start = i * step + j * fine
                ref[1, j, index, i * fine : (i + 1) * fine] = part[start : start + fine, lane:]


def node_grad_kernel(
    side_ref, agg_ref, nodes_ref, pooled_ref, hid_ref, gpre_ref, gpool_ref, cot_ref, own_ref, send_ref,
    *, patches, scale
):
    order = row_order(side_ref[1], nodes_ref.shape[1], patches)
    first = side_ref[0] == 0
    pairs = [(agg_ref, gpool_ref), (nodes_ref, gpre_ref), (pooled_ref, gpre_ref), (hid_ref, cot_ref)]
    for index, (left, right) in enumerate(pairs):
        turned = dot_nt(order, left[...]).astype(BF)
        put(own_ref, send_ref, index, dot(turned, right[...]) * scale, first)


def edge_grad_kernel(
    side_ref, dst_ref, second_ref, edges_ref, src_ref, nodes_ref, wa_ref, low_ref, high_ref, slope_ref, gpool_ref,
    own_ref, send_ref, gpre_ref, bysrc_ref, bydst_ref, glow_ref, ghigh_ref,
    *, patches, scale
):
    count, width = nodes_ref.shape
    inner = edges_ref.shape[0] - edges_ref.shape[0] // 4
    depth = low_ref.shape[0]
    first = side_ref[0] == 0
    gpool = gpool_ref[...]
    second = second_ref[...]
    dst_row, src_row = dst_ref[...], src_ref[...]
    dst = column(dst_row)
    for r in tiles(edges_ref.shape[0]):
        message = dot(pick(dst[r], count), gpool).astype(BF)
        gpre_ref[r] = (dot_nt(message, second) * slope_ref[r].astype(F32)).astype(BF)
    order = row_order(side_ref[1], width, patches)
    turned = dot_nt(order, edges_ref[...]).astype(BF)
    put(own_ref, send_ref, 2, dot(turned, gpre_ref[...]) * scale, first)
    for r in tiles(count):
        bydst_ref[r] = dot(pick_t(dst_row, r.start, TILE), gpre_ref[...]).astype(BF)
        bysrc_ref[r] = dot(pick_t(src_row[:, :inner], r.start, TILE), gpre_ref[:inner]).astype(BF)
    halo = dot(pick_t(src_row[:, inner:], count, 2 * depth), gpre_ref[inner:]).astype(BF)
    turned = dot_nt(order, nodes_ref[...]).astype(BF)
    put(own_ref, send_ref, 1, dot(turned, bydst_ref[...]) * scale, first)
    rim = dot_nt(order, jnp.concatenate([low_ref[...], high_ref[...]], axis=0)).astype(BF)
    put(own_ref, send_ref, 0, (dot(turned, bysrc_ref[...]) + dot(rim, halo)) * scale, first)
    back = dot_nt(halo, wa_ref[...]).astype(BF)
    glow_ref[...] = back[:depth]
    ghigh_ref[...] = back[depth:]


def edge_rest_kernel(
    wc_ref, wa_ref, wb_ref, gpre_ref, bysrc_ref, bydst_ref, part_ref, edge_ref, total_ref
):
    count, width = bysrc_ref.shape
    for r in tiles(gpre_ref.shape[0]):
        edge_ref[r] = dot_nt(gpre_ref[r], wc_ref[...]).astype(BF)
    for r in tiles(count):
        total_ref[r] = (
            part_ref[r]
            + dot_nt(bysrc_ref[r], wa_ref[...])
            + dot_nt(bydst_ref[r], wb_ref[...])
        )


def last_kernel(live_ref, halo_ref, total_ref, low_ref, high_ref, back_ref, out_ref):
    halo_back = jnp.concatenate([low_ref[...], high_ref[...]], axis=0)
    for r in tiles(total_ref.shape[0]):
        out_ref[r] = (
            total_ref[r]
            + dot(pick_t(halo_ref[...], r.start, TILE), halo_back)
            + dot(pick_t(live_ref[...], r.start, TILE), back_ref[...])
        ).astype(BF)


def from_partner(value):
    return lax.ppermute(value, "mesh", [(0, 1), (1, 0)])


def shift(value, step):
    count = lax.axis_size("patch")
    return lax.ppermute(value, "patch", [(i, (i + step) % count) for i in range(count)])


def route(crossed):
    rows, width = crossed.shape
    patches = lax.axis_size("patch")
    crossed = crossed.reshape(patches, rows // patches, width)
    routed = lax.all_to_all(crossed, "patch", split_axis=0, concat_axis=0, tiled=True)
    return routed.reshape(rows, width)


def hop(value, dz=0, dy=0, dx=0):
    depth = lax.axis_size("patch") // PLANE
    pairs = []
    for p in range(depth * PLANE):
        z, y, x = p // PLANE, p // RING % RING, p % RING
        pairs.append((p, (z + dz) % depth * PLANE + (y + dy) % RING * RING + (x + dx) % RING))
    return lax.ppermute(value, "patch", pairs)


def join_kernel(own_a, other_a, own_b, other_b, *outs):
    for index, out in enumerate(outs):
        c, d = index // RING, index % RING
        base = 0
        for own, other in ((own_a, other_a), (own_b, other_b)):
            blocks = own.shape[2]
            joined = own[c, d].astype(F32) + other[c, d].astype(F32)
            out[base : base + blocks] = joined.astype(BF)
            base += blocks


def total_of(refs):
    total = refs[0][...].astype(F32)
    for ref in refs[1:]:
        total = total + ref[...].astype(F32)
    return total


def plane_kernel(*refs):
    for c in range(2):
        total = total_of(refs[c * RING : (c + 1) * RING])
        fine = total.shape[1] // RING
        for d in range(RING):
            refs[(2 + c) * RING + d][...] = total[:, d * fine : (d + 1) * fine].astype(BF)


def depth_kernel(*refs):
    ins, outs = refs[: 2 * RING], refs[2 * RING :]
    for c in range(2):
        total = total_of(ins[c * RING : (c + 1) * RING])
        blocks, rows, lane = total.shape
        fine = rows // len(outs)
        for block in range(blocks):
            for d, out in enumerate(outs):
                out[block * fine : (block + 1) * fine, c * lane : (c + 1) * lane] = total[
                    block, d * fine : (d + 1) * fine
                ]


def weight_sums(own_a, other_a, own_b, other_b, tied):
    depth = lax.axis_size("patch") // PLANE
    rows, lane = own_a.shape[3:]
    blocks = own_a.shape[2] + own_b.shape[2]
    fine = rows // RING // depth
    piece = shape(BF, blocks, rows, lane)
    small = shape(BF, blocks, rows // RING, lane)
    pieces = call(join_kernel, (own_a, other_a, own_b, other_b), (piece,) * (2 * RING))
    pieces, tied = lax.optimization_barrier((pieces, tied))
    for kernel, axes in ((plane_kernel, ("dx", "dy")), (None, ("dy", "dx"))):
        pieces = [
            pieces[c * RING + d] if d == 0 else hop(pieces[c * RING + d], **{axis: d})
            for c, axis in enumerate(axes)
            for d in range(RING)
        ]
        if kernel is not None:
            pieces = call(kernel, pieces, (small,) * (2 * RING))
    pieces = call(depth_kernel, pieces, (shape(F32, blocks * fine, 2 * lane),) * depth)
    own = pieces[0]
    for d in range(1, depth):
        own = own + hop(pieces[d], dz=d)
    other = from_partner(own)
    first = lax.axis_index("mesh") == 0
    both = jnp.concatenate([jnp.where(first, own, other), jnp.where(first, other, own)], axis=1)
    return both.reshape(blocks, fine * 4 * lane), tied


def shards(
    nodes,
    edges,
    cot_nodes,
    weights,
    edge_src,
    edge_dst,
    halo_rows,
    couple_rows,
    couple_count,
    couple_target,
    couple_weight,
):
    nodes_own = nodes[0]
    edges_own = edges[0]
    cotangent = cot_nodes[0]
    count, width = nodes_own.shape
    edge_count = edges_own.shape[0]
    depth = halo_rows.shape[1] // 2
    patches = lax.axis_size("patch")
    slots = couple_rows.shape[2]
    scale = 1.0 / math.sqrt(2 * patches * edge_count)
    side = jnp.stack([lax.axis_index("mesh"), lax.axis_index("patch")]).astype(I32)
    target, margin = couple_target[0], couple_weight[0]
    unit = 2 * width * width

    def weight(block):
        return Far(weights, block * width, width)

    outgoing, low_out, high_out, live = call(
        send_kernel,
        (Far(couple_rows[0]), Far(couple_count[0]), Far(halo_rows), Far(nodes_own)),
        (shape(BF, slots, width), shape(BF, depth, width), shape(BF, depth, width), shape(I32, 1, slots)),
        flops=(slots + 2 * depth) * unit,
    )
    crossed = from_partner(outgoing)
    low, high = shift(high_out, 1), shift(low_out, -1)
    crossed, low, high = lax.optimization_barrier((crossed, low, high))
    received = route(crossed)
    slope, agg, message = call(
        edge_kernel,
        (
            Far(edge_dst), Far(nodes_own), weight(1), Far(edge_src), low, high, weight(0),
            Far(edges_own), weight(2), weight(3),
        ),
        (shape(BF, edge_count, width), shape(BF, count, width), shape(F32, count, width)),
        scratch=(pltpu.VMEM((edge_count, width), BF),),
        flops=edge_count * 6 * unit,
    )
    square = shape(BF, count, width)
    new_nodes, pooled, hidden, grad_pre, grad_pooled, part, returned = call(
        node_kernel,
        (
            Far(target), Far(margin), Far(nodes_own), weight(4), weight(5), Far(cotangent), weight(6),
            message, received,
        ),
        (square, square, square, square, square, shape(F32, count, width), shape(BF, slots, width)),
        flops=count * 10 * unit,
    )
    crossed_back = from_partner(returned)
    grad_shape = lambda blocks: shape(BF, 2, RING, blocks, width // RING, width // 4)
    own_b, send_b = call(
        lambda *refs: node_grad_kernel(*refs, patches=patches, scale=scale),
        (side, agg, Far(nodes_own), pooled, hidden, grad_pre, grad_pooled, Far(cotangent)),
        (grad_shape(4), grad_shape(4)),
        flops=count * 8 * unit,
    )
    other_b = from_partner(send_b)
    grad_pooled, other_b = lax.optimization_barrier((grad_pooled, other_b))
    own_a, send_a, grad_edge_pre, by_source, by_target, grad_low, grad_high = call(
        lambda *refs: edge_grad_kernel(*refs, patches=patches, scale=scale),
        (
            side, Far(edge_dst), weight(3), Far(edges_own), Far(edge_src), Far(nodes_own), weight(0),
            low, high, slope, grad_pooled,
        ),
        (
            grad_shape(3), grad_shape(3), shape(BF, edge_count, width), square, square,
            shape(BF, depth, width), shape(BF, depth, width),
        ),
        flops=edge_count * 8 * unit,
    )
    summed, crossed_back = weight_sums(own_a, from_partner(send_a), own_b, other_b, crossed_back)
    couple_back = route(crossed_back)
    back_low, back_high = shift(grad_high, 1), shift(grad_low, -1)
    edge_grads, total = call(
        edge_rest_kernel,
        (weight(2), weight(0), weight(1), grad_edge_pre, by_source, by_target, part),
        (shape(BF, edge_count, width), shape(F32, count, width)),
        flops=edge_count * 2 * unit,
    )
    (node_grads,) = call(
        last_kernel,
        (live, Far(halo_rows), total, back_low, back_high, couple_back),
        (square,),
        flops=count * 2 * unit,
    )
    return (new_nodes[None], node_grads[None], edge_grads[None], summed)


def solution(mesh):
    return jax.shard_map(
        shards,
        mesh=mesh,
        in_specs=(
            P("mesh", "patch", None),
            P("mesh", "patch", None),
            P("mesh", "patch", None),
            P(),
            P("mesh", "patch"),
            P("mesh", "patch"),
            P("mesh", "patch"),
            P("mesh", "patch", None),
            P("mesh", "patch", None),
            P("mesh", "patch", None),
            P("mesh", "patch", None),
        ),
        out_specs=(
            P("mesh", "patch", None),
            P("mesh", "patch", None),
            P("mesh", "patch", None),
            P(None, "patch"),
        ),
        check_vma=False,
    )
```

```python
import math

import jax
import jax.numpy as jnp
from jax import lax
from jax.experimental import pallas as pl
from jax.experimental.pallas import tpu as pltpu
from jax.sharding import PartitionSpec as P

SLOT = 8
RING = 4
PLANE = RING * RING
TILE = 256
LIMIT = 61 * 2**20 - 2**16
BF = jnp.bfloat16
F32 = jnp.float32
I32 = jnp.int32
VMEM = pl.BlockSpec(memory_space=pltpu.VMEM)
SMEM = pl.BlockSpec(memory_space=pltpu.SMEM)


def dot(a, b):
    return jnp.dot(a, b, preferred_element_type=F32)


def dot_nt(a, b):
    return lax.dot_general(a, b, (((1,), (1,)), ((), ())), preferred_element_type=F32)


def column(row):
    return jnp.transpose(jnp.broadcast_to(row.astype(F32), (128, row.shape[1])))


def pick(col, count, value=None):
    base = lax.broadcasted_iota(I32, (col.shape[0], 128), 1).astype(F32)
    one = jnp.ones_like(base) if value is None else value
    parts = [jnp.where(col == base + float(k), one, 0.0).astype(BF) for k in range(0, count, 128)]
    return parts[0] if len(parts) == 1 else jnp.concatenate(parts, axis=1)


def pick_t(row, start, size, value=None):
    base = lax.broadcasted_iota(I32, (size, row.shape[1]), 0) + start
    one = jnp.ones(base.shape, F32) if value is None else jnp.broadcast_to(value, base.shape)
    return jnp.where(base == row, one, 0.0).astype(BF)


def row_order(place, width, patches):
    fine = width // patches
    depth = patches // PLANE
    row = lax.broadcasted_iota(I32, (width, width), 0)
    col = lax.broadcasted_iota(I32, (width, width), 1)
    dx, dy = row // (width // RING), (row // (width // PLANE)) % RING
    dz, offset = (row // fine) % depth, row % fine
    x, y = place % RING, (place // RING) % RING
    patch = dz * PLANE + (y + dy) % RING * RING + (x + dx) % RING
    return jnp.where(col == patch * fine + offset, 1.0, 0.0).astype(BF)


def tiles(count):
    return [slice(i, i + TILE) for i in range(0, count, TILE)]


class Far:
    def __init__(self, array, start=0, size=None):
        self.array = array
        self.start = start
        self.size = array.shape[0] if size is None else size


class Fetched:
    def __init__(self, copy, buffer):
        self.copy, self.buffer, self.waited = copy, buffer, False
        self.shape = buffer.shape

    def wait(self):
        if not self.waited:
            self.copy.wait()
            self.waited = True

    def __getitem__(self, index):
        self.wait()
        return self.buffer[index]


class Staged:
    def __init__(self, copy, buffer):
        self.copy, self.buffer, self.sent = copy, buffer, False
        self.shape = buffer.shape

    def __getitem__(self, index):
        return self.buffer[index]

    def __setitem__(self, index, value):
        self.buffer[index] = value

    def flush(self):
        if not self.sent:
            self.copy.start()
            self.sent = True


def flush(*refs):
    for ref in refs:
        ref.flush()


def cost(arrays, flops):
    size = sum(math.prod(a.shape) * a.dtype.itemsize for a in arrays)
    return pl.CostEstimate(flops=flops, bytes_accessed=size, transcendentals=0)


def call(kernel, args, outs):
    return pl.pallas_call(
        kernel,
        out_shape=tuple(outs),
        in_specs=[VMEM] * len(args),
        out_specs=tuple([VMEM] * len(outs)),
        compiler_params=pltpu.CompilerParams(vmem_limit_bytes=14 * 2**20),
        cost_estimate=cost(list(args) + list(outs), 0),
    )(*args)


def stream(kernel, args, outs, scratch=(), flops=0):
    args = [a if isinstance(a, Far) or a.ndim == 1 else Far(a) for a in args]
    far = [i for i, a in enumerate(args) if isinstance(a, Far)]
    arrays = [a.array if isinstance(a, Far) else a for a in args]
    held = [
        pltpu.VMEM((args[i].size,) + args[i].array.shape[1:], args[i].array.dtype) for i in far
    ]
    held += [pltpu.VMEM(o.shape, o.dtype) for o in outs]
    hbm = pl.BlockSpec(memory_space=pltpu.HBM)
    ins, made, moved = len(args), len(args) + len(outs), len(far) + len(outs)

    def body(*refs):
        buffers, sems, rest = refs[made : made + moved], refs[made + moved], refs[made + moved + 1 :]
        reads = list(refs[:ins])
        for k, i in enumerate(far):
            source = reads[i].at[args[i].start : args[i].start + args[i].size]
            copy = pltpu.make_async_copy(source, buffers[k], sems.at[k])
            copy.start()
            reads[i] = Fetched(copy, buffers[k])
        writes = []
        for k, out in enumerate(refs[ins:made], len(far)):
            writes.append(Staged(pltpu.make_async_copy(buffers[k], out, sems.at[k]), buffers[k]))
        kernel(*reads, *writes, *rest)
        flush(*writes)
        for i in far:
            reads[i].wait()
        for write in writes:
            write.copy.wait()

    return pl.pallas_call(
        body,
        out_shape=tuple(outs),
        in_specs=[hbm if isinstance(a, Far) else SMEM for a in args],
        out_specs=tuple([hbm] * len(outs)),
        scratch_shapes=held + [pltpu.SemaphoreType.DMA((moved,))] + list(scratch),
        compiler_params=pltpu.CompilerParams(vmem_limit_bytes=LIMIT),
        cost_estimate=cost(arrays + list(outs), flops),
    )(*arrays)


def shape(dtype, *dims):
    return jax.ShapeDtypeStruct(dims, dtype)


def send_kernel(rows_ref, count_ref, halo_ref, nodes_ref, out_ref, low_ref, high_ref, live_ref):
    slots = rows_ref.shape[1]
    patches = count_ref.shape[1]
    width = nodes_ref.shape[0]
    owner = lax.broadcasted_iota(I32, (patches, slots), 0)
    place = lax.broadcasted_iota(I32, (patches, slots), 1)
    repeat = jnp.where(place // SLOT == owner, 1.0, 0.0).astype(BF)
    counts = jnp.broadcast_to(count_ref[...].astype(F32), (8, patches)).astype(BF)
    spread = dot(counts, repeat)[:1].astype(I32)
    slot = lax.broadcasted_iota(I32, (1, slots), 1) % SLOT
    live = jnp.where(slot < spread, rows_ref[...], -1)
    live_ref[...] = live
    nodes = nodes_ref[...]
    depth = low_ref.shape[0]
    halo = dot(pick(column(halo_ref[...]), width), nodes).astype(BF)
    low_ref[...] = halo[:depth]
    high_ref[...] = halo[depth:]
    flush(low_ref, high_ref, live_ref)
    col = column(live)
    for r in tiles(slots):
        out_ref[r] = dot(pick(col[r], width), nodes).astype(BF)


def edge_kernel(
    dst_ref, nodes_ref, wb_ref, src_ref, low_ref, high_ref, wa_ref, edges_ref, wc_ref, second_ref,
    slope_ref, agg_ref, msg_ref, hid_ref,
):
    count, width = nodes_ref.shape
    inner = edges_ref.shape[0] - edges_ref.shape[0] // 4
    dst = column(dst_ref[...])
    nodes = nodes_ref[...]
    src = column(src_ref[...])
    halo = jnp.concatenate([low_ref[...], high_ref[...]], axis=0)
    for r in tiles(edges_ref.shape[0]):
        if r.stop <= inner:
            feat = dot(pick(src[r], count), nodes).astype(BF)
        else:
            feat = dot(pick(src[r] - float(count), halo.shape[0]), halo).astype(BF)
        own = dot(pick(dst[r], count), nodes).astype(BF)
        pre = dot(own, wb_ref[...]) + dot(feat, wa_ref[...]) + dot(edges_ref[r], wc_ref[...])
        sigma = jax.nn.sigmoid(pre)
        hid_ref[r] = (pre * sigma).astype(BF)
        slope_ref[r] = (sigma * (1.0 + pre * (1.0 - sigma))).astype(BF)
    flush(slope_ref)
    for r in tiles(count):
        agg = dot(pick_t(dst_ref[...], r.start, TILE), hid_ref[...]).astype(BF)
        agg_ref[r] = agg
        msg_ref[r] = dot(agg, second_ref[...])


def node_kernel(
    target_ref, margin_ref, recv_ref, msg_ref, nodes_ref, a_ref, b_ref, cot_ref, second_ref,
    new_ref, pooled_ref, hid_ref, gpre_ref, gpool_ref, part_ref, ret_ref,
):
    count, width = nodes_ref.shape
    target, margin = target_ref[...], margin_ref[...]
    for r in tiles(count):
        coupled = dot(pick_t(target, r.start, TILE, margin), recv_ref[...])
        pooled = (msg_ref[r] + coupled).astype(BF)
        pooled_ref[r] = pooled
        nodes = nodes_ref[r]
        pre = dot(nodes, a_ref[...]) + dot(pooled, b_ref[...])
        sigma = jax.nn.sigmoid(pre)
        hidden = (pre * sigma).astype(BF)
        hid_ref[r] = hidden
        slope = sigma * (1.0 + pre * (1.0 - sigma))
        cot = cot_ref[r]
        gpre = (dot_nt(cot, second_ref[...]) * slope).astype(BF)
        gpre_ref[r] = gpre
        gpool_ref[r] = dot_nt(gpre, b_ref[...]).astype(BF)
        new_ref[r] = (nodes.astype(F32) + dot(hidden, second_ref[...])).astype(BF)
        part_ref[r] = cot.astype(F32) + dot_nt(gpre, a_ref[...])
    flush(new_ref, pooled_ref, hid_ref, gpre_ref, gpool_ref, part_ref)
    col, weight = column(target), column(margin)
    gpool = gpool_ref[...]
    for r in tiles(recv_ref.shape[0]):
        ret_ref[r] = dot(pick(col[r], count, weight[r]), gpool).astype(BF)


def put(own_ref, send_ref, index, value, first):
    half = value.shape[1] // 2
    lane = half // 2
    step = value.shape[0] // RING
    fine = step // RING
    own = jnp.where(first, value[:, :half], value[:, half:]).astype(BF)
    send = jnp.where(first, value[:, half:], value[:, :half]).astype(BF)
    for ref, part in ((own_ref, own), (send_ref, send)):
        for i in range(RING):
            ref[0, i, index] = part[i * step : (i + 1) * step, :lane]
            for j in range(RING):
                start = i * step + j * fine
                ref[1, j, index, i * fine : (i + 1) * fine] = part[start : start + fine, lane:]


def node_grad_kernel(
    side_ref, agg_ref, gpool_ref, nodes_ref, gpre_ref, pooled_ref, hid_ref, cot_ref, own_ref, send_ref,
    *, patches, scale
):
    order = row_order(side_ref[1], nodes_ref.shape[1], patches)
    first = side_ref[0] == 0
    pairs = [(agg_ref, gpool_ref), (nodes_ref, gpre_ref), (pooled_ref, gpre_ref), (hid_ref, cot_ref)]
    for index, (left, right) in enumerate(pairs):
        turned = dot_nt(order, left[...]).astype(BF)
        put(own_ref, send_ref, index, dot(turned, right[...]) * scale, first)


def edge_grad_kernel(
    side_ref, dst_ref, gpool_ref, second_ref, slope_ref, edges_ref, src_ref, nodes_ref, low_ref, high_ref, wa_ref,
    own_ref, send_ref, gpre_ref, bysrc_ref, bydst_ref, glow_ref, ghigh_ref,
    *, patches, scale
):
    count, width = nodes_ref.shape
    inner = edges_ref.shape[0] - edges_ref.shape[0] // 4
    depth = low_ref.shape[0]
    first = side_ref[0] == 0
    gpool = gpool_ref[...]
    second = second_ref[...]
    dst_row, src_row = dst_ref[...], src_ref[...]
    dst = column(dst_row)
    for r in tiles(edges_ref.shape[0]):
        message = dot(pick(dst[r], count), gpool).astype(BF)
        gpre_ref[r] = (dot_nt(message, second) * slope_ref[r].astype(F32)).astype(BF)
    flush(gpre_ref)
    order = row_order(side_ref[1], width, patches)
    turned = dot_nt(order, edges_ref[...]).astype(BF)
    put(own_ref, send_ref, 2, dot(turned, gpre_ref[...]) * scale, first)
    for r in tiles(count):
        bydst_ref[r] = dot(pick_t(dst_row, r.start, TILE), gpre_ref[...]).astype(BF)
        bysrc_ref[r] = dot(pick_t(src_row[:, :inner], r.start, TILE), gpre_ref[:inner]).astype(BF)
    flush(bysrc_ref, bydst_ref)
    halo = dot(pick_t(src_row[:, inner:], count, 2 * depth), gpre_ref[inner:]).astype(BF)
    turned = dot_nt(order, nodes_ref[...]).astype(BF)
    put(own_ref, send_ref, 1, dot(turned, bydst_ref[...]) * scale, first)
    rim = dot_nt(order, jnp.concatenate([low_ref[...], high_ref[...]], axis=0)).astype(BF)
    put(own_ref, send_ref, 0, (dot(turned, bysrc_ref[...]) + dot(rim, halo)) * scale, first)
    back = dot_nt(halo, wa_ref[...]).astype(BF)
    glow_ref[...] = back[:depth]
    ghigh_ref[...] = back[depth:]


def edge_rest_kernel(
    gpre_ref, wc_ref, bysrc_ref, wa_ref, bydst_ref, wb_ref, part_ref, edge_ref, total_ref
):
    count, width = bysrc_ref.shape
    for r in tiles(gpre_ref.shape[0]):
        edge_ref[r] = dot_nt(gpre_ref[r], wc_ref[...]).astype(BF)
    flush(edge_ref)
    for r in tiles(count):
        total_ref[r] = (
            part_ref[r]
            + dot_nt(bysrc_ref[r], wa_ref[...])
            + dot_nt(bydst_ref[r], wb_ref[...])
        )


def last_kernel(live_ref, halo_ref, total_ref, low_ref, high_ref, back_ref, out_ref):
    halo_back = jnp.concatenate([low_ref[...], high_ref[...]], axis=0)
    for r in tiles(total_ref.shape[0]):
        out_ref[r] = (
            total_ref[r]
            + dot(pick_t(halo_ref[...], r.start, TILE), halo_back)
            + dot(pick_t(live_ref[...], r.start, TILE), back_ref[...])
        ).astype(BF)


def from_partner(value):
    return lax.ppermute(value, "mesh", [(0, 1), (1, 0)])


def shift(value, step):
    count = lax.axis_size("patch")
    return lax.ppermute(value, "patch", [(i, (i + step) % count) for i in range(count)])


def route(crossed):
    rows, width = crossed.shape
    patches = lax.axis_size("patch")
    crossed = crossed.reshape(patches, rows // patches, width)
    routed = lax.all_to_all(crossed, "patch", split_axis=0, concat_axis=0, tiled=True)
    return routed.reshape(rows, width)


def hop(value, dz=0, dy=0, dx=0):
    depth = lax.axis_size("patch") // PLANE
    pairs = []
    for p in range(depth * PLANE):
        z, y, x = p // PLANE, p // RING % RING, p % RING
        pairs.append((p, (z + dz) % depth * PLANE + (y + dy) % RING * RING + (x + dx) % RING))
    return lax.ppermute(value, "patch", pairs)


def join_kernel(own_a, other_a, own_b, other_b, *outs):
    for index, out in enumerate(outs):
        c, d = index // RING, index % RING
        base = 0
        for own, other in ((own_a, other_a), (own_b, other_b)):
            blocks = own.shape[2]
            joined = own[c, d].astype(F32) + other[c, d].astype(F32)
            out[base : base + blocks] = joined.astype(BF)
            base += blocks


def total_of(refs):
    total = refs[0][...].astype(F32)
    for ref in refs[1:]:
        total = total + ref[...].astype(F32)
    return total


def plane_kernel(*refs):
    for c in range(2):
        total = total_of(refs[c * RING : (c + 1) * RING])
        fine = total.shape[1] // RING
        for d in range(RING):
            refs[(2 + c) * RING + d][...] = total[:, d * fine : (d + 1) * fine].astype(BF)


def depth_kernel(*refs):
    ins, (out, hold) = refs[: 2 * RING], refs[2 * RING :]
    depth = hold.shape[0]
    hold[...] = jnp.zeros(hold.shape, F32)
    for c in range(2):
        total = total_of(ins[c * RING : (c + 1) * RING])
        blocks, rows, lane = total.shape
        fine = rows // depth
        for block in range(blocks):
            for d in range(depth):
                hold[d, block * fine : (block + 1) * fine, c * lane : (c + 1) * lane] = total[
                    block, d * fine : (d + 1) * fine
                ]
    value = hold[...].astype(BF)
    out[:depth] = value
    out[depth:] = value


def finish_kernel(in_ref, out_ref):
    count, _, lane = in_ref.shape
    depth = count // 2
    for side in range(2):
        total = in_ref[side * depth].astype(F32)
        for d in range(1, depth):
            total = total + in_ref[side * depth + d].astype(F32)
        out_ref[:, side * lane : (side + 1) * lane] = total[: out_ref.shape[0]]


def weight_sums(own_a, other_a, own_b, other_b, couple_back, total):
    patches = lax.axis_size("patch")
    depth = patches // PLANE
    rows, lane = own_a.shape[3:]
    blocks = own_a.shape[2] + own_b.shape[2]
    fine = rows // RING // depth
    piece = shape(BF, blocks, rows, lane)
    small = shape(BF, blocks, rows // RING, lane)
    pieces = call(join_kernel, (own_a, other_a, own_b, other_b), (piece,) * (2 * RING))
    for kernel, axes in ((plane_kernel, ("dx", "dy")), (None, ("dy", "dx"))):
        pieces = [
            pieces[c * RING + d] if d == 0 else hop(pieces[c * RING + d], **{axis: d})
            for c, axis in enumerate(axes)
            for d in range(RING)
        ]
        if kernel is not None:
            pieces = call(kernel, pieces, (small,) * (2 * RING))
    padded = (blocks * fine + 15) // 16 * 16
    (part,) = pl.pallas_call(
        depth_kernel,
        out_shape=(shape(BF, 2 * depth, padded, 2 * lane),),
        in_specs=[VMEM] * len(pieces),
        out_specs=(VMEM,),
        scratch_shapes=[pltpu.VMEM((depth, padded, 2 * lane), F32)],
    )(*pieces)
    part, couple_back, total = lax.optimization_barrier((part, couple_back, total))
    columns = [
        [m * patches + z * PLANE + i for m in range(2) for z in range(depth)] for i in range(PLANE)
    ]
    both = lax.all_to_all(
        part, ("mesh", "patch"), split_axis=0, concat_axis=0, axis_index_groups=columns, tiled=True
    )
    (result,) = call(finish_kernel, (both,), (shape(F32, blocks * fine, 4 * lane),))
    return result.reshape(blocks, fine * 4 * lane), couple_back, total


def shards(
    nodes,
    edges,
    cot_nodes,
    weights,
    edge_src,
    edge_dst,
    halo_rows,
    couple_rows,
    couple_count,
    couple_target,
    couple_weight,
):
    nodes_own = nodes[0]
    edges_own = edges[0]
    cotangent = cot_nodes[0]
    count, width = nodes_own.shape
    edge_count = edges_own.shape[0]
    depth = halo_rows.shape[1] // 2
    patches = lax.axis_size("patch")
    slots = couple_rows.shape[2]
    scale = 1.0 / math.sqrt(2 * patches * edge_count)
    side = jnp.stack([lax.axis_index("mesh"), lax.axis_index("patch")]).astype(I32)
    target, margin = couple_target[0], couple_weight[0]
    unit = 2 * width * width

    def weight(block):
        return Far(weights, block * width, width)

    def weight(block):
        return Far(weights, block * width, width)

    outgoing, low_out, high_out, live = stream(
        send_kernel,
        (couple_rows[0], couple_count[0], halo_rows, nodes_own),
        (shape(BF, slots, width), shape(BF, depth, width), shape(BF, depth, width), shape(I32, 1, slots)),
        flops=(slots + 2 * depth) * unit,
    )
    crossed = from_partner(outgoing)
    low, high = shift(high_out, 1), shift(low_out, -1)
    crossed, low, high = lax.optimization_barrier((crossed, low, high))
    received = route(crossed)
    slope, agg, message = stream(
        edge_kernel,
        (
            edge_dst, nodes_own, weight(1), edge_src, low, high, weight(0), edges_own, weight(2),
            weight(3),
        ),
        (shape(BF, edge_count, width), shape(BF, count, width), shape(F32, count, width)),
        scratch=(pltpu.VMEM((edge_count, width), BF),),
        flops=edge_count * 6 * unit,
    )
    square = shape(BF, count, width)
    new_nodes, pooled, hidden, grad_pre, grad_pooled, part, returned = stream(
        node_kernel,
        (target, margin, received, message, nodes_own, weight(4), weight(5), cotangent, weight(6)),
        (square, square, square, square, square, shape(F32, count, width), shape(BF, slots, width)),
        flops=count * 10 * unit,
    )
    crossed_back = from_partner(returned)
    couple_back = route(crossed_back)
    grad_shape = lambda blocks: shape(BF, 2, RING, blocks, width // RING, width // 4)
    own_b, send_b = stream(
        lambda *refs: node_grad_kernel(*refs, patches=patches, scale=scale),
        (side, agg, grad_pooled, nodes_own, grad_pre, pooled, hidden, cotangent),
        (grad_shape(4), grad_shape(4)),
        flops=count * 8 * unit,
    )
    other_b = from_partner(send_b)
    grad_pooled, other_b, crossed_back = lax.optimization_barrier((grad_pooled, other_b, crossed_back))
    own_a, send_a, grad_edge_pre, by_source, by_target, grad_low, grad_high = stream(
        lambda *refs: edge_grad_kernel(*refs, patches=patches, scale=scale),
        (
            side, edge_dst, grad_pooled, weight(3), slope, edges_own, edge_src, nodes_own, low, high,
            weight(0),
        ),
        (
            grad_shape(3), grad_shape(3), shape(BF, edge_count, width), square, square,
            shape(BF, depth, width), shape(BF, depth, width),
        ),
        flops=edge_count * 8 * unit,
    )
    edge_grads, total = stream(
        edge_rest_kernel,
        (grad_edge_pre, weight(2), by_source, weight(0), by_target, weight(1), part),
        (shape(BF, edge_count, width), shape(F32, count, width)),
        flops=edge_count * 2 * unit,
    )
    back_low, back_high = shift(grad_high, 1), shift(grad_low, -1)
    other_a = from_partner(send_a)
    summed, couple_back, total = weight_sums(own_a, other_a, own_b, other_b, couple_back, total)
    (node_grads,) = stream(
        last_kernel,
        (live, halo_rows, total, back_low, back_high, couple_back),
        (square,),
        flops=count * 2 * unit,
    )
    return (new_nodes[None], node_grads[None], edge_grads[None], summed)


def solution(mesh):
    return jax.shard_map(
        shards,
        mesh=mesh,
        in_specs=(
            P("mesh", "patch", None),
            P("mesh", "patch", None),
            P("mesh", "patch", None),
            P(),
            P("mesh", "patch"),
            P("mesh", "patch"),
            P("mesh", "patch"),
            P("mesh", "patch", None),
            P("mesh", "patch", None),
            P("mesh", "patch", None),
            P("mesh", "patch", None),
        ),
        out_specs=(
            P("mesh", "patch", None),
            P("mesh", "patch", None),
            P("mesh", "patch", None),
            P(None, "patch"),
        ),
        check_vma=False,
    )
```

```python
import math

import jax
import jax.numpy as jnp
from jax import lax
from jax.experimental import pallas as pl
from jax.experimental.pallas import tpu as pltpu
from jax.sharding import PartitionSpec as P

SLOT = 8
RING = 4
PLANE = RING * RING
TILE = 256
LIMIT = 61 * 2**20 - 2**16
BF = jnp.bfloat16
F32 = jnp.float32
I32 = jnp.int32
VMEM = pl.BlockSpec(memory_space=pltpu.VMEM)
SMEM = pl.BlockSpec(memory_space=pltpu.SMEM)


def dot(a, b):
    return jnp.dot(a, b, preferred_element_type=F32)


def dot_nt(a, b):
    return lax.dot_general(a, b, (((1,), (1,)), ((), ())), preferred_element_type=F32)


def column(row):
    return jnp.transpose(jnp.broadcast_to(row.astype(F32), (128, row.shape[1])))


def pick(col, count, value=None):
    base = lax.broadcasted_iota(I32, (col.shape[0], 128), 1).astype(F32)
    one = jnp.ones_like(base) if value is None else value
    parts = [jnp.where(col == base + float(k), one, 0.0).astype(BF) for k in range(0, count, 128)]
    return parts[0] if len(parts) == 1 else jnp.concatenate(parts, axis=1)


def pick_t(row, start, size, value=None):
    base = lax.broadcasted_iota(I32, (size, row.shape[1]), 0) + start
    one = jnp.ones(base.shape, F32) if value is None else jnp.broadcast_to(value, base.shape)
    return jnp.where(base == row, one, 0.0).astype(BF)


def row_order(place, width, patches):
    fine = width // patches
    depth = patches // PLANE
    row = lax.broadcasted_iota(I32, (width, width), 0)
    col = lax.broadcasted_iota(I32, (width, width), 1)
    dx, dy = row // (width // RING), (row // (width // PLANE)) % RING
    dz, offset = (row // fine) % depth, row % fine
    x, y = place % RING, (place // RING) % RING
    patch = dz * PLANE + (y + dy) % RING * RING + (x + dx) % RING
    return jnp.where(col == patch * fine + offset, 1.0, 0.0).astype(BF)


def tiles(count):
    return [slice(i, i + TILE) for i in range(0, count, TILE)]


class Far:
    def __init__(self, array, start=0, size=None):
        self.array = array
        self.start = start
        self.size = array.shape[0] if size is None else size


class Fetched:
    def __init__(self, copy, buffer):
        self.copy, self.buffer, self.waited = copy, buffer, False
        self.shape = buffer.shape

    def wait(self):
        if not self.waited:
            self.copy.wait()
            self.waited = True

    def __getitem__(self, index):
        self.wait()
        return self.buffer[index]


class Staged:
    def __init__(self, copy, buffer):
        self.copy, self.buffer, self.sent = copy, buffer, False
        self.shape = buffer.shape

    def __getitem__(self, index):
        return self.buffer[index]

    def __setitem__(self, index, value):
        self.buffer[index] = value

    def flush(self):
        if not self.sent:
            self.copy.start()
            self.sent = True


def flush(*refs):
    for ref in refs:
        ref.flush()


def cost(arrays, flops):
    size = sum(math.prod(a.shape) * a.dtype.itemsize for a in arrays)
    return pl.CostEstimate(flops=flops, bytes_accessed=size, transcendentals=0)


def call(kernel, args, outs):
    return pl.pallas_call(
        kernel,
        out_shape=tuple(outs),
        in_specs=[VMEM] * len(args),
        out_specs=tuple([VMEM] * len(outs)),
        compiler_params=pltpu.CompilerParams(vmem_limit_bytes=14 * 2**20),
        cost_estimate=cost(list(args) + list(outs), 0),
    )(*args)


def stream(kernel, args, outs, scratch=(), flops=0):
    args = [a if isinstance(a, Far) or a.ndim == 1 else Far(a) for a in args]
    far = [i for i, a in enumerate(args) if isinstance(a, Far)]
    arrays = [a.array if isinstance(a, Far) else a for a in args]
    held = [
        pltpu.VMEM((args[i].size,) + args[i].array.shape[1:], args[i].array.dtype) for i in far
    ]
    held += [pltpu.VMEM(o.shape, o.dtype) for o in outs]
    hbm = pl.BlockSpec(memory_space=pltpu.HBM)
    ins, made, moved = len(args), len(args) + len(outs), len(far) + len(outs)

    def body(*refs):
        buffers, sems, rest = refs[made : made + moved], refs[made + moved], refs[made + moved + 1 :]
        reads = list(refs[:ins])
        for k, i in enumerate(far):
            source = reads[i].at[args[i].start : args[i].start + args[i].size]
            copy = pltpu.make_async_copy(source, buffers[k], sems.at[k])
            copy.start()
            reads[i] = Fetched(copy, buffers[k])
        writes = []
        for k, out in enumerate(refs[ins:made], len(far)):
            writes.append(Staged(pltpu.make_async_copy(buffers[k], out, sems.at[k]), buffers[k]))
        kernel(*reads, *writes, *rest)
        flush(*writes)
        for i in far:
            reads[i].wait()
        for write in writes:
            write.copy.wait()

    return pl.pallas_call(
        body,
        out_shape=tuple(outs),
        in_specs=[hbm if isinstance(a, Far) else SMEM for a in args],
        out_specs=tuple([hbm] * len(outs)),
        scratch_shapes=held + [pltpu.SemaphoreType.DMA((moved,))] + list(scratch),
        compiler_params=pltpu.CompilerParams(vmem_limit_bytes=LIMIT),
        cost_estimate=cost(arrays + list(outs), flops),
    )(*arrays)


def shape(dtype, *dims):
    return jax.ShapeDtypeStruct(dims, dtype)


def send_kernel(rows_ref, count_ref, halo_ref, nodes_ref, out_ref, low_ref, high_ref, live_ref):
    slots = rows_ref.shape[1]
    patches = count_ref.shape[1]
    width = nodes_ref.shape[0]
    owner = lax.broadcasted_iota(I32, (patches, slots), 0)
    place = lax.broadcasted_iota(I32, (patches, slots), 1)
    repeat = jnp.where(place // SLOT == owner, 1.0, 0.0).astype(BF)
    counts = jnp.broadcast_to(count_ref[...].astype(F32), (8, patches)).astype(BF)
    spread = dot(counts, repeat)[:1].astype(I32)
    slot = lax.broadcasted_iota(I32, (1, slots), 1) % SLOT
    live = jnp.where(slot < spread, rows_ref[...], -1)
    live_ref[...] = live
    nodes = nodes_ref[...]
    depth = low_ref.shape[0]
    halo = dot(pick(column(halo_ref[...]), width), nodes).astype(BF)
    low_ref[...] = halo[:depth]
    high_ref[...] = halo[depth:]
    flush(low_ref, high_ref, live_ref)
    col = column(live)
    for r in tiles(slots):
        out_ref[r] = dot(pick(col[r], width), nodes).astype(BF)


def edge_kernel(
    dst_ref, nodes_ref, wb_ref, src_ref, low_ref, high_ref, wa_ref, edges_ref, wc_ref, second_ref,
    slope_ref, agg_ref, msg_ref, hid_ref,
):
    count, width = nodes_ref.shape
    inner = edges_ref.shape[0] - edges_ref.shape[0] // 4
    dst = column(dst_ref[...])
    nodes = nodes_ref[...]
    src = column(src_ref[...])
    halo = jnp.concatenate([low_ref[...], high_ref[...]], axis=0)
    for r in tiles(edges_ref.shape[0]):
        if r.stop <= inner:
            feat = dot(pick(src[r], count), nodes).astype(BF)
        else:
            feat = dot(pick(src[r] - float(count), halo.shape[0]), halo).astype(BF)
        own = dot(pick(dst[r], count), nodes).astype(BF)
        pre = dot(own, wb_ref[...]) + dot(feat, wa_ref[...]) + dot(edges_ref[r], wc_ref[...])
        sigma = jax.nn.sigmoid(pre)
        hid_ref[r] = (pre * sigma).astype(BF)
        slope_ref[r] = (sigma * (1.0 + pre * (1.0 - sigma))).astype(BF)
    flush(slope_ref)
    for r in tiles(count):
        agg = dot(pick_t(dst_ref[...], r.start, TILE), hid_ref[...]).astype(BF)
        agg_ref[r] = agg
        msg_ref[r] = dot(agg, second_ref[...])


def put(ref, index, value, first):
    half = value.shape[1] // 2
    lane = half // 2
    step = value.shape[0] // RING
    fine = step // RING
    own = jnp.where(first, value[:, :half], value[:, half:]).astype(BF)
    send = jnp.where(first, value[:, half:], value[:, :half]).astype(BF)
    for buffer, part in ((ref.own, own), (ref.send, send)):
        for i in range(RING):
            buffer[index, 0, i] = part[i * step : (i + 1) * step, :lane]
            for j in range(RING):
                start = i * step + j * fine
                buffer[index, 1, j, i * fine : (i + 1) * fine] = part[start : start + fine, lane:]


class Blocks:
    def __init__(self, own, send):
        self.own, self.send = own, send


def core_kernel(
    side_ref, target_ref, margin_ref, recv_ref, msg_ref, nodes_ref, na_ref, nb_ref, cot_ref, nsec_ref,
    dst_ref, esec_ref, slope_ref, agg_ref, edges_ref, src_ref, low_ref, high_ref, wa_ref,
    send_ref, ret_ref, own_ref, new_ref, part_ref, gedge_ref, bysrc_ref, bydst_ref, glow_ref, ghigh_ref,
    pooled_ref, hid_ref, gnode_ref, gpool_ref, turned_ref,
    *, patches, scale
):
    count, width = nodes_ref.shape
    inner = edges_ref.shape[0] - edges_ref.shape[0] // 4
    depth = low_ref.shape[0]
    first = side_ref[0] == 0
    target, margin = target_ref[...], margin_ref[...]
    for r in tiles(count):
        coupled = dot(pick_t(target, r.start, TILE, margin), recv_ref[...])
        pooled = (msg_ref[r] + coupled).astype(BF)
        pooled_ref[r] = pooled
        nodes = nodes_ref[r]
        pre = dot(nodes, na_ref[...]) + dot(pooled, nb_ref[...])
        sigma = jax.nn.sigmoid(pre)
        hidden = (pre * sigma).astype(BF)
        hid_ref[r] = hidden
        slope = sigma * (1.0 + pre * (1.0 - sigma))
        gnode = (dot_nt(cot_ref[r], nsec_ref[...]) * slope).astype(BF)
        gnode_ref[r] = gnode
        gpool_ref[r] = dot_nt(gnode, nb_ref[...]).astype(BF)
        new_ref[r] = (nodes.astype(F32) + dot(hidden, nsec_ref[...])).astype(BF)
        part_ref[r] = cot_ref[r].astype(F32) + dot_nt(gnode, na_ref[...])
    flush(new_ref, part_ref)
    gpool = gpool_ref[...]
    col, weight = column(target), column(margin)
    for r in tiles(recv_ref.shape[0]):
        ret_ref[r] = dot(pick(col[r], count, weight[r]), gpool).astype(BF)
    flush(ret_ref)
    dst_row, src_row = dst_ref[...], src_ref[...]
    dst = column(dst_row)
    for r in tiles(edges_ref.shape[0]):
        message = dot(pick(dst[r], count), gpool).astype(BF)
        gedge_ref[r] = (dot_nt(message, esec_ref[...]) * slope_ref[r].astype(F32)).astype(BF)
    flush(gedge_ref)
    for r in tiles(count):
        bydst_ref[r] = dot(pick_t(dst_row, r.start, TILE), gedge_ref[...]).astype(BF)
        bysrc_ref[r] = dot(pick_t(src_row[:, :inner], r.start, TILE), gedge_ref[:inner]).astype(BF)
    flush(bysrc_ref, bydst_ref)
    halo = dot(pick_t(src_row[:, inner:], count, 2 * depth), gedge_ref[inner:]).astype(BF)
    back = dot_nt(halo, wa_ref[...]).astype(BF)
    glow_ref[...] = back[:depth]
    ghigh_ref[...] = back[depth:]
    flush(glow_ref, ghigh_ref)
    order = row_order(side_ref[1], width, patches)
    blocks = Blocks(own_ref, send_ref)
    turned_ref[...] = dot_nt(order, nodes_ref[...]).astype(BF)
    rim = dot_nt(order, jnp.concatenate([low_ref[...], high_ref[...]], axis=0)).astype(BF)
    put(blocks, 0, (dot(turned_ref[...], bysrc_ref[...]) + dot(rim, halo)) * scale, first)
    put(blocks, 1, dot(turned_ref[...], bydst_ref[...]) * scale, first)
    put(blocks, 4, dot(turned_ref[...], gnode_ref[...]) * scale, first)
    pairs = ((2, edges_ref, gedge_ref), (3, agg_ref, gpool_ref), (5, pooled_ref, gnode_ref), (6, hid_ref, cot_ref))
    for index, left, right in pairs:
        turned = dot_nt(order, left[...]).astype(BF)
        put(blocks, index, dot(turned, right[...]) * scale, first)


def edge_rest_kernel(
    gpre_ref, wc_ref, bysrc_ref, wa_ref, bydst_ref, wb_ref, part_ref, edge_ref, total_ref
):
    count, width = bysrc_ref.shape
    for r in tiles(gpre_ref.shape[0]):
        edge_ref[r] = dot_nt(gpre_ref[r], wc_ref[...]).astype(BF)
    flush(edge_ref)
    for r in tiles(count):
        total_ref[r] = (
            part_ref[r]
            + dot_nt(bysrc_ref[r], wa_ref[...])
            + dot_nt(bydst_ref[r], wb_ref[...])
        )


def last_kernel(live_ref, halo_ref, total_ref, low_ref, high_ref, back_ref, out_ref):
    halo_back = jnp.concatenate([low_ref[...], high_ref[...]], axis=0)
    for r in tiles(total_ref.shape[0]):
        out_ref[r] = (
            total_ref[r]
            + dot(pick_t(halo_ref[...], r.start, TILE), halo_back)
            + dot(pick_t(live_ref[...], r.start, TILE), back_ref[...])
        ).astype(BF)


def from_partner(value):
    return lax.ppermute(value, "mesh", [(0, 1), (1, 0)])


def shift(value, step):
    count = lax.axis_size("patch")
    return lax.ppermute(value, "patch", [(i, (i + step) % count) for i in range(count)])


def route(crossed):
    rows, width = crossed.shape
    patches = lax.axis_size("patch")
    crossed = crossed.reshape(patches, rows // patches, width)
    routed = lax.all_to_all(crossed, "patch", split_axis=0, concat_axis=0, tiled=True)
    return routed.reshape(rows, width)


def hop(value, dz=0, dy=0, dx=0):
    depth = lax.axis_size("patch") // PLANE
    pairs = []
    for p in range(depth * PLANE):
        z, y, x = p // PLANE, p // RING % RING, p % RING
        pairs.append((p, (z + dz) % depth * PLANE + (y + dy) % RING * RING + (x + dx) % RING))
    return lax.ppermute(value, "patch", pairs)


def join_kernel(own_ref, other_ref, *outs):
    for index, out in enumerate(outs):
        c, d = index // RING, index % RING
        out[...] = (own_ref[:, c, d].astype(F32) + other_ref[:, c, d].astype(F32)).astype(BF)


def total_of(refs):
    total = refs[0][...].astype(F32)
    for ref in refs[1:]:
        total = total + ref[...].astype(F32)
    return total


def plane_kernel(*refs):
    for c in range(2):
        total = total_of(refs[c * RING : (c + 1) * RING])
        fine = total.shape[1] // RING
        for d in range(RING):
            refs[(2 + c) * RING + d][...] = total[:, d * fine : (d + 1) * fine].astype(BF)


def depth_kernel(place_ref, *refs):
    ins, (keep_ref, send_ref, hold) = refs[: 2 * RING], refs[2 * RING :]
    depth = hold.shape[0]
    hold[...] = jnp.zeros(hold.shape, F32)
    for c in range(2):
        total = total_of(ins[c * RING : (c + 1) * RING])
        blocks, rows, lane = total.shape
        fine = rows // depth
        for block in range(blocks):
            for d in range(depth):
                hold[d, block * fine : (block + 1) * fine, c * lane : (c + 1) * lane] = total[
                    block, d * fine : (d + 1) * fine
                ]
    even = (place_ref[1] // PLANE) % 2 == 0
    for j in range(depth // 2):
        low, high = hold[2 * j], hold[2 * j + 1]
        keep_ref[j] = jnp.where(even, low, high)
        send_ref[j] = jnp.where(even, high, low).astype(BF)


def pair_kernel(place_ref, keep_ref, other_ref, *outs):
    mine = place_ref[1] // PLANE // 2
    for d, out in enumerate(outs):
        j = (mine + d) % len(outs)
        out[...] = keep_ref[j] + other_ref[j].astype(F32)


def small_call(kernel, place, args, outs, scratch=()):
    return pl.pallas_call(
        kernel,
        out_shape=tuple(outs),
        in_specs=[SMEM] + [VMEM] * len(args),
        out_specs=tuple([VMEM] * len(outs)),
        scratch_shapes=list(scratch),
        compiler_params=pltpu.CompilerParams(vmem_limit_bytes=14 * 2**20),
        cost_estimate=cost(list(args) + list(outs), 0),
    )(place, *args)


def spread(pieces, axes):
    return [
        pieces[c * RING + d] if d == 0 else hop(pieces[c * RING + d], **{axis: d})
        for c, axis in enumerate(axes)
        for d in range(RING)
    ]


def weight_sums(own, other, place, tied):
    patches = lax.axis_size("patch")
    depth = patches // PLANE
    blocks, _, _, rows, lane = own.shape
    fine = rows // RING // depth
    pieces = call(join_kernel, (own, other), (shape(BF, blocks, rows, lane),) * (2 * RING))
    pieces = spread(pieces, ("dx", "dy"))
    pieces[1], tied = lax.optimization_barrier((pieces[1], tied))
    pieces = call(plane_kernel, pieces, (shape(BF, blocks, rows // RING, lane),) * (2 * RING))
    pieces = spread(pieces, ("dy", "dx"))
    padded = (blocks * fine + 15) // 16 * 16
    half = depth // 2
    keep, send = small_call(
        depth_kernel,
        place,
        pieces,
        (shape(F32, half, padded, 2 * lane), shape(BF, half, padded, 2 * lane)),
        scratch=(pltpu.VMEM((depth, padded, 2 * lane), F32),),
    )
    pairs = [(p, (p // PLANE ^ 1) * PLANE + p % PLANE) for p in range(patches)]
    other = lax.ppermute(send, "patch", pairs)
    pieces = small_call(pair_kernel, place, (keep, other), (shape(F32, padded, 2 * lane),) * half)
    own = pieces[0]
    for d in range(1, half):
        own = own + hop(pieces[d], dz=2 * d)
    other = from_partner(own)
    first = lax.axis_index("mesh") == 0
    both = jnp.concatenate([jnp.where(first, own, other), jnp.where(first, other, own)], axis=1)
    return both[: blocks * fine].reshape(blocks, fine * 4 * lane), tied


def shards(
    nodes,
    edges,
    cot_nodes,
    weights,
    edge_src,
    edge_dst,
    halo_rows,
    couple_rows,
    couple_count,
    couple_target,
    couple_weight,
):
    nodes_own = nodes[0]
    edges_own = edges[0]
    cotangent = cot_nodes[0]
    count, width = nodes_own.shape
    edge_count = edges_own.shape[0]
    depth = halo_rows.shape[1] // 2
    patches = lax.axis_size("patch")
    slots = couple_rows.shape[2]
    scale = 1.0 / math.sqrt(2 * patches * edge_count)
    side = jnp.stack([lax.axis_index("mesh"), lax.axis_index("patch")]).astype(I32)
    target, margin = couple_target[0], couple_weight[0]
    unit = 2 * width * width

    def weight(block):
        return Far(weights, block * width, width)

    def weight(block):
        return Far(weights, block * width, width)

    outgoing, low_out, high_out, live = stream(
        send_kernel,
        (couple_rows[0], couple_count[0], halo_rows, nodes_own),
        (shape(BF, slots, width), shape(BF, depth, width), shape(BF, depth, width), shape(I32, 1, slots)),
        flops=(slots + 2 * depth) * unit,
    )
    crossed = from_partner(outgoing)
    low, high = shift(high_out, 1), shift(low_out, -1)
    crossed, low, high = lax.optimization_barrier((crossed, low, high))
    received = route(crossed)
    slope, agg, message = stream(
        edge_kernel,
        (
            edge_dst, nodes_own, weight(1), edge_src, low, high, weight(0), edges_own, weight(2),
            weight(3),
        ),
        (shape(BF, edge_count, width), shape(BF, count, width), shape(F32, count, width)),
        scratch=(pltpu.VMEM((edge_count, width), BF),),
        flops=edge_count * 6 * unit,
    )
    square = shape(BF, count, width)
    grads = shape(BF, 7, 2, RING, width // RING, width // 4)
    rim = shape(BF, depth, width)
    slot_block = shape(BF, slots, width)
    edge_block = shape(BF, edge_count, width)
    total = shape(F32, count, width)
    send, returned, own, new_nodes, part, grad_edge_pre, by_source, by_target, grad_low, grad_high = stream(
        lambda *refs: core_kernel(*refs, patches=patches, scale=scale),
        (
            side, target, margin, received, message, nodes_own, weight(4), weight(5), cotangent,
            weight(6), edge_dst, weight(3), slope, agg, edges_own, edge_src, low, high, weight(0),
        ),
        (grads, slot_block, grads, square, total, edge_block, square, square, rim, rim),
        scratch=[pltpu.VMEM((count, width), BF)] * 5,
        flops=edge_count * 18 * unit,
    )
    other = from_partner(send)
    crossed_back = from_partner(returned)
    back_low, back_high = shift(grad_high, 1), shift(grad_low, -1)
    summed, tied = weight_sums(own, other, side, (crossed_back, back_low, back_high))
    crossed_back, back_low, back_high = tied
    couple_back = route(crossed_back)
    edge_grads, total = stream(
        edge_rest_kernel,
        (grad_edge_pre, weight(2), by_source, weight(0), by_target, weight(1), part),
        (edge_block, total),
        flops=edge_count * 2 * unit,
    )
    (node_grads,) = stream(
        last_kernel,
        (live, halo_rows, total, back_low, back_high, couple_back),
        (square,),
        flops=count * 2 * unit,
    )
    return (new_nodes[None], node_grads[None], edge_grads[None], summed)


def solution(mesh):
    return jax.shard_map(
        shards,
        mesh=mesh,
        in_specs=(
            P("mesh", "patch", None),
            P("mesh", "patch", None),
            P("mesh", "patch", None),
            P(),
            P("mesh", "patch"),
            P("mesh", "patch"),
            P("mesh", "patch"),
            P("mesh", "patch", None),
            P("mesh", "patch", None),
            P("mesh", "patch", None),
            P("mesh", "patch", None),
        ),
        out_specs=(
            P("mesh", "patch", None),
            P("mesh", "patch", None),
            P("mesh", "patch", None),
            P(None, "patch"),
        ),
        check_vma=False,
    )
```

```python
import math

import jax
import jax.numpy as jnp
from jax import lax
from jax.experimental import pallas as pl
from jax.experimental.pallas import tpu as pltpu
from jax.sharding import PartitionSpec as P

SLOT = 8
RING = 4
PLANE = RING * RING
TILE = 256
LIMIT = 61 * 2**20 - 2**16
BF = jnp.bfloat16
F32 = jnp.float32
I32 = jnp.int32
VMEM = pl.BlockSpec(memory_space=pltpu.VMEM)
SMEM = pl.BlockSpec(memory_space=pltpu.SMEM)


def dot(a, b):
    return jnp.dot(a, b, preferred_element_type=F32)


def dot_nt(a, b):
    return lax.dot_general(a, b, (((1,), (1,)), ((), ())), preferred_element_type=F32)


def column(row):
    return jnp.transpose(jnp.broadcast_to(row.astype(F32), (128, row.shape[1])))


def pick(col, count, value=None):
    base = lax.broadcasted_iota(I32, (col.shape[0], 128), 1).astype(F32)
    one = jnp.ones_like(base) if value is None else value
    parts = [jnp.where(col == base + float(k), one, 0.0).astype(BF) for k in range(0, count, 128)]
    return parts[0] if len(parts) == 1 else jnp.concatenate(parts, axis=1)


def pick_t(row, start, size, value=None):
    base = lax.broadcasted_iota(I32, (size, row.shape[1]), 0) + start
    one = jnp.ones(base.shape, F32) if value is None else jnp.broadcast_to(value, base.shape)
    return jnp.where(base == row, one, 0.0).astype(BF)


def row_order(place, width, patches):
    fine = width // patches
    depth = patches // PLANE
    row = lax.broadcasted_iota(I32, (width, width), 0)
    col = lax.broadcasted_iota(I32, (width, width), 1)
    dx, dy = row // (width // RING), (row // (width // PLANE)) % RING
    dz, offset = (row // fine) % depth, row % fine
    x, y = place % RING, (place // RING) % RING
    patch = dz * PLANE + (y + dy) % RING * RING + (x + dx) % RING
    return jnp.where(col == patch * fine + offset, 1.0, 0.0).astype(BF)


def tiles(count):
    return [slice(i, i + TILE) for i in range(0, count, TILE)]


class Far:
    def __init__(self, array, start=0, size=None):
        self.array = array
        self.start = start
        self.size = array.shape[0] if size is None else size


class Fetched:
    def __init__(self, copy, buffer):
        self.copy, self.buffer, self.waited = copy, buffer, False
        self.shape = buffer.shape

    def wait(self):
        if not self.waited:
            self.copy.wait()
            self.waited = True

    def __getitem__(self, index):
        self.wait()
        return self.buffer[index]


class Staged:
    def __init__(self, copy, buffer):
        self.copy, self.buffer, self.sent = copy, buffer, False
        self.shape = buffer.shape

    def __getitem__(self, index):
        return self.buffer[index]

    def __setitem__(self, index, value):
        self.buffer[index] = value

    def flush(self):
        if not self.sent:
            self.copy.start()
            self.sent = True


def flush(*refs):
    for ref in refs:
        ref.flush()


def cost(arrays, flops):
    size = sum(math.prod(a.shape) * a.dtype.itemsize for a in arrays)
    return pl.CostEstimate(flops=flops, bytes_accessed=size, transcendentals=0)


def call(kernel, args, outs):
    return pl.pallas_call(
        kernel,
        out_shape=tuple(outs),
        in_specs=[VMEM] * len(args),
        out_specs=tuple([VMEM] * len(outs)),
        compiler_params=pltpu.CompilerParams(vmem_limit_bytes=14 * 2**20),
        cost_estimate=cost(list(args) + list(outs), 0),
    )(*args)


def stream(kernel, args, outs, scratch=(), flops=0):
    args = [a if isinstance(a, Far) or a.ndim == 1 else Far(a) for a in args]
    far = [i for i, a in enumerate(args) if isinstance(a, Far)]
    arrays = [a.array if isinstance(a, Far) else a for a in args]
    held = [
        pltpu.VMEM((args[i].size,) + args[i].array.shape[1:], args[i].array.dtype) for i in far
    ]
    held += [pltpu.VMEM(o.shape, o.dtype) for o in outs]
    hbm = pl.BlockSpec(memory_space=pltpu.HBM)
    ins, made, moved = len(args), len(args) + len(outs), len(far) + len(outs)

    def body(*refs):
        buffers, sems, rest = refs[made : made + moved], refs[made + moved], refs[made + moved + 1 :]
        reads = list(refs[:ins])
        for k, i in enumerate(far):
            source = reads[i].at[args[i].start : args[i].start + args[i].size]
            copy = pltpu.make_async_copy(source, buffers[k], sems.at[k])
            copy.start()
            reads[i] = Fetched(copy, buffers[k])
        writes = []
        for k, out in enumerate(refs[ins:made], len(far)):
            writes.append(Staged(pltpu.make_async_copy(buffers[k], out, sems.at[k]), buffers[k]))
        kernel(*reads, *writes, *rest)
        flush(*writes)
        for i in far:
            reads[i].wait()
        for write in writes:
            write.copy.wait()

    return pl.pallas_call(
        body,
        out_shape=tuple(outs),
        in_specs=[hbm if isinstance(a, Far) else SMEM for a in args],
        out_specs=tuple([hbm] * len(outs)),
        scratch_shapes=held + [pltpu.SemaphoreType.DMA((moved,))] + list(scratch),
        compiler_params=pltpu.CompilerParams(vmem_limit_bytes=LIMIT),
        cost_estimate=cost(arrays + list(outs), flops),
    )(*arrays)


def shape(dtype, *dims):
    return jax.ShapeDtypeStruct(dims, dtype)


def send_kernel(rows_ref, count_ref, halo_ref, nodes_ref, out_ref, low_ref, high_ref, live_ref):
    slots = rows_ref.shape[1]
    patches = count_ref.shape[1]
    width = nodes_ref.shape[0]
    owner = lax.broadcasted_iota(I32, (patches, slots), 0)
    place = lax.broadcasted_iota(I32, (patches, slots), 1)
    repeat = jnp.where(place // SLOT == owner, 1.0, 0.0).astype(BF)
    counts = jnp.broadcast_to(count_ref[...].astype(F32), (8, patches)).astype(BF)
    spread = dot(counts, repeat)[:1].astype(I32)
    slot = lax.broadcasted_iota(I32, (1, slots), 1) % SLOT
    live = jnp.where(slot < spread, rows_ref[...], -1)
    live_ref[...] = live
    nodes = nodes_ref[...]
    depth = low_ref.shape[0]
    halo = dot(pick(column(halo_ref[...]), width), nodes).astype(BF)
    low_ref[...] = halo[:depth]
    high_ref[...] = halo[depth:]
    flush(low_ref, high_ref, live_ref)
    col = column(live)
    for r in tiles(slots):
        out_ref[r] = dot(pick(col[r], width), nodes).astype(BF)


def edge_kernel(
    dst_ref, nodes_ref, wb_ref, src_ref, low_ref, high_ref, wa_ref, edges_ref, wc_ref, second_ref,
    slope_ref, agg_ref, msg_ref, hid_ref,
):
    count, width = nodes_ref.shape
    inner = edges_ref.shape[0] - edges_ref.shape[0] // 4
    dst = column(dst_ref[...])
    nodes = nodes_ref[...]
    src = column(src_ref[...])
    halo = jnp.concatenate([low_ref[...], high_ref[...]], axis=0)
    for r in tiles(edges_ref.shape[0]):
        if r.stop <= inner:
            feat = dot(pick(src[r], count), nodes).astype(BF)
        else:
            feat = dot(pick(src[r] - float(count), halo.shape[0]), halo).astype(BF)
        own = dot(pick(dst[r], count), nodes).astype(BF)
        pre = dot(own, wb_ref[...]) + dot(feat, wa_ref[...]) + dot(edges_ref[r], wc_ref[...])
        sigma = jax.nn.sigmoid(pre)
        hid_ref[r] = (pre * sigma).astype(BF)
        slope_ref[r] = (sigma * (1.0 + pre * (1.0 - sigma))).astype(BF)
    flush(slope_ref)
    for r in tiles(count):
        agg = dot(pick_t(dst_ref[...], r.start, TILE), hid_ref[...]).astype(BF)
        agg_ref[r] = agg
        msg_ref[r] = dot(agg, second_ref[...])


def put(ref, index, value, first):
    half = value.shape[1] // 2
    lane = half // 2
    step = value.shape[0] // RING
    fine = step // RING
    own = jnp.where(first, value[:, :half], value[:, half:]).astype(BF)
    send = jnp.where(first, value[:, half:], value[:, :half]).astype(BF)
    for buffer, part in ((ref.own, own), (ref.send, send)):
        for i in range(RING):
            buffer[index, 0, i] = part[i * step : (i + 1) * step, :lane]
            for j in range(RING):
                start = i * step + j * fine
                buffer[index, 1, j, i * fine : (i + 1) * fine] = part[start : start + fine, lane:]


class Blocks:
    def __init__(self, own, send):
        self.own, self.send = own, send


def node_kernel(
    target_ref, margin_ref, recv_ref, msg_ref, nodes_ref, na_ref, nb_ref, cot_ref, nsec_ref,
    ret_ref, gpool_ref, pooled_ref, hid_ref, gnode_ref,
):
    count = nodes_ref.shape[0]
    target, margin = target_ref[...], margin_ref[...]
    for r in tiles(count):
        coupled = dot(pick_t(target, r.start, TILE, margin), recv_ref[...])
        pooled = (msg_ref[r] + coupled).astype(BF)
        pooled_ref[r] = pooled
        nodes = nodes_ref[r]
        pre = dot(nodes, na_ref[...]) + dot(pooled, nb_ref[...])
        sigma = jax.nn.sigmoid(pre)
        hidden = (pre * sigma).astype(BF)
        hid_ref[r] = hidden
        slope = sigma * (1.0 + pre * (1.0 - sigma))
        gnode = (dot_nt(cot_ref[r], nsec_ref[...]) * slope).astype(BF)
        gnode_ref[r] = gnode
        gpool_ref[r] = dot_nt(gnode, nb_ref[...]).astype(BF)
    flush(gpool_ref, pooled_ref, hid_ref, gnode_ref)
    gpool = gpool_ref[...]
    col, weight = column(target), column(margin)
    for r in tiles(recv_ref.shape[0]):
        ret_ref[r] = dot(pick(col[r], count, weight[r]), gpool).astype(BF)


def grad_kernel(
    side_ref, dst_ref, gpool_ref, esec_ref, slope_ref, src_ref, nodes_ref, low_ref, high_ref, edges_ref,
    gnode_ref, agg_ref, pooled_ref, hid_ref, cot_ref, wa_ref,
    send_ref, own_ref, gedge_ref, bysrc_ref, bydst_ref, glow_ref, ghigh_ref, turned_ref,
    *, patches, scale
):
    count, width = nodes_ref.shape
    inner = edges_ref.shape[0] - edges_ref.shape[0] // 4
    depth = low_ref.shape[0]
    first = side_ref[0] == 0
    gpool = gpool_ref[...]
    dst_row, src_row = dst_ref[...], src_ref[...]
    dst = column(dst_row)
    for r in tiles(edges_ref.shape[0]):
        message = dot(pick(dst[r], count), gpool).astype(BF)
        gedge_ref[r] = (dot_nt(message, esec_ref[...]) * slope_ref[r].astype(F32)).astype(BF)
    flush(gedge_ref)
    for r in tiles(count):
        bydst_ref[r] = dot(pick_t(dst_row, r.start, TILE), gedge_ref[...]).astype(BF)
        bysrc_ref[r] = dot(pick_t(src_row[:, :inner], r.start, TILE), gedge_ref[:inner]).astype(BF)
    flush(bysrc_ref, bydst_ref)
    halo = dot(pick_t(src_row[:, inner:], count, 2 * depth), gedge_ref[inner:]).astype(BF)
    back = dot_nt(halo, wa_ref[...]).astype(BF)
    glow_ref[...] = back[:depth]
    ghigh_ref[...] = back[depth:]
    flush(glow_ref, ghigh_ref)
    order = row_order(side_ref[1], width, patches)
    blocks = Blocks(own_ref, send_ref)
    turned_ref[...] = dot_nt(order, nodes_ref[...]).astype(BF)
    rim = dot_nt(order, jnp.concatenate([low_ref[...], high_ref[...]], axis=0)).astype(BF)
    put(blocks, 0, (dot(turned_ref[...], bysrc_ref[...]) + dot(rim, halo)) * scale, first)
    put(blocks, 1, dot(turned_ref[...], bydst_ref[...]) * scale, first)
    put(blocks, 4, dot(turned_ref[...], gnode_ref[...]) * scale, first)
    pairs = ((2, edges_ref, gedge_ref), (3, agg_ref, gpool_ref), (5, pooled_ref, gnode_ref), (6, hid_ref, cot_ref))
    for index, left, right in pairs:
        turned = dot_nt(order, left[...]).astype(BF)
        put(blocks, index, dot(turned, right[...]) * scale, first)


def rest_kernel(
    gedge_ref, wc_ref, hid_ref, nsec_ref, nodes_ref, bysrc_ref, wa_ref, bydst_ref, wb_ref, gnode_ref, na_ref,
    cot_ref, edge_ref, new_ref, total_ref,
):
    for r in tiles(gedge_ref.shape[0]):
        edge_ref[r] = dot_nt(gedge_ref[r], wc_ref[...]).astype(BF)
    flush(edge_ref)
    for r in tiles(bysrc_ref.shape[0]):
        new_ref[r] = (nodes_ref[r].astype(F32) + dot(hid_ref[r], nsec_ref[...])).astype(BF)
    flush(new_ref)
    for r in tiles(bysrc_ref.shape[0]):
        total_ref[r] = (
            cot_ref[r].astype(F32)
            + dot_nt(bysrc_ref[r], wa_ref[...])
            + dot_nt(bydst_ref[r], wb_ref[...])
            + dot_nt(gnode_ref[r], na_ref[...])
        )


def last_kernel(live_ref, halo_ref, total_ref, low_ref, high_ref, back_ref, out_ref):
    halo_back = jnp.concatenate([low_ref[...], high_ref[...]], axis=0)
    for r in tiles(total_ref.shape[0]):
        out_ref[r] = (
            total_ref[r]
            + dot(pick_t(halo_ref[...], r.start, TILE), halo_back)
            + dot(pick_t(live_ref[...], r.start, TILE), back_ref[...])
        ).astype(BF)


def from_partner(value):
    return lax.ppermute(value, "mesh", [(0, 1), (1, 0)])


def shift(value, step):
    count = lax.axis_size("patch")
    return lax.ppermute(value, "patch", [(i, (i + step) % count) for i in range(count)])


def route(crossed):
    rows, width = crossed.shape
    patches = lax.axis_size("patch")
    crossed = crossed.reshape(patches, rows // patches, width)
    routed = lax.all_to_all(crossed, "patch", split_axis=0, concat_axis=0, tiled=True)
    return routed.reshape(rows, width)


def hop(value, dz=0, dy=0, dx=0):
    depth = lax.axis_size("patch") // PLANE
    pairs = []
    for p in range(depth * PLANE):
        z, y, x = p // PLANE, p // RING % RING, p % RING
        pairs.append((p, (z + dz) % depth * PLANE + (y + dy) % RING * RING + (x + dx) % RING))
    return lax.ppermute(value, "patch", pairs)


def join_kernel(own_ref, other_ref, *outs):
    for index, out in enumerate(outs):
        c, d = index // RING, index % RING
        out[...] = (own_ref[:, c, d].astype(F32) + other_ref[:, c, d].astype(F32)).astype(BF)


def total_of(refs):
    total = refs[0][...].astype(F32)
    for ref in refs[1:]:
        total = total + ref[...].astype(F32)
    return total


def plane_kernel(place_ref, *refs):
    ins, outs = refs[: 2 * RING], refs[2 * RING :]
    spots = (place_ref[1] // RING % RING, place_ref[1] % RING)
    for c, spot in enumerate(spots):
        keep_ref, send_ref = outs[2 * c : 2 * c + 2]
        total = total_of(ins[c * RING : (c + 1) * RING])
        fine = total.shape[1] // RING
        parts = [total[:, d * fine : (d + 1) * fine] for d in range(RING)]
        even = spot % 2 == 0
        keep_ref[0] = parts[0]
        keep_ref[1] = jnp.where(even, parts[3], parts[1])
        send_ref[0] = jnp.where(even, parts[1], parts[3]).astype(BF)
        send_ref[1] = parts[2].astype(BF)


def line_kernel(keep_x, other_x, keep_y, other_y, mine_x, send_x, mine_y, send_y):
    for keep, other, mine, send in ((keep_x, other_x, mine_x, send_x), (keep_y, other_y, mine_y, send_y)):
        mine[...] = keep[0] + other[0].astype(F32)
        send[...] = (keep[1] + other[1].astype(F32)).astype(BF)


def depth_kernel(place_ref, mine_x, other_x, mine_y, other_y, keep_ref, send_ref, hold):
    depth = hold.shape[0]
    hold[...] = jnp.zeros(hold.shape, F32)
    for c, (mine, other) in enumerate(((mine_x, other_x), (mine_y, other_y))):
        total = mine[...] + other[...].astype(F32)
        blocks, rows, lane = total.shape
        fine = rows // depth
        for block in range(blocks):
            for d in range(depth):
                hold[d, block * fine : (block + 1) * fine, c * lane : (c + 1) * lane] = total[
                    block, d * fine : (d + 1) * fine
                ]
    even = (place_ref[1] // PLANE) % 2 == 0
    for j in range(depth // 2):
        low, high = hold[2 * j], hold[2 * j + 1]
        keep_ref[j] = jnp.where(even, low, high)
        send_ref[j] = jnp.where(even, high, low).astype(BF)


def halve_kernel(place_ref, keep_ref, other_ref, mine_ref, send_ref, *, bit):
    clear = (place_ref[1] // PLANE >> bit) % 2 == 0
    for k in range(mine_ref.shape[0]):
        low = keep_ref[2 * k] + other_ref[2 * k].astype(F32)
        high = keep_ref[2 * k + 1] + other_ref[2 * k + 1].astype(F32)
        mine_ref[k] = jnp.where(clear, low, high)
        send_ref[k] = jnp.where(clear, high, low).astype(send_ref.dtype)


def finish_kernel(place_ref, own_ref, own_far, other_ref, other_far, out_ref):
    rows = out_ref.shape[0]
    own = own_ref[0, :rows] + own_far[0, :rows]
    other = other_ref[0, :rows] + other_far[0, :rows]
    first = place_ref[0] == 0
    lane = own.shape[1]
    out_ref[:, :lane] = jnp.where(first, own, other)
    out_ref[:, lane:] = jnp.where(first, other, own)


def small_call(kernel, place, args, outs, scratch=()):
    return pl.pallas_call(
        kernel,
        out_shape=tuple(outs),
        in_specs=[SMEM] + [VMEM] * len(args),
        out_specs=tuple([VMEM] * len(outs)),
        scratch_shapes=list(scratch),
        compiler_params=pltpu.CompilerParams(vmem_limit_bytes=14 * 2**20),
        cost_estimate=cost(list(args) + list(outs), 0),
    )(place, *args)


def spread(pieces, axes):
    return [
        pieces[c * RING + d] if d == 0 else hop(pieces[c * RING + d], **{axis: d})
        for c, axis in enumerate(axes)
        for d in range(RING)
    ]


def flip(value, dz=0, dy=0, dx=0, core=0):
    patches = lax.axis_size("patch")
    mask = dz * PLANE + dy * RING + dx
    pairs = [
        (m * patches + p, (m ^ core) * patches + (p ^ mask)) for m in range(2) for p in range(patches)
    ]
    return lax.ppermute(value, ("mesh", "patch"), pairs)


def weight_sums(own, other, place, tied, last):
    depth = lax.axis_size("patch") // PLANE
    blocks, _, _, rows, lane = own.shape
    fine = rows // RING // depth
    padded = (blocks * fine + 15) // 16 * 16
    pieces = call(join_kernel, (own, other), (shape(BF, blocks, rows, lane),) * (2 * RING))
    pieces = spread(pieces, ("dx", "dy"))
    pieces, tied = lax.optimization_barrier((pieces, tied))
    pair = lambda dtype: shape(dtype, 2, blocks, rows // RING, lane)
    one = lambda dtype: shape(dtype, blocks, rows // RING, lane)
    keep_x, send_x, keep_y, send_y = small_call(
        plane_kernel, place, pieces, (pair(F32), pair(BF), pair(F32), pair(BF))
    )
    mine_x, send_x, mine_y, send_y = call(
        line_kernel,
        (keep_x, flip(send_x, dy=1), keep_y, flip(send_y, dx=1)),
        (one(F32), one(BF), one(F32), one(BF)),
    )
    other_x, other_y = flip(send_x, dy=3), flip(send_y, dx=3)
    half = depth // 2
    deep = lambda dtype, count: shape(dtype, count, padded, 2 * lane)
    keep, send = small_call(
        depth_kernel,
        place,
        (mine_x, other_x, mine_y, other_y),
        (deep(F32, half), deep(BF, half)),
        scratch=(pltpu.VMEM((depth, padded, 2 * lane), F32),),
    )
    bit = 0
    while half > 1:
        other = flip(send, dz=1 << bit)
        bit, half = bit + 1, half // 2
        keep, send = small_call(
            lambda *refs, bit=bit: halve_kernel(*refs, bit=bit),
            place,
            (keep, other),
            (deep(F32, half), deep(F32 if half == 1 else BF, half)),
        )
    tied, last, send = lax.optimization_barrier((tied, last(tied), send))
    far = 1 << bit
    (result,) = small_call(
        finish_kernel,
        place,
        (keep, flip(send, dz=far), flip(keep, core=1), flip(send, dz=far, core=1)),
        (shape(F32, blocks * fine, 4 * lane),),
    )
    return result.reshape(blocks, fine * 4 * lane), tied, last


def shards(
    nodes,
    edges,
    cot_nodes,
    weights,
    edge_src,
    edge_dst,
    halo_rows,
    couple_rows,
    couple_count,
    couple_target,
    couple_weight,
):
    nodes_own = nodes[0]
    edges_own = edges[0]
    cotangent = cot_nodes[0]
    count, width = nodes_own.shape
    edge_count = edges_own.shape[0]
    depth = halo_rows.shape[1] // 2
    patches = lax.axis_size("patch")
    slots = couple_rows.shape[2]
    scale = 1.0 / math.sqrt(2 * patches * edge_count)
    side = jnp.stack([lax.axis_index("mesh"), lax.axis_index("patch")]).astype(I32)
    target, margin = couple_target[0], couple_weight[0]
    unit = 2 * width * width

    def weight(block):
        return Far(weights, block * width, width)

    def weight(block):
        return Far(weights, block * width, width)

    outgoing, low_out, high_out, live = stream(
        send_kernel,
        (couple_rows[0], couple_count[0], halo_rows, nodes_own),
        (shape(BF, slots, width), shape(BF, depth, width), shape(BF, depth, width), shape(I32, 1, slots)),
        flops=(slots + 2 * depth) * unit,
    )
    crossed = from_partner(outgoing)
    low, high = shift(high_out, 1), shift(low_out, -1)
    crossed, low, high = lax.optimization_barrier((crossed, low, high))
    received = route(crossed)
    slope, agg, message = stream(
        edge_kernel,
        (
            edge_dst, nodes_own, weight(1), edge_src, low, high, weight(0), edges_own, weight(2),
            weight(3),
        ),
        (shape(BF, edge_count, width), shape(BF, count, width), shape(F32, count, width)),
        scratch=(pltpu.VMEM((edge_count, width), BF),),
        flops=edge_count * 6 * unit,
    )
    square = shape(BF, count, width)
    grads = shape(BF, 7, 2, RING, width // RING, width // 4)
    rim = shape(BF, depth, width)
    slot_block = shape(BF, slots, width)
    edge_block = shape(BF, edge_count, width)
    returned, grad_pooled, pooled, hidden, grad_node_pre = stream(
        node_kernel,
        (target, margin, received, message, nodes_own, weight(4), weight(5), cotangent, weight(6)),
        (slot_block, square, square, square, square),
        flops=count * 8 * unit,
    )
    crossed_back = from_partner(returned)
    couple_back = route(crossed_back)
    grad_pooled, crossed_back = lax.optimization_barrier((grad_pooled, crossed_back))
    send, own, grad_edge_pre, by_source, by_target, grad_low, grad_high = stream(
        lambda *refs: grad_kernel(*refs, patches=patches, scale=scale),
        (
            side, edge_dst, grad_pooled, weight(3), slope, edge_src, nodes_own, low, high, edges_own,
            grad_node_pre, agg, pooled, hidden, cotangent, weight(0),
        ),
        (grads, grads, edge_block, square, square, rim, rim),
        scratch=[pltpu.VMEM((count, width), BF)],
        flops=edge_count * 14 * unit,
    )
    other = from_partner(send)
    back_low, back_high = shift(grad_high, 1), shift(grad_low, -1)
    edge_grads, new_nodes, total = stream(
        rest_kernel,
        (
            grad_edge_pre, weight(2), hidden, weight(6), nodes_own, by_source, weight(0), by_target,
            weight(1), grad_node_pre, weight(4), cotangent,
        ),
        (edge_block, square, shape(F32, count, width)),
        flops=edge_count * 3 * unit,
    )

    def last(tied):
        low_rows, high_rows, sums = tied
        (grads,) = stream(
            last_kernel,
            (live, halo_rows, sums, low_rows, high_rows, couple_back),
            (square,),
            flops=count * 2 * unit,
        )
        return grads

    summed, _, node_grads = weight_sums(own, other, side, (back_low, back_high, total), last)
    return (new_nodes[None], node_grads[None], edge_grads[None], summed)


def solution(mesh):
    return jax.shard_map(
        shards,
        mesh=mesh,
        in_specs=(
            P("mesh", "patch", None),
            P("mesh", "patch", None),
            P("mesh", "patch", None),
            P(),
            P("mesh", "patch"),
            P("mesh", "patch"),
            P("mesh", "patch"),
            P("mesh", "patch", None),
            P("mesh", "patch", None),
            P("mesh", "patch", None),
            P("mesh", "patch", None),
        ),
        out_specs=(
            P("mesh", "patch", None),
            P("mesh", "patch", None),
            P("mesh", "patch", None),
            P(None, "patch"),
        ),
        check_vma=False,
    )
```

```python
import math

import jax
import jax.numpy as jnp
from jax import lax
from jax.experimental import pallas as pl
from jax.experimental.pallas import tpu as pltpu
from jax.sharding import PartitionSpec as P

SLOT = 8
RING = 4
PLANE = RING * RING
TILE = 256
LIMIT = 61 * 2**20 - 2**16
BF = jnp.bfloat16
F32 = jnp.float32
I32 = jnp.int32
VMEM = pl.BlockSpec(memory_space=pltpu.VMEM)
SMEM = pl.BlockSpec(memory_space=pltpu.SMEM)


def dot(a, b):
    return jnp.dot(a, b, preferred_element_type=F32)


def dot_nt(a, b):
    return lax.dot_general(a, b, (((1,), (1,)), ((), ())), preferred_element_type=F32)


def column(row):
    return jnp.transpose(jnp.broadcast_to(row.astype(F32), (128, row.shape[1])))


def pick(col, count, value=None):
    base = lax.broadcasted_iota(I32, (col.shape[0], 128), 1).astype(F32)
    one = jnp.ones_like(base) if value is None else value
    parts = [jnp.where(col == base + float(k), one, 0.0).astype(BF) for k in range(0, count, 128)]
    return parts[0] if len(parts) == 1 else jnp.concatenate(parts, axis=1)


def pick_t(row, start, size, value=None):
    base = lax.broadcasted_iota(I32, (size, row.shape[1]), 0) + start
    one = jnp.ones(base.shape, F32) if value is None else jnp.broadcast_to(value, base.shape)
    return jnp.where(base == row, one, 0.0).astype(BF)


def row_order(place, width, patches):
    fine = width // patches
    depth = patches // PLANE
    row = lax.broadcasted_iota(I32, (width, width), 0)
    col = lax.broadcasted_iota(I32, (width, width), 1)
    dx, dy = row // (width // RING), (row // (width // PLANE)) % RING
    dz, offset = (row // fine) % depth, row % fine
    x, y = place % RING, (place // RING) % RING
    patch = dz * PLANE + (y + dy) % RING * RING + (x + dx) % RING
    return jnp.where(col == patch * fine + offset, 1.0, 0.0).astype(BF)


def tiles(count):
    return [slice(i, i + TILE) for i in range(0, count, TILE)]


class Far:
    def __init__(self, array, start=0, size=None):
        self.array = array
        self.start = start
        self.size = array.shape[0] if size is None else size


class Fetched:
    def __init__(self, copy, buffer):
        self.copy, self.buffer, self.waited = copy, buffer, False
        self.shape = buffer.shape

    def wait(self):
        if not self.waited:
            self.copy.wait()
            self.waited = True

    def __getitem__(self, index):
        self.wait()
        return self.buffer[index]


class Staged:
    def __init__(self, copies, buffer):
        self.copies, self.buffer, self.sent = copies, buffer, set()
        self.shape = buffer.shape

    def __getitem__(self, index):
        return self.buffer[index]

    def __setitem__(self, index, value):
        self.buffer[index] = value

    def flush(self, index=None):
        for i in range(len(self.copies)) if index is None else [index]:
            if i not in self.sent:
                self.copies[i].start()
                self.sent.add(i)

    def wait(self):
        for copy in self.copies:
            copy.wait()


def flush(self):
        if not self.sent:
            self.copy.start()
            self.sent = True


def flush(*refs):
    for ref in refs:
        ref.flush()


def cost(arrays, flops):
    size = sum(math.prod(a.shape) * a.dtype.itemsize for a in arrays)
    return pl.CostEstimate(flops=flops, bytes_accessed=size, transcendentals=0)


def call(kernel, args, outs):
    return pl.pallas_call(
        kernel,
        out_shape=tuple(outs),
        in_specs=[VMEM] * len(args),
        out_specs=tuple([VMEM] * len(outs)),
        compiler_params=pltpu.CompilerParams(vmem_limit_bytes=14 * 2**20),
        cost_estimate=cost(list(args) + list(outs), 0),
    )(*args)


def stream(kernel, args, outs, scratch=(), flops=0):
    args = [a if isinstance(a, Far) or a.ndim == 1 else Far(a) for a in args]
    far = [i for i, a in enumerate(args) if isinstance(a, Far)]
    arrays = [a.array if isinstance(a, Far) else a for a in args]
    held = [
        pltpu.VMEM((args[i].size,) + args[i].array.shape[1:], args[i].array.dtype) for i in far
    ]
    held += [pltpu.VMEM(o.shape, o.dtype) for o in outs]
    hbm = pl.BlockSpec(memory_space=pltpu.HBM)
    ins, made, moved = len(args), len(args) + len(outs), len(far) + len(outs)
    parts = [o.shape[0] if len(o.shape) > 3 else 1 for o in outs]

    def body(*refs):
        buffers, sems, rest = refs[made : made + moved], refs[made + moved], refs[made + moved + 1 :]
        reads = list(refs[:ins])
        for k, i in enumerate(far):
            source = reads[i].at[args[i].start : args[i].start + args[i].size]
            copy = pltpu.make_async_copy(source, buffers[k], sems.at[k])
            copy.start()
            reads[i] = Fetched(copy, buffers[k])
        writes = []
        used = len(far)
        for out, buffer, count in zip(refs[ins:made], buffers[len(far) :], parts):
            pairs = [(buffer, out)] if count == 1 else [(buffer.at[i], out.at[i]) for i in range(count)]
            copies = [pltpu.make_async_copy(x, y, sems.at[used + i]) for i, (x, y) in enumerate(pairs)]
            used += count
            writes.append(Staged(copies, buffer))
        kernel(*reads, *writes, *rest)
        flush(*writes)
        for i in far:
            reads[i].wait()
        for write in writes:
            write.wait()

    return pl.pallas_call(
        body,
        out_shape=tuple(outs),
        in_specs=[hbm if isinstance(a, Far) else SMEM for a in args],
        out_specs=tuple([hbm] * len(outs)),
        scratch_shapes=held + [pltpu.SemaphoreType.DMA((len(far) + sum(parts),))] + list(scratch),
        compiler_params=pltpu.CompilerParams(vmem_limit_bytes=LIMIT),
        cost_estimate=cost(arrays + list(outs), flops),
    )(*arrays)


def shape(dtype, *dims):
    return jax.ShapeDtypeStruct(dims, dtype)


def send_kernel(rows_ref, count_ref, halo_ref, nodes_ref, out_ref, low_ref, high_ref, live_ref):
    slots = rows_ref.shape[1]
    patches = count_ref.shape[1]
    width = nodes_ref.shape[0]
    owner = lax.broadcasted_iota(I32, (patches, slots), 0)
    place = lax.broadcasted_iota(I32, (patches, slots), 1)
    repeat = jnp.where(place // SLOT == owner, 1.0, 0.0).astype(BF)
    counts = jnp.broadcast_to(count_ref[...].astype(F32), (8, patches)).astype(BF)
    spread = dot(counts, repeat)[:1].astype(I32)
    slot = lax.broadcasted_iota(I32, (1, slots), 1) % SLOT
    live = jnp.where(slot < spread, rows_ref[...], -1)
    live_ref[...] = live
    nodes = nodes_ref[...]
    depth = low_ref.shape[0]
    halo = dot(pick(column(halo_ref[...]), width), nodes).astype(BF)
    low_ref[...] = halo[:depth]
    high_ref[...] = halo[depth:]
    flush(low_ref, high_ref, live_ref)
    col = column(live)
    for r in tiles(slots):
        out_ref[r] = dot(pick(col[r], width), nodes).astype(BF)


def edge_kernel(
    dst_ref, nodes_ref, wb_ref, na_ref, cot_ref, nsec_ref, src_ref, low_ref, high_ref, wa_ref, edges_ref, wc_ref,
    second_ref, slope_ref, agg_ref, msg_ref, half_ref, ghid_ref, hid_ref,
):
    count, width = nodes_ref.shape
    inner = edges_ref.shape[0] - edges_ref.shape[0] // 4
    dst = column(dst_ref[...])
    nodes = nodes_ref[...]
    src = column(src_ref[...])
    halo = jnp.concatenate([low_ref[...], high_ref[...]], axis=0)
    for r in tiles(edges_ref.shape[0]):
        if r.stop <= inner:
            feat = dot(pick(src[r], count), nodes).astype(BF)
        else:
            feat = dot(pick(src[r] - float(count), halo.shape[0]), halo).astype(BF)
        own = dot(pick(dst[r], count), nodes).astype(BF)
        pre = dot(own, wb_ref[...]) + dot(feat, wa_ref[...]) + dot(edges_ref[r], wc_ref[...])
        sigma = jax.nn.sigmoid(pre)
        hid_ref[r] = (pre * sigma).astype(BF)
        slope_ref[r] = (sigma * (1.0 + pre * (1.0 - sigma))).astype(BF)
    flush(slope_ref)
    for r in tiles(count):
        agg = dot(pick_t(dst_ref[...], r.start, TILE), hid_ref[...]).astype(BF)
        agg_ref[r] = agg
        msg_ref[r] = dot(agg, second_ref[...])
        half_ref[r] = dot(nodes_ref[r], na_ref[...])
        ghid_ref[r] = dot_nt(cot_ref[r], nsec_ref[...])


def put(ref, index, value, first):
    half = value.shape[1] // 2
    lane = half // 2
    step = value.shape[0] // RING
    fine = step // RING
    own = jnp.where(first, value[:, :half], value[:, half:]).astype(BF)
    send = jnp.where(first, value[:, half:], value[:, :half]).astype(BF)
    for buffer, part in ((ref.own, own), (ref.send, send)):
        for i in range(RING):
            buffer[index, 0, i] = part[i * step : (i + 1) * step, :lane]
            for j in range(RING):
                start = i * step + j * fine
                buffer[index, 1, j, i * fine : (i + 1) * fine] = part[start : start + fine, lane:]
        buffer.flush(index)


class Blocks:
    def __init__(self, own, send):
        self.own, self.send = own, send


def node_kernel(
    target_ref, margin_ref, recv_ref, msg_ref, half_ref, nb_ref, ghid_ref,
    ret_ref, gpool_ref, pooled_ref, hid_ref, gnode_ref,
):
    count = msg_ref.shape[0]
    target, margin = target_ref[...], margin_ref[...]
    for r in tiles(count):
        coupled = dot(pick_t(target, r.start, TILE, margin), recv_ref[...])
        pooled = (msg_ref[r] + coupled).astype(BF)
        pooled_ref[r] = pooled
        pre = half_ref[r] + dot(pooled, nb_ref[...])
        sigma = jax.nn.sigmoid(pre)
        hid_ref[r] = (pre * sigma).astype(BF)
        gnode = (ghid_ref[r] * (sigma * (1.0 + pre * (1.0 - sigma)))).astype(BF)
        gnode_ref[r] = gnode
        gpool_ref[r] = dot_nt(gnode, nb_ref[...]).astype(BF)
    flush(gpool_ref, pooled_ref, hid_ref, gnode_ref)
    gpool = gpool_ref[...]
    col, weight = column(target), column(margin)
    for r in tiles(recv_ref.shape[0]):
        ret_ref[r] = dot(pick(col[r], count, weight[r]), gpool).astype(BF)


def grad_kernel(
    side_ref, nodes_ref, gnode_ref, gpool_ref, agg_ref, dst_ref, esec_ref, slope_ref, src_ref, pooled_ref,
    edges_ref, hid_ref, cot_ref, low_ref, high_ref, wa_ref,
    send_ref, own_ref, gedge_ref, bysrc_ref, bydst_ref, glow_ref, ghigh_ref, turned_ref,
    *, patches, scale
):
    count, width = nodes_ref.shape
    inner = edges_ref.shape[0] - edges_ref.shape[0] // 4
    depth = low_ref.shape[0]
    first = side_ref[0] == 0
    order = row_order(side_ref[1], width, patches)
    blocks = Blocks(own_ref, send_ref)
    turned_ref[...] = dot_nt(order, nodes_ref[...]).astype(BF)
    put(blocks, 4, dot(turned_ref[...], gnode_ref[...]) * scale, first)
    put(blocks, 3, dot(dot_nt(order, agg_ref[...]).astype(BF), gpool_ref[...]) * scale, first)
    gpool = gpool_ref[...]
    dst_row, src_row = dst_ref[...], src_ref[...]
    dst = column(dst_row)
    for r in tiles(edges_ref.shape[0]):
        message = dot(pick(dst[r], count), gpool).astype(BF)
        gedge_ref[r] = (dot_nt(message, esec_ref[...]) * slope_ref[r].astype(F32)).astype(BF)
    flush(gedge_ref)
    for r in tiles(count):
        bydst_ref[r] = dot(pick_t(dst_row, r.start, TILE), gedge_ref[...]).astype(BF)
        bysrc_ref[r] = dot(pick_t(src_row[:, :inner], r.start, TILE), gedge_ref[:inner]).astype(BF)
    flush(bysrc_ref, bydst_ref)
    put(blocks, 1, dot(turned_ref[...], bydst_ref[...]) * scale, first)
    halo = dot(pick_t(src_row[:, inner:], count, 2 * depth), gedge_ref[inner:]).astype(BF)
    rim = dot_nt(order, jnp.concatenate([low_ref[...], high_ref[...]], axis=0)).astype(BF)
    put(blocks, 0, (dot(turned_ref[...], bysrc_ref[...]) + dot(rim, halo)) * scale, first)
    back = dot_nt(halo, wa_ref[...]).astype(BF)
    glow_ref[...] = back[:depth]
    ghigh_ref[...] = back[depth:]
    flush(glow_ref, ghigh_ref)
    pairs = ((2, edges_ref, gedge_ref), (5, pooled_ref, gnode_ref), (6, hid_ref, cot_ref))
    for index, left, right in pairs:
        turned = dot_nt(order, left[...]).astype(BF)
        put(blocks, index, dot(turned, right[...]) * scale, first)


def rest_kernel(
    gedge_ref, wc_ref, hid_ref, nsec_ref, nodes_ref, bysrc_ref, wa_ref, bydst_ref, wb_ref, gnode_ref, na_ref,
    cot_ref, edge_ref, new_ref, total_ref,
):
    for r in tiles(gedge_ref.shape[0]):
        edge_ref[r] = dot_nt(gedge_ref[r], wc_ref[...]).astype(BF)
    flush(edge_ref)
    for r in tiles(bysrc_ref.shape[0]):
        new_ref[r] = (nodes_ref[r].astype(F32) + dot(hid_ref[r], nsec_ref[...])).astype(BF)
    flush(new_ref)
    for r in tiles(bysrc_ref.shape[0]):
        total_ref[r] = (
            cot_ref[r].astype(F32)
            + dot_nt(bysrc_ref[r], wa_ref[...])
            + dot_nt(bydst_ref[r], wb_ref[...])
            + dot_nt(gnode_ref[r], na_ref[...])
        )


def last_kernel(live_ref, halo_ref, total_ref, low_ref, high_ref, back_ref, out_ref):
    halo_back = jnp.concatenate([low_ref[...], high_ref[...]], axis=0)
    for r in tiles(total_ref.shape[0]):
        out_ref[r] = (
            total_ref[r]
            + dot(pick_t(halo_ref[...], r.start, TILE), halo_back)
            + dot(pick_t(live_ref[...], r.start, TILE), back_ref[...])
        ).astype(BF)


def from_partner(value):
    return lax.ppermute(value, "mesh", [(0, 1), (1, 0)])


def shift(value, step):
    count = lax.axis_size("patch")
    return lax.ppermute(value, "patch", [(i, (i + step) % count) for i in range(count)])


def route(crossed):
    rows, width = crossed.shape
    patches = lax.axis_size("patch")
    crossed = crossed.reshape(patches, rows // patches, width)
    routed = lax.all_to_all(crossed, "patch", split_axis=0, concat_axis=0, tiled=True)
    return routed.reshape(rows, width)


def hop(value, dz=0, dy=0, dx=0):
    depth = lax.axis_size("patch") // PLANE
    pairs = []
    for p in range(depth * PLANE):
        z, y, x = p // PLANE, p // RING % RING, p % RING
        pairs.append((p, (z + dz) % depth * PLANE + (y + dy) % RING * RING + (x + dx) % RING))
    return lax.ppermute(value, "patch", pairs)


def join_kernel(own_ref, other_ref, *outs):
    for index, out in enumerate(outs):
        c, d = index // RING, index % RING
        out[...] = (own_ref[:, c, d].astype(F32) + other_ref[:, c, d].astype(F32)).astype(BF)


def total_of(refs):
    total = refs[0][...].astype(F32)
    for ref in refs[1:]:
        total = total + ref[...].astype(F32)
    return total


def plane_kernel(*refs):
    for c in range(2):
        total = total_of(refs[c * RING : (c + 1) * RING])
        fine = total.shape[1] // RING
        for d in range(RING):
            refs[(2 + c) * RING + d][...] = total[:, d * fine : (d + 1) * fine].astype(BF)


def depth_kernel(place_ref, *refs):
    ins, (keep_ref, send_ref, hold) = refs[: 2 * RING], refs[2 * RING :]
    depth = hold.shape[0]
    hold[...] = jnp.zeros(hold.shape, F32)
    for c in range(2):
        total = total_of(ins[c * RING : (c + 1) * RING])
        blocks, rows, lane = total.shape
        fine = rows // depth
        for block in range(blocks):
            for d in range(depth):
                hold[d, block * fine : (block + 1) * fine, c * lane : (c + 1) * lane] = total[
                    block, d * fine : (d + 1) * fine
                ]
    even = (place_ref[1] // PLANE) % 2 == 0
    for j in range(depth // 2):
        low, high = hold[2 * j], hold[2 * j + 1]
        keep_ref[j] = jnp.where(even, low, high)
        send_ref[j] = jnp.where(even, high, low).astype(BF)


def pair_kernel(place_ref, keep_ref, other_ref, *outs):
    mine = place_ref[1] // PLANE // 2
    for d, out in enumerate(outs):
        j = (mine + d) % len(outs)
        out[...] = keep_ref[j] + other_ref[j].astype(F32)


def sum_kernel(*refs):
    refs[-1][...] = total_of(refs[:-1])


def finish_kernel(place_ref, own_ref, other_ref, out_ref):
    first = place_ref[0] == 0
    lane = own_ref.shape[1]
    left = jnp.where(first, own_ref[...], other_ref[...])
    right = jnp.where(first, other_ref[...], own_ref[...])
    blocks, width = out_ref.shape
    for block in range(blocks):
        for k in range(width // (2 * lane)):
            row = block * (width // (2 * lane)) + k
            start = 2 * k * lane
            out_ref[block : block + 1, start : start + lane] = left[row : row + 1]
            out_ref[block : block + 1, start + lane : start + 2 * lane] = right[row : row + 1]


def small_call(kernel, place, args, outs, scratch=()):
    return pl.pallas_call(
        kernel,
        out_shape=tuple(outs),
        in_specs=[SMEM] + [VMEM] * len(args),
        out_specs=tuple([VMEM] * len(outs)),
        scratch_shapes=list(scratch),
        compiler_params=pltpu.CompilerParams(vmem_limit_bytes=14 * 2**20),
        cost_estimate=cost(list(args) + list(outs), 0),
    )(place, *args)


def spread(pieces, axes):
    return [
        pieces[c * RING + d] if d == 0 else hop(pieces[c * RING + d], **{axis: d})
        for c, axis in enumerate(axes)
        for d in range(RING)
    ]


def weight_sums(own, other, place, couple_back, total, rims, last):
    patches = lax.axis_size("patch")
    depth = patches // PLANE
    blocks, _, _, rows, lane = own.shape
    fine = rows // RING // depth
    pieces = call(join_kernel, (own, other), (shape(BF, blocks, rows, lane),) * (2 * RING))
    pieces = spread(pieces, ("dx", "dy"))
    pieces, couple_back, total = lax.optimization_barrier((pieces, couple_back, total))
    pieces = call(plane_kernel, pieces, (shape(BF, blocks, rows // RING, lane),) * (2 * RING))
    pieces, rims = lax.optimization_barrier((pieces, rims))
    back_low, back_high = shift(rims[1], 1), shift(rims[0], -1)
    pieces = spread(pieces, ("dy", "dx"))
    padded = (blocks * fine + 15) // 16 * 16
    half = depth // 2
    keep, send = small_call(
        depth_kernel,
        place,
        pieces,
        (shape(F32, half, padded, 2 * lane), shape(BF, half, padded, 2 * lane)),
        scratch=(pltpu.VMEM((depth, padded, 2 * lane), F32),),
    )
    pairs = [(p, (p // PLANE ^ 1) * PLANE + p % PLANE) for p in range(patches)]
    other = lax.ppermute(send, "patch", pairs)
    pieces = small_call(pair_kernel, place, (keep, other), (shape(F32, padded, 2 * lane),) * half)
    final = last(total, back_low, back_high, couple_back)
    pieces = [pieces[0]] + [hop(pieces[d], dz=2 * d) for d in range(1, half)]
    (own,) = call(sum_kernel, pieces, (shape(F32, padded, 2 * lane),))
    own, final = lax.optimization_barrier((own, final))
    (result,) = small_call(
        finish_kernel, place, (own, from_partner(own)), (shape(F32, blocks, fine * 4 * lane),)
    )
    return result, final


def shards(
    nodes,
    edges,
    cot_nodes,
    weights,
    edge_src,
    edge_dst,
    halo_rows,
    couple_rows,
    couple_count,
    couple_target,
    couple_weight,
):
    nodes_own = nodes[0]
    edges_own = edges[0]
    cotangent = cot_nodes[0]
    count, width = nodes_own.shape
    edge_count = edges_own.shape[0]
    depth = halo_rows.shape[1] // 2
    patches = lax.axis_size("patch")
    slots = couple_rows.shape[2]
    scale = 1.0 / math.sqrt(2 * patches * edge_count)
    side = jnp.stack([lax.axis_index("mesh"), lax.axis_index("patch")]).astype(I32)
    target, margin = couple_target[0], couple_weight[0]
    unit = 2 * width * width

    def weight(block):
        return Far(weights, block * width, width)

    def weight(block):
        return Far(weights, block * width, width)

    outgoing, low_out, high_out, live = stream(
        send_kernel,
        (couple_rows[0], couple_count[0], halo_rows, nodes_own),
        (shape(BF, slots, width), shape(BF, depth, width), shape(BF, depth, width), shape(I32, 1, slots)),
        flops=(slots + 2 * depth) * unit,
    )
    crossed = from_partner(outgoing)
    low, high = shift(high_out, 1), shift(low_out, -1)
    crossed, low, high = lax.optimization_barrier((crossed, low, high))
    received = route(crossed)
    slope, agg, message, half, grad_hidden = stream(
        edge_kernel,
        (
            edge_dst, nodes_own, weight(1), weight(4), cotangent, weight(6), edge_src, low, high,
            weight(0), edges_own, weight(2), weight(3),
        ),
        (shape(BF, edge_count, width), shape(BF, count, width)) + (shape(F32, count, width),) * 3,
        scratch=(pltpu.VMEM((edge_count, width), BF),),
        flops=edge_count * 6 * unit,
    )
    square = shape(BF, count, width)
    grads = shape(BF, 7, 2, RING, width // RING, width // 4)
    rim = shape(BF, depth, width)
    slot_block = shape(BF, slots, width)
    edge_block = shape(BF, edge_count, width)
    returned, grad_pooled, pooled, hidden, grad_node_pre = stream(
        node_kernel,
        (target, margin, received, message, half, weight(5), grad_hidden),
        (slot_block, square, square, square, square),
        flops=count * 8 * unit,
    )
    crossed_back = from_partner(returned)
    couple_back = route(crossed_back)
    grad_pooled, crossed_back = lax.optimization_barrier((grad_pooled, crossed_back))
    send, own, grad_edge_pre, by_source, by_target, grad_low, grad_high = stream(
        lambda *refs: grad_kernel(*refs, patches=patches, scale=scale),
        (
            side, nodes_own, grad_node_pre, grad_pooled, agg, edge_dst, weight(3), slope, edge_src, pooled,
            edges_own, hidden, cotangent, low, high, weight(0),
        ),
        (grads, grads, edge_block, square, square, rim, rim),
        scratch=[pltpu.VMEM((count, width), BF)],
        flops=edge_count * 14 * unit,
    )
    other = from_partner(send)
    edge_grads, new_nodes, total = stream(
        rest_kernel,
        (
            grad_edge_pre, weight(2), hidden, weight(6), nodes_own, by_source, weight(0), by_target,
            weight(1), grad_node_pre, weight(4), cotangent,
        ),
        (edge_block, square, shape(F32, count, width)),
        flops=edge_count * 3 * unit,
    )

    def last(sums, back_low, back_high, back):
        (final,) = stream(
            last_kernel,
            (live, halo_rows, sums, back_low, back_high, back),
            (square,),
            flops=count * 2 * unit,
        )
        return final

    summed, node_grads = weight_sums(own, other, side, couple_back, total, (grad_low, grad_high), last)
    return (new_nodes[None], node_grads[None], edge_grads[None], summed)


def solution(mesh):
    return jax.shard_map(
        shards,
        mesh=mesh,
        in_specs=(
            P("mesh", "patch", None),
            P("mesh", "patch", None),
            P("mesh", "patch", None),
            P(),
            P("mesh", "patch"),
            P("mesh", "patch"),
            P("mesh", "patch"),
            P("mesh", "patch", None),
            P("mesh", "patch", None),
            P("mesh", "patch", None),
            P("mesh", "patch", None),
        ),
        out_specs=(
            P("mesh", "patch", None),
            P("mesh", "patch", None),
            P("mesh", "patch", None),
            P(None, "patch"),
        ),
        check_vma=False,
    )
```

```python
import math

import jax
import jax.numpy as jnp
from jax import lax
from jax.experimental import pallas as pl
from jax.experimental.pallas import tpu as pltpu
from jax.sharding import PartitionSpec as P

SLOT = 8
RING = 4
PLANE = RING * RING
TILE = 256
LIMIT = 61 * 2**20 - 2**16
BF = jnp.bfloat16
F32 = jnp.float32
I32 = jnp.int32
VMEM = pl.BlockSpec(memory_space=pltpu.VMEM)
SMEM = pl.BlockSpec(memory_space=pltpu.SMEM)


def dot(a, b):
    return jnp.dot(a, b, preferred_element_type=F32)


def dot_nt(a, b):
    return lax.dot_general(a, b, (((1,), (1,)), ((), ())), preferred_element_type=F32)


def column(row):
    return jnp.transpose(jnp.broadcast_to(row.astype(F32), (128, row.shape[1])))


def pick(col, count, value=None):
    base = lax.broadcasted_iota(I32, (col.shape[0], 128), 1).astype(F32)
    one = jnp.ones_like(base) if value is None else value
    parts = [jnp.where(col == base + float(k), one, 0.0).astype(BF) for k in range(0, count, 128)]
    return parts[0] if len(parts) == 1 else jnp.concatenate(parts, axis=1)


def pick_t(row, start, size, value=None):
    base = lax.broadcasted_iota(I32, (size, row.shape[1]), 0) + start
    one = jnp.ones(base.shape, F32) if value is None else jnp.broadcast_to(value, base.shape)
    return jnp.where(base == row, one, 0.0).astype(BF)


def row_order(place, width, patches):
    fine = width // patches
    depth = patches // PLANE
    row = lax.broadcasted_iota(I32, (width, width), 0)
    col = lax.broadcasted_iota(I32, (width, width), 1)
    dx, dy = row // (width // RING), (row // (width // PLANE)) % RING
    dz, offset = (row // fine) % depth, row % fine
    x, y = place % RING, (place // RING) % RING
    patch = dz * PLANE + (y + dy) % RING * RING + (x + dx) % RING
    return jnp.where(col == patch * fine + offset, 1.0, 0.0).astype(BF)


def tiles(count):
    return [slice(i, i + TILE) for i in range(0, count, TILE)]


class Far:
    def __init__(self, array, start=0, size=None):
        self.array = array
        self.start = start
        self.size = array.shape[0] if size is None else size


class Fetched:
    def __init__(self, copies, buffer, then):
        self.copies, self.buffer, self.then = copies, buffer, then
        self.started, self.waited = False, False
        self.shape = buffer.shape

    def start(self):
        if not self.started:
            self.started = True
            for copy in self.copies:
                copy.start()

    def wait(self):
        if not self.waited:
            self.waited = True
            self.start()
            for copy in self.copies:
                copy.wait()
            for later in self.then:
                later.start()

    def __getitem__(self, index):
        self.wait()
        return self.buffer[index]


def cuts(dims):
    if len(dims) > 3:
        return [(i, 1) for i in range(dims[0])]
    step = TILE if len(dims) == 2 and dims[0] % TILE == 0 else dims[0]
    return [(i, step) for i in range(0, dims[0], step)]


class Staged:
    def __init__(self, copies, buffer):
        self.copies, self.buffer, self.sent = copies, buffer, set()
        self.shape = buffer.shape

    def __getitem__(self, index):
        return self.buffer[index]

    def __setitem__(self, index, value):
        self.buffer[index] = value

    def flush(self, index=None):
        for i in range(len(self.copies)) if index is None else [index]:
            if i not in self.sent:
                self.copies[i].start()
                self.sent.add(i)

    def wait(self):
        for copy in self.copies:
            copy.wait()


def flush(self):
        if not self.sent:
            self.copy.start()
            self.sent = True


def flush(*refs):
    for ref in refs:
        ref.flush()


def cost(arrays, flops):
    size = sum(math.prod(a.shape) * a.dtype.itemsize for a in arrays)
    return pl.CostEstimate(flops=flops, bytes_accessed=size, transcendentals=0)


def call(kernel, args, outs):
    return pl.pallas_call(
        kernel,
        out_shape=tuple(outs),
        in_specs=[VMEM] * len(args),
        out_specs=tuple([VMEM] * len(outs)),
        compiler_params=pltpu.CompilerParams(vmem_limit_bytes=14 * 2**20),
        cost_estimate=cost(list(args) + list(outs), 0),
    )(*args)


def stream(kernel, args, outs, scratch=(), flops=0, early=None, local=False):
    args = [a if isinstance(a, Far) or a.ndim == 1 else Far(a) for a in args]
    far = [i for i, a in enumerate(args) if isinstance(a, Far)]
    arrays = [a.array if isinstance(a, Far) else a for a in args]
    moved = [((args[i].size,) + args[i].array.shape[1:], args[i].array.dtype) for i in far]
    moved += [] if local else [(o.shape, o.dtype) for o in outs]
    hbm = pl.BlockSpec(memory_space=pltpu.HBM)
    ins, made = len(args), len(args) + len(outs)
    early = len(far) if early is None else early

    def body(*refs):
        buffers, sems, rest = refs[made : made + len(moved)], refs[made + len(moved)], refs[made + len(moved) + 1 :]
        used = 0

        def copies(source, target, dims, first=0):
            nonlocal used
            made_here = []
            for start, size in cuts(dims):
                x, y = source.at[pl.ds(first + start, size)], target.at[pl.ds(start, size)]
                if first == 0 and size == dims[0]:
                    x, y = source, target
                made_here.append(pltpu.make_async_copy(x, y, sems.at[used]))
                used += 1
            return made_here

        reads, later = list(refs[:ins]), []
        for k, i in enumerate(far):
            held = copies(reads[i], buffers[k], moved[k][0], args[i].start)
            reads[i] = Fetched(held, buffers[k], later if k == early - 1 else [])
            if k < early:
                reads[i].start()
            else:
                later.append(reads[i])
        writes = list(refs[ins:made])
        if not local:
            for k, out in enumerate(writes):
                buffer = buffers[len(far) + k]
                writes[k] = Staged(copies(buffer, out, out.shape), buffer)
        kernel(*reads, *writes, *rest)
        if not local:
            flush(*writes)
        for i in far:
            reads[i].wait()
        if not local:
            for write in writes:
                write.wait()

    count = sum(len(cuts(dims)) for dims, _ in moved)
    return pl.pallas_call(
        body,
        out_shape=tuple(outs),
        in_specs=[hbm if isinstance(a, Far) else SMEM for a in args],
        out_specs=tuple([VMEM if local else hbm] * len(outs)),
        scratch_shapes=[pltpu.VMEM(*m) for m in moved] + [pltpu.SemaphoreType.DMA((count,))] + list(scratch),
        compiler_params=pltpu.CompilerParams(vmem_limit_bytes=14 * 2**20 if local else LIMIT),
        cost_estimate=cost(arrays + list(outs), flops),
    )(*arrays)


def shape(dtype, *dims):
    return jax.ShapeDtypeStruct(dims, dtype)


def send_kernel(rows_ref, count_ref, halo_ref, nodes_ref, out_ref, low_ref, high_ref, live_ref):
    slots = rows_ref.shape[1]
    patches = count_ref.shape[1]
    width = nodes_ref.shape[0]
    owner = lax.broadcasted_iota(I32, (patches, slots), 0)
    place = lax.broadcasted_iota(I32, (patches, slots), 1)
    repeat = jnp.where(place // SLOT == owner, 1.0, 0.0).astype(BF)
    counts = jnp.broadcast_to(count_ref[...].astype(F32), (8, patches)).astype(BF)
    spread = dot(counts, repeat)[:1].astype(I32)
    slot = lax.broadcasted_iota(I32, (1, slots), 1) % SLOT
    live = jnp.where(slot < spread, rows_ref[...], -1)
    live_ref[...] = live
    nodes = nodes_ref[...]
    depth = low_ref.shape[0]
    halo = dot(pick(column(halo_ref[...]), width), nodes).astype(BF)
    low_ref[...] = halo[:depth]
    high_ref[...] = halo[depth:]
    flush(low_ref, high_ref, live_ref)
    col = column(live)
    for i, r in enumerate(tiles(slots)):
        out_ref[i, 0] = dot(pick(col[r], width), nodes).astype(BF)
        out_ref.flush(i)


def edge_kernel(
    dst_ref, nodes_ref, wb_ref, na_ref, cot_ref, nsec_ref, src_ref, low_ref, high_ref, wa_ref, edges_ref, wc_ref,
    second_ref, slope_ref, agg_ref, msg_ref, half_ref, ghid_ref, hid_ref,
):
    count, width = nodes_ref.shape
    inner = edges_ref.shape[0] - edges_ref.shape[0] // 4
    dst = column(dst_ref[...])
    nodes = nodes_ref[...]
    src = column(src_ref[...])
    halo = jnp.concatenate([low_ref[...], high_ref[...]], axis=0)
    for r in tiles(edges_ref.shape[0]):
        if r.stop <= inner:
            feat = dot(pick(src[r], count), nodes).astype(BF)
        else:
            feat = dot(pick(src[r] - float(count), halo.shape[0]), halo).astype(BF)
        own = dot(pick(dst[r], count), nodes).astype(BF)
        pre = dot(own, wb_ref[...]) + dot(feat, wa_ref[...]) + dot(edges_ref[r], wc_ref[...])
        sigma = jax.nn.sigmoid(pre)
        hid_ref[r] = (pre * sigma).astype(BF)
        slope_ref[r] = (sigma * (1.0 + pre * (1.0 - sigma))).astype(BF)
    flush(slope_ref)
    for r in tiles(count):
        agg = dot(pick_t(dst_ref[...], r.start, TILE), hid_ref[...]).astype(BF)
        agg_ref[r] = agg
        msg_ref[r] = dot(agg, second_ref[...])
        half_ref[r] = dot(nodes_ref[r], na_ref[...])
        ghid_ref[r] = dot_nt(cot_ref[r], nsec_ref[...])


def put(ref, index, value, first):
    half = value.shape[1] // 2
    lane = half // 2
    step = value.shape[0] // RING
    fine = step // RING
    own = jnp.where(first, value[:, :half], value[:, half:]).astype(BF)
    send = jnp.where(first, value[:, half:], value[:, :half]).astype(BF)
    for buffer, part in ((ref.own, own), (ref.send, send)):
        for i in range(RING):
            buffer[index, 0, i] = part[i * step : (i + 1) * step, :lane]
            for j in range(RING):
                start = i * step + j * fine
                buffer[index, 1, j, i * fine : (i + 1) * fine] = part[start : start + fine, lane:]
        buffer.flush(index)


class Blocks:
    def __init__(self, own, send):
        self.own, self.send = own, send


def core_kernel(
    side_ref, target_ref, margin_ref, recv_ref, msg_ref, half_ref, nb_ref, ghid_ref, dst_ref, nodes_ref, agg_ref,
    esec_ref, slope_ref, src_ref, edges_ref, cot_ref, low_ref, high_ref, wa_ref,
    ret_ref, send_ref, own_ref, gedge_ref, bysrc_ref, bydst_ref, glow_ref, ghigh_ref, hid_ref, gnode_ref,
    turned_ref, pooled_ref, gpool_ref, *, patches, scale
):
    count, width = nodes_ref.shape
    inner = edges_ref.shape[0] - edges_ref.shape[0] // 4
    depth = low_ref.shape[0]
    first = side_ref[0] == 0
    target, margin = target_ref[...], margin_ref[...]
    for r in tiles(count):
        coupled = dot(pick_t(target, r.start, TILE, margin), recv_ref[...])
        pooled = (msg_ref[r] + coupled).astype(BF)
        pooled_ref[r] = pooled
        pre = half_ref[r] + dot(pooled, nb_ref[...])
        sigma = jax.nn.sigmoid(pre)
        hid_ref[r] = (pre * sigma).astype(BF)
        gnode = (ghid_ref[r] * (sigma * (1.0 + pre * (1.0 - sigma)))).astype(BF)
        gnode_ref[r] = gnode
        gpool_ref[r] = dot_nt(gnode, nb_ref[...]).astype(BF)
    flush(hid_ref, gnode_ref)
    gpool = gpool_ref[...]
    col, weight = column(target), column(margin)
    for i, r in enumerate(tiles(recv_ref.shape[0])):
        ret_ref[i, 0] = dot(pick(col[r], count, weight[r]), gpool).astype(BF)
        ret_ref.flush(i)
    dst_row, src_row = dst_ref[...], src_ref[...]
    dst = column(dst_row)
    for r in tiles(edges_ref.shape[0]):
        message = dot(pick(dst[r], count), gpool).astype(BF)
        gedge_ref[r] = (dot_nt(message, esec_ref[...]) * slope_ref[r].astype(F32)).astype(BF)
    flush(gedge_ref)
    for r in tiles(count):
        bydst_ref[r] = dot(pick_t(dst_row, r.start, TILE), gedge_ref[...]).astype(BF)
        bysrc_ref[r] = dot(pick_t(src_row[:, :inner], r.start, TILE), gedge_ref[:inner]).astype(BF)
    flush(bysrc_ref, bydst_ref)
    halo = dot(pick_t(src_row[:, inner:], count, 2 * depth), gedge_ref[inner:]).astype(BF)
    back = dot_nt(halo, wa_ref[...]).astype(BF)
    glow_ref[...] = back[:depth]
    ghigh_ref[...] = back[depth:]
    flush(glow_ref, ghigh_ref)
    order = row_order(side_ref[1], width, patches)
    blocks = Blocks(own_ref, send_ref)
    turned_ref[...] = dot_nt(order, nodes_ref[...]).astype(BF)
    put(blocks, 1, dot(turned_ref[...], bydst_ref[...]) * scale, first)
    rim = dot_nt(order, jnp.concatenate([low_ref[...], high_ref[...]], axis=0)).astype(BF)
    put(blocks, 0, (dot(turned_ref[...], bysrc_ref[...]) + dot(rim, halo)) * scale, first)
    put(blocks, 4, dot(turned_ref[...], gnode_ref[...]) * scale, first)
    pairs = ((2, edges_ref, gedge_ref), (3, agg_ref, gpool_ref), (5, pooled_ref, gnode_ref), (6, hid_ref, cot_ref))
    for index, left, right in pairs:
        turned = dot_nt(order, left[...]).astype(BF)
        put(blocks, index, dot(turned, right[...]) * scale, first)


def rest_kernel(
    gedge_ref, wc_ref, hid_ref, nsec_ref, nodes_ref, bysrc_ref, wa_ref, bydst_ref, wb_ref, gnode_ref, na_ref,
    cot_ref, edge_ref, new_ref, total_ref,
):
    for r in tiles(gedge_ref.shape[0]):
        edge_ref[r] = dot_nt(gedge_ref[r], wc_ref[...]).astype(BF)
    flush(edge_ref)
    for r in tiles(bysrc_ref.shape[0]):
        new_ref[r] = (nodes_ref[r].astype(F32) + dot(hid_ref[r], nsec_ref[...])).astype(BF)
    flush(new_ref)
    for r in tiles(bysrc_ref.shape[0]):
        total_ref[r] = (
            cot_ref[r].astype(F32)
            + dot_nt(bysrc_ref[r], wa_ref[...])
            + dot_nt(bydst_ref[r], wb_ref[...])
            + dot_nt(gnode_ref[r], na_ref[...])
        )


def last_kernel(live_ref, halo_ref, total_ref, low_ref, high_ref, back_ref, out_ref):
    halo_back = jnp.concatenate([low_ref[...], high_ref[...]], axis=0)
    for r in tiles(total_ref.shape[0]):
        out_ref[r] = (
            total_ref[r]
            + dot(pick_t(halo_ref[...], r.start, TILE), halo_back)
            + dot(pick_t(live_ref[...], r.start, TILE), back_ref[...])
        ).astype(BF)


def from_partner(value):
    return lax.ppermute(value, "mesh", [(0, 1), (1, 0)])


def shift(value, step):
    count = lax.axis_size("patch")
    return lax.ppermute(value, "patch", [(i, (i + step) % count) for i in range(count)])


def route(crossed):
    rows, width = crossed.shape
    patches = lax.axis_size("patch")
    crossed = crossed.reshape(patches, rows // patches, width)
    routed = lax.all_to_all(crossed, "patch", split_axis=0, concat_axis=0, tiled=True)
    return routed.reshape(rows, width)


def hop(value, dz=0, dy=0, dx=0):
    depth = lax.axis_size("patch") // PLANE
    pairs = []
    for p in range(depth * PLANE):
        z, y, x = p // PLANE, p // RING % RING, p % RING
        pairs.append((p, (z + dz) % depth * PLANE + (y + dy) % RING * RING + (x + dx) % RING))
    return lax.ppermute(value, "patch", pairs)


def join_kernel(own_ref, other_ref, *outs):
    for index, out in enumerate(outs):
        c, d = index // RING, index % RING
        out[...] = (own_ref[:, c, d].astype(F32) + other_ref[:, c, d].astype(F32)).astype(BF)


def total_of(refs):
    total = refs[0][...].astype(F32)
    for ref in refs[1:]:
        total = total + ref[...].astype(F32)
    return total


def plane_kernel(*refs):
    for c in range(2):
        total = total_of(refs[c * RING : (c + 1) * RING])
        fine = total.shape[1] // RING
        for d in range(RING):
            refs[(2 + c) * RING + d][...] = total[:, d * fine : (d + 1) * fine].astype(BF)


def depth_kernel(place_ref, *refs):
    ins, (keep_ref, send_ref, hold) = refs[: 2 * RING], refs[2 * RING :]
    depth = hold.shape[0]
    hold[...] = jnp.zeros(hold.shape, F32)
    for c in range(2):
        total = total_of(ins[c * RING : (c + 1) * RING])
        blocks, rows, lane = total.shape
        fine = rows // depth
        for block in range(blocks):
            for d in range(depth):
                hold[d, block * fine : (block + 1) * fine, c * lane : (c + 1) * lane] = total[
                    block, d * fine : (d + 1) * fine
                ]
    even = (place_ref[1] // PLANE) % 2 == 0
    for j in range(depth // 2):
        low, high = hold[2 * j], hold[2 * j + 1]
        keep_ref[j] = jnp.where(even, low, high)
        send_ref[j] = jnp.where(even, high, low).astype(BF)


def pair_kernel(place_ref, keep_ref, other_ref, *outs):
    mine = place_ref[1] // PLANE // 2
    for d, out in enumerate(outs):
        j = (mine + d) % len(outs)
        out[...] = keep_ref[j] + other_ref[j].astype(F32)


def sum_kernel(*refs):
    refs[-1][...] = total_of(refs[:-1])


def finish_kernel(place_ref, own_ref, other_ref, out_ref):
    first = place_ref[0] == 0
    lane = own_ref.shape[1]
    left = jnp.where(first, own_ref[...], other_ref[...])
    right = jnp.where(first, other_ref[...], own_ref[...])
    blocks, width = out_ref.shape
    for block in range(blocks):
        for k in range(width // (2 * lane)):
            row = block * (width // (2 * lane)) + k
            start = 2 * k * lane
            out_ref[block : block + 1, start : start + lane] = left[row : row + 1]
            out_ref[block : block + 1, start + lane : start + 2 * lane] = right[row : row + 1]


def small_call(kernel, place, args, outs, scratch=()):
    return pl.pallas_call(
        kernel,
        out_shape=tuple(outs),
        in_specs=[SMEM] + [VMEM] * len(args),
        out_specs=tuple([VMEM] * len(outs)),
        scratch_shapes=list(scratch),
        compiler_params=pltpu.CompilerParams(vmem_limit_bytes=14 * 2**20),
        cost_estimate=cost(list(args) + list(outs), 0),
    )(place, *args)


def spread(pieces, axes):
    return [
        pieces[c * RING + d] if d == 0 else hop(pieces[c * RING + d], **{axis: d})
        for c, axis in enumerate(axes)
        for d in range(RING)
    ]


def weight_sums(own, other, place, couple_back, total, rims, last):
    patches = lax.axis_size("patch")
    depth = patches // PLANE
    blocks, _, _, rows, lane = own.shape
    fine = rows // RING // depth
    pieces = stream(join_kernel, (own, other), (shape(BF, blocks, rows, lane),) * (2 * RING), local=True)
    pieces = spread(pieces, ("dx", "dy"))
    pieces[1], rims = lax.optimization_barrier((pieces[1], rims))
    back_low, back_high = shift(rims[1], 1), shift(rims[0], -1)
    pieces, couple_back, total, back_low, back_high = lax.optimization_barrier(
        (pieces, couple_back, total, back_low, back_high)
    )
    pieces = call(plane_kernel, pieces, (shape(BF, blocks, rows // RING, lane),) * (2 * RING))
    pieces = spread(pieces, ("dy", "dx"))
    padded = (blocks * fine + 15) // 16 * 16
    half = depth // 2
    keep, send = small_call(
        depth_kernel,
        place,
        pieces,
        (shape(F32, half, padded, 2 * lane), shape(BF, half, padded, 2 * lane)),
        scratch=(pltpu.VMEM((depth, padded, 2 * lane), F32),),
    )
    pairs = [(p, (p // PLANE ^ 1) * PLANE + p % PLANE) for p in range(patches)]
    other = lax.ppermute(send, "patch", pairs)
    pieces = small_call(pair_kernel, place, (keep, other), (shape(F32, padded, 2 * lane),) * half)
    final = last(total, back_low, back_high, couple_back)
    pieces = [pieces[0]] + [hop(pieces[d], dz=2 * d) for d in range(1, half)]
    (own,) = call(sum_kernel, pieces, (shape(F32, padded, 2 * lane),))
    own, final = lax.optimization_barrier((own, final))
    (result,) = small_call(
        finish_kernel, place, (own, from_partner(own)), (shape(F32, blocks, fine * 4 * lane),)
    )
    return result, final


def shards(
    nodes,
    edges,
    cot_nodes,
    weights,
    edge_src,
    edge_dst,
    halo_rows,
    couple_rows,
    couple_count,
    couple_target,
    couple_weight,
):
    nodes_own = nodes[0]
    edges_own = edges[0]
    cotangent = cot_nodes[0]
    count, width = nodes_own.shape
    edge_count = edges_own.shape[0]
    depth = halo_rows.shape[1] // 2
    patches = lax.axis_size("patch")
    slots = couple_rows.shape[2]
    scale = 1.0 / math.sqrt(2 * patches * edge_count)
    side = jnp.stack([lax.axis_index("mesh"), lax.axis_index("patch")]).astype(I32)
    target, margin = couple_target[0], couple_weight[0]
    unit = 2 * width * width

    def weight(block):
        return Far(weights, block * width, width)

    def weight(block):
        return Far(weights, block * width, width)

    slot_block = shape(BF, slots // TILE, 1, TILE, width)
    outgoing, low_out, high_out, live = stream(
        send_kernel,
        (couple_rows[0], couple_count[0], halo_rows, nodes_own),
        (slot_block, shape(BF, depth, width), shape(BF, depth, width), shape(I32, 1, slots)),
        flops=(slots + 2 * depth) * unit,
    )
    crossed = from_partner(outgoing.reshape(slots, width))
    low, high = shift(high_out, 1), shift(low_out, -1)
    crossed, low, high = lax.optimization_barrier((crossed, low, high))
    received = route(crossed)
    slope, agg, message, half, grad_hidden = stream(
        edge_kernel,
        (
            edge_dst, nodes_own, weight(1), weight(4), cotangent, weight(6), edge_src, low, high,
            weight(0), edges_own, weight(2), weight(3),
        ),
        (shape(BF, edge_count, width), shape(BF, count, width)) + (shape(F32, count, width),) * 3,
        scratch=(pltpu.VMEM((edge_count, width), BF),),
        flops=edge_count * 6 * unit,
    )
    square = shape(BF, count, width)
    grads = shape(BF, 7, 2, RING, width // RING, width // 4)
    rim = shape(BF, depth, width)
    edge_block = shape(BF, edge_count, width)
    (
        returned, send, own, grad_edge_pre, by_source, by_target, grad_low, grad_high, hidden, grad_node_pre
    ) = stream(
        lambda *refs: core_kernel(*refs, patches=patches, scale=scale),
        (
            side, target, margin, received, message, half, weight(5), grad_hidden, edge_dst, nodes_own, agg,
            weight(3), slope, edge_src, edges_own, cotangent, low, high, weight(0),
        ),
        (slot_block, grads, grads, edge_block, square, square, rim, rim, square, square),
        scratch=[pltpu.VMEM((count, width), BF)] * 3,
        flops=edge_count * 18 * unit,
        early=7,
    )
    crossed_back = from_partner(returned.reshape(slots, width))
    couple_back = route(crossed_back)
    other = from_partner(send)
    edge_grads, new_nodes, total = stream(
        rest_kernel,
        (
            grad_edge_pre, weight(2), hidden, weight(6), nodes_own, by_source, weight(0), by_target,
            weight(1), grad_node_pre, weight(4), cotangent,
        ),
        (edge_block, square, shape(F32, count, width)),
        flops=edge_count * 3 * unit,
    )

    def last(sums, back_low, back_high, back):
        (final,) = stream(
            last_kernel,
            (live, halo_rows, sums, back_low, back_high, back),
            (square,),
            flops=count * 2 * unit,
        )
        return final

    summed, node_grads = weight_sums(own, other, side, couple_back, total, (grad_low, grad_high), last)
    return (new_nodes[None], node_grads[None], edge_grads[None], summed)


def solution(mesh):
    return jax.shard_map(
        shards,
        mesh=mesh,
        in_specs=(
            P("mesh", "patch", None),
            P("mesh", "patch", None),
            P("mesh", "patch", None),
            P(),
            P("mesh", "patch"),
            P("mesh", "patch"),
            P("mesh", "patch"),
            P("mesh", "patch", None),
            P("mesh", "patch", None),
            P("mesh", "patch", None),
            P("mesh", "patch", None),
        ),
        out_specs=(
            P("mesh", "patch", None),
            P("mesh", "patch", None),
            P("mesh", "patch", None),
            P(None, "patch"),
        ),
        check_vma=False,
    )
```

```python
import math

import jax
import jax.numpy as jnp
from jax import lax
from jax.experimental import pallas as pl
from jax.experimental.pallas import tpu as pltpu
from jax.sharding import PartitionSpec as P

SLOT = 8
RING = 4
PLANE = RING * RING
TILE = 256
LIMIT = 61 * 2**20 - 2**16
BF = jnp.bfloat16
F32 = jnp.float32
I32 = jnp.int32
VMEM = pl.BlockSpec(memory_space=pltpu.VMEM)
SMEM = pl.BlockSpec(memory_space=pltpu.SMEM)


def dot(a, b):
    return jnp.dot(a, b, preferred_element_type=F32)


def dot_nt(a, b):
    return lax.dot_general(a, b, (((1,), (1,)), ((), ())), preferred_element_type=F32)


def column(row):
    return jnp.transpose(jnp.broadcast_to(row.astype(F32), (128, row.shape[1])))


def pick(col, count, value=None):
    base = lax.broadcasted_iota(I32, (col.shape[0], 128), 1).astype(F32)
    one = jnp.ones_like(base) if value is None else value
    parts = [jnp.where(col == base + float(k), one, 0.0).astype(BF) for k in range(0, count, 128)]
    return parts[0] if len(parts) == 1 else jnp.concatenate(parts, axis=1)


def pick_t(row, start, size, value=None):
    base = lax.broadcasted_iota(I32, (size, row.shape[1]), 0) + start
    one = jnp.ones(base.shape, F32) if value is None else jnp.broadcast_to(value, base.shape)
    return jnp.where(base == row, one, 0.0).astype(BF)


def row_order(place, width, patches):
    fine = width // patches
    depth = patches // PLANE
    row = lax.broadcasted_iota(I32, (width, width), 0)
    col = lax.broadcasted_iota(I32, (width, width), 1)
    dx, dy = row // (width // RING), (row // (width // PLANE)) % RING
    dz, offset = (row // fine) % depth, row % fine
    x, y = place % RING, (place // RING) % RING
    patch = dz * PLANE + (y + dy) % RING * RING + (x + dx) % RING
    return jnp.where(col == patch * fine + offset, 1.0, 0.0).astype(BF)


def tiles(count):
    return [slice(i, i + TILE) for i in range(0, count, TILE)]


class Far:
    def __init__(self, array, start=0, size=None):
        self.array = array
        self.start = start
        self.size = array.shape[0] if size is None else size


class Fetched:
    def __init__(self, copies, buffer, then):
        self.copies, self.buffer, self.then = copies, buffer, then
        self.started, self.waited = False, False
        self.shape = buffer.shape

    def start(self):
        if not self.started:
            self.started = True
            for copy in self.copies:
                copy.start()

    def wait(self):
        if not self.waited:
            self.waited = True
            self.start()
            for copy in self.copies:
                copy.wait()
            for later in self.then:
                later.start()

    def __getitem__(self, index):
        self.wait()
        return self.buffer[index]


def cuts(dims):
    if len(dims) > 3:
        return [(i, 1) for i in range(dims[0])]
    step = TILE if len(dims) == 2 and dims[0] % TILE == 0 else dims[0]
    return [(i, step) for i in range(0, dims[0], step)]


class Staged:
    def __init__(self, copies, buffer):
        self.copies, self.buffer, self.sent = copies, buffer, set()
        self.shape = buffer.shape

    def __getitem__(self, index):
        return self.buffer[index]

    def __setitem__(self, index, value):
        self.buffer[index] = value

    def flush(self, index=None):
        for i in range(len(self.copies)) if index is None else [index]:
            if i not in self.sent:
                self.copies[i].start()
                self.sent.add(i)

    def wait(self):
        for copy in self.copies:
            copy.wait()


def flush(self):
        if not self.sent:
            self.copy.start()
            self.sent = True


def flush(*refs):
    for ref in refs:
        ref.flush()


def cost(arrays, flops):
    size = sum(math.prod(a.shape) * a.dtype.itemsize for a in arrays) if flops else 0
    return pl.CostEstimate(flops=flops, bytes_accessed=size, transcendentals=0)


def call(kernel, args, outs):
    return pl.pallas_call(
        kernel,
        out_shape=tuple(outs),
        in_specs=[VMEM] * len(args),
        out_specs=tuple([VMEM] * len(outs)),
        compiler_params=pltpu.CompilerParams(vmem_limit_bytes=14 * 2**20),
        cost_estimate=cost(list(args) + list(outs), 0),
    )(*args)


def stream(kernel, args, outs, scratch=(), flops=0, early=None, local=False):
    args = [a if isinstance(a, Far) or a.ndim == 1 else Far(a) for a in args]
    far = [i for i, a in enumerate(args) if isinstance(a, Far)]
    arrays = [a.array if isinstance(a, Far) else a for a in args]
    moved = [((args[i].size,) + args[i].array.shape[1:], args[i].array.dtype) for i in far]
    moved += [] if local else [(o.shape, o.dtype) for o in outs]
    hbm = pl.BlockSpec(memory_space=pltpu.HBM)
    ins, made = len(args), len(args) + len(outs)
    early = len(far) if early is None else early

    def body(*refs):
        buffers, sems, rest = refs[made : made + len(moved)], refs[made + len(moved)], refs[made + len(moved) + 1 :]
        used = 0

        def copies(source, target, dims, first=0):
            nonlocal used
            made_here = []
            for start, size in cuts(dims):
                x, y = source.at[pl.ds(first + start, size)], target.at[pl.ds(start, size)]
                if first == 0 and size == dims[0]:
                    x, y = source, target
                made_here.append(pltpu.make_async_copy(x, y, sems.at[used]))
                used += 1
            return made_here

        reads, later = list(refs[:ins]), []
        for k, i in enumerate(far):
            held = copies(reads[i], buffers[k], moved[k][0], args[i].start)
            reads[i] = Fetched(held, buffers[k], later if k == early - 1 else [])
            if k < early:
                reads[i].start()
            else:
                later.append(reads[i])
        writes = list(refs[ins:made])
        if not local:
            for k, out in enumerate(writes):
                buffer = buffers[len(far) + k]
                writes[k] = Staged(copies(buffer, out, out.shape), buffer)
        kernel(*reads, *writes, *rest)
        if not local:
            flush(*writes)
        for i in far:
            reads[i].wait()
        if not local:
            for write in writes:
                write.wait()

    count = sum(len(cuts(dims)) for dims, _ in moved)
    return pl.pallas_call(
        body,
        out_shape=tuple(outs),
        in_specs=[hbm if isinstance(a, Far) else SMEM for a in args],
        out_specs=tuple([VMEM if local else hbm] * len(outs)),
        scratch_shapes=[pltpu.VMEM(*m) for m in moved] + [pltpu.SemaphoreType.DMA((count,))] + list(scratch),
        compiler_params=pltpu.CompilerParams(vmem_limit_bytes=14 * 2**20 if local else LIMIT),
        cost_estimate=cost(arrays + list(outs), flops),
    )(*arrays)


def shape(dtype, *dims):
    return jax.ShapeDtypeStruct(dims, dtype)


def send_kernel(rows_ref, count_ref, halo_ref, nodes_ref, out_ref, low_ref, high_ref, live_ref):
    slots = rows_ref.shape[1]
    patches = count_ref.shape[1]
    width = nodes_ref.shape[0]
    owner = lax.broadcasted_iota(I32, (patches, slots), 0)
    place = lax.broadcasted_iota(I32, (patches, slots), 1)
    repeat = jnp.where(place // SLOT == owner, 1.0, 0.0).astype(BF)
    counts = jnp.broadcast_to(count_ref[...].astype(F32), (8, patches)).astype(BF)
    spread = dot(counts, repeat)[:1].astype(I32)
    slot = lax.broadcasted_iota(I32, (1, slots), 1) % SLOT
    live = jnp.where(slot < spread, rows_ref[...], -1)
    live_ref[...] = live
    nodes = nodes_ref[...]
    depth = low_ref.shape[0]
    halo = dot(pick(column(halo_ref[...]), width), nodes).astype(BF)
    low_ref[...] = halo[:depth]
    high_ref[...] = halo[depth:]
    flush(low_ref, high_ref, live_ref)
    col = column(live)
    for i, r in enumerate(tiles(slots)):
        out_ref[i, 0] = dot(pick(col[r], width), nodes).astype(BF)
        out_ref.flush(i)


def edge_kernel(
    dst_ref, nodes_ref, wb_ref, na_ref, cot_ref, nsec_ref, src_ref, low_ref, high_ref, wa_ref, edges_ref, wc_ref,
    second_ref, slope_ref, agg_ref, msg_ref, half_ref, ghid_ref, hid_ref,
):
    count, width = nodes_ref.shape
    inner = edges_ref.shape[0] - edges_ref.shape[0] // 4
    dst = column(dst_ref[...])
    nodes = nodes_ref[...]
    src = column(src_ref[...])
    halo = jnp.concatenate([low_ref[...], high_ref[...]], axis=0)
    for r in tiles(edges_ref.shape[0]):
        if r.stop <= inner:
            feat = dot(pick(src[r], count), nodes).astype(BF)
        else:
            feat = dot(pick(src[r] - float(count), halo.shape[0]), halo).astype(BF)
        own = dot(pick(dst[r], count), nodes).astype(BF)
        pre = dot(own, wb_ref[...]) + dot(feat, wa_ref[...]) + dot(edges_ref[r], wc_ref[...])
        sigma = jax.nn.sigmoid(pre)
        hid_ref[r] = (pre * sigma).astype(BF)
        slope_ref[r] = (sigma * (1.0 + pre * (1.0 - sigma))).astype(BF)
    flush(slope_ref)
    for r in tiles(count):
        agg = dot(pick_t(dst_ref[...], r.start, TILE), hid_ref[...]).astype(BF)
        agg_ref[r] = agg
        msg_ref[r] = dot(agg, second_ref[...])
        half_ref[r] = dot(nodes_ref[r], na_ref[...])
        ghid_ref[r] = dot_nt(cot_ref[r], nsec_ref[...])


def put(ref, index, value, first):
    half = value.shape[1] // 2
    lane = half // 2
    step = value.shape[0] // RING
    fine = step // RING
    own = jnp.where(first, value[:, :half], value[:, half:]).astype(BF)
    send = jnp.where(first, value[:, half:], value[:, :half]).astype(BF)
    for buffer, part in ((ref.own, own), (ref.send, send)):
        for i in range(RING):
            buffer[index, 0, i] = part[i * step : (i + 1) * step, :lane]
            for j in range(RING):
                start = i * step + j * fine
                buffer[index, 1, j, i * fine : (i + 1) * fine] = part[start : start + fine, lane:]
        buffer.flush(index)


class Blocks:
    def __init__(self, own, send):
        self.own, self.send = own, send


def node_kernel(
    target_ref, margin_ref, recv_ref, msg_ref, half_ref, nb_ref, ghid_ref,
    ret_ref, gpool_ref, pooled_ref, hid_ref, gnode_ref,
):
    count = msg_ref.shape[0]
    target, margin = target_ref[...], margin_ref[...]
    for r in tiles(count):
        coupled = dot(pick_t(target, r.start, TILE, margin), recv_ref[...])
        pooled = (msg_ref[r] + coupled).astype(BF)
        pooled_ref[r] = pooled
        pre = half_ref[r] + dot(pooled, nb_ref[...])
        sigma = jax.nn.sigmoid(pre)
        hid_ref[r] = (pre * sigma).astype(BF)
        gnode = (ghid_ref[r] * (sigma * (1.0 + pre * (1.0 - sigma)))).astype(BF)
        gnode_ref[r] = gnode
        gpool_ref[r] = dot_nt(gnode, nb_ref[...]).astype(BF)
    flush(gpool_ref, gnode_ref, pooled_ref, hid_ref)
    gpool = gpool_ref[...]
    col, weight = column(target), column(margin)
    for i, r in enumerate(tiles(recv_ref.shape[0])):
        ret_ref[i, 0] = dot(pick(col[r], count, weight[r]), gpool).astype(BF)
        ret_ref.flush(i)


def grad_kernel(
    side_ref, nodes_ref, gnode_ref, gpool_ref, agg_ref, dst_ref, esec_ref, slope_ref, src_ref, pooled_ref,
    edges_ref, hid_ref, cot_ref, low_ref, high_ref, wa_ref,
    send_ref, own_ref, gedge_ref, bysrc_ref, bydst_ref, glow_ref, ghigh_ref, turned_ref,
    *, patches, scale
):
    count, width = nodes_ref.shape
    inner = edges_ref.shape[0] - edges_ref.shape[0] // 4
    depth = low_ref.shape[0]
    first = side_ref[0] == 0
    order = row_order(side_ref[1], width, patches)
    blocks = Blocks(own_ref, send_ref)
    turned_ref[...] = dot_nt(order, nodes_ref[...]).astype(BF)
    put(blocks, 4, dot(turned_ref[...], gnode_ref[...]) * scale, first)
    put(blocks, 3, dot(dot_nt(order, agg_ref[...]).astype(BF), gpool_ref[...]) * scale, first)
    gpool = gpool_ref[...]
    dst_row, src_row = dst_ref[...], src_ref[...]
    dst = column(dst_row)
    for r in tiles(edges_ref.shape[0]):
        message = dot(pick(dst[r], count), gpool).astype(BF)
        gedge_ref[r] = (dot_nt(message, esec_ref[...]) * slope_ref[r].astype(F32)).astype(BF)
    flush(gedge_ref)
    for r in tiles(count):
        bydst_ref[r] = dot(pick_t(dst_row, r.start, TILE), gedge_ref[...]).astype(BF)
        bysrc_ref[r] = dot(pick_t(src_row[:, :inner], r.start, TILE), gedge_ref[:inner]).astype(BF)
    flush(bysrc_ref, bydst_ref)
    put(blocks, 1, dot(turned_ref[...], bydst_ref[...]) * scale, first)
    halo = dot(pick_t(src_row[:, inner:], count, 2 * depth), gedge_ref[inner:]).astype(BF)
    rim = dot_nt(order, jnp.concatenate([low_ref[...], high_ref[...]], axis=0)).astype(BF)
    put(blocks, 0, (dot(turned_ref[...], bysrc_ref[...]) + dot(rim, halo)) * scale, first)
    back = dot_nt(halo, wa_ref[...]).astype(BF)
    glow_ref[...] = back[:depth]
    ghigh_ref[...] = back[depth:]
    flush(glow_ref, ghigh_ref)
    pairs = ((2, edges_ref, gedge_ref), (5, pooled_ref, gnode_ref), (6, hid_ref, cot_ref))
    for index, left, right in pairs:
        turned = dot_nt(order, left[...]).astype(BF)
        put(blocks, index, dot(turned, right[...]) * scale, first)


def rest_kernel(
    gedge_ref, wc_ref, hid_ref, nsec_ref, nodes_ref, bysrc_ref, wa_ref, bydst_ref, wb_ref, gnode_ref, na_ref,
    cot_ref, edge_ref, new_ref, total_ref,
):
    for r in tiles(gedge_ref.shape[0]):
        edge_ref[r] = dot_nt(gedge_ref[r], wc_ref[...]).astype(BF)
    flush(edge_ref)
    for r in tiles(bysrc_ref.shape[0]):
        new_ref[r] = (nodes_ref[r].astype(F32) + dot(hid_ref[r], nsec_ref[...])).astype(BF)
    flush(new_ref)
    for r in tiles(bysrc_ref.shape[0]):
        total_ref[r] = (
            cot_ref[r].astype(F32)
            + dot_nt(bysrc_ref[r], wa_ref[...])
            + dot_nt(bydst_ref[r], wb_ref[...])
            + dot_nt(gnode_ref[r], na_ref[...])
        )


def last_kernel(live_ref, halo_ref, total_ref, low_ref, high_ref, back_ref, out_ref):
    halo_back = jnp.concatenate([low_ref[...], high_ref[...]], axis=0)
    for r in tiles(total_ref.shape[0]):
        out_ref[r] = (
            total_ref[r]
            + dot(pick_t(halo_ref[...], r.start, TILE), halo_back)
            + dot(pick_t(live_ref[...], r.start, TILE), back_ref[...])
        ).astype(BF)


def from_partner(value):
    return lax.ppermute(value, "mesh", [(0, 1), (1, 0)])


def shift(value, step):
    count = lax.axis_size("patch")
    return lax.ppermute(value, "patch", [(i, (i + step) % count) for i in range(count)])


def route(crossed):
    rows, width = crossed.shape
    patches = lax.axis_size("patch")
    crossed = crossed.reshape(patches, rows // patches, width)
    routed = lax.all_to_all(crossed, "patch", split_axis=0, concat_axis=0, tiled=True)
    return routed.reshape(rows, width)


def hop(value, dz=0, dy=0, dx=0):
    depth = lax.axis_size("patch") // PLANE
    pairs = []
    for p in range(depth * PLANE):
        z, y, x = p // PLANE, p // RING % RING, p % RING
        pairs.append((p, (z + dz) % depth * PLANE + (y + dy) % RING * RING + (x + dx) % RING))
    return lax.ppermute(value, "patch", pairs)


def join_kernel(own_ref, other_ref, *outs):
    for index, out in enumerate(outs):
        c, d = index // RING, index % RING
        out[...] = (own_ref[:, c, d].astype(F32) + other_ref[:, c, d].astype(F32)).astype(BF)


def total_of(refs):
    total = refs[0][...].astype(F32)
    for ref in refs[1:]:
        total = total + ref[...].astype(F32)
    return total


def plane_kernel(*refs):
    for c in range(2):
        total = total_of(refs[c * RING : (c + 1) * RING])
        fine = total.shape[1] // RING
        for d in range(RING):
            refs[(2 + c) * RING + d][...] = total[:, d * fine : (d + 1) * fine].astype(BF)


def depth_kernel(place_ref, *refs):
    ins, (keep_ref, send_ref, hold) = refs[: 2 * RING], refs[2 * RING :]
    depth = hold.shape[0]
    hold[...] = jnp.zeros(hold.shape, F32)
    for c in range(2):
        total = total_of(ins[c * RING : (c + 1) * RING])
        blocks, rows, lane = total.shape
        fine = rows // depth
        for block in range(blocks):
            for d in range(depth):
                hold[d, block * fine : (block + 1) * fine, c * lane : (c + 1) * lane] = total[
                    block, d * fine : (d + 1) * fine
                ]
    even = (place_ref[1] // PLANE) % 2 == 0
    for j in range(depth // 2):
        low, high = hold[2 * j], hold[2 * j + 1]
        keep_ref[j] = jnp.where(even, low, high)
        send_ref[j] = jnp.where(even, high, low).astype(BF)


def pair_kernel(place_ref, keep_ref, other_ref, *outs):
    mine = place_ref[1] // PLANE // 2
    for d, out in enumerate(outs):
        j = (mine + d) % len(outs)
        out[...] = keep_ref[j] + other_ref[j].astype(F32)


def sum_kernel(*refs):
    refs[-1][...] = total_of(refs[:-1])


def finish_kernel(place_ref, own_ref, other_ref, out_ref):
    first = place_ref[0] == 0
    lane = own_ref.shape[1]
    left = jnp.where(first, own_ref[...], other_ref[...])
    right = jnp.where(first, other_ref[...], own_ref[...])
    blocks, width = out_ref.shape
    for block in range(blocks):
        for k in range(width // (2 * lane)):
            row = block * (width // (2 * lane)) + k
            start = 2 * k * lane
            out_ref[block : block + 1, start : start + lane] = left[row : row + 1]
            out_ref[block : block + 1, start + lane : start + 2 * lane] = right[row : row + 1]


def small_call(kernel, place, args, outs, scratch=()):
    return pl.pallas_call(
        kernel,
        out_shape=tuple(outs),
        in_specs=[SMEM] + [VMEM] * len(args),
        out_specs=tuple([VMEM] * len(outs)),
        scratch_shapes=list(scratch),
        compiler_params=pltpu.CompilerParams(vmem_limit_bytes=14 * 2**20),
        cost_estimate=cost(list(args) + list(outs), 0),
    )(place, *args)


def spread(pieces, axes):
    return [
        pieces[c * RING + d] if d == 0 else hop(pieces[c * RING + d], **{axis: d})
        for c, axis in enumerate(axes)
        for d in range(RING)
    ]


def weight_sums(own, other, place, couple_back, total, rims, last):
    patches = lax.axis_size("patch")
    depth = patches // PLANE
    blocks, _, _, rows, lane = own.shape
    fine = rows // RING // depth
    other, total = lax.optimization_barrier((other, total))
    pieces = stream(join_kernel, (own, other), (shape(BF, blocks, rows, lane),) * (2 * RING), local=True)
    pieces = spread(pieces, ("dx", "dy"))
    pieces[1], rims = lax.optimization_barrier((pieces[1], rims))
    back_low, back_high = shift(rims[1], 1), shift(rims[0], -1)
    pieces, couple_back, total, back_low, back_high = lax.optimization_barrier(
        (pieces, couple_back, total, back_low, back_high)
    )
    pieces = call(plane_kernel, pieces, (shape(BF, blocks, rows // RING, lane),) * (2 * RING))
    pieces = spread(pieces, ("dy", "dx"))
    padded = (blocks * fine + 15) // 16 * 16
    half = depth // 2
    keep, send = small_call(
        depth_kernel,
        place,
        pieces,
        (shape(F32, half, padded, 2 * lane), shape(BF, half, padded, 2 * lane)),
        scratch=(pltpu.VMEM((depth, padded, 2 * lane), F32),),
    )
    pairs = [(p, (p // PLANE ^ 1) * PLANE + p % PLANE) for p in range(patches)]
    other = lax.ppermute(send, "patch", pairs)
    pieces = small_call(pair_kernel, place, (keep, other), (shape(F32, padded, 2 * lane),) * half)
    final = last(total, back_low, back_high, couple_back)
    pieces = [pieces[0]] + [hop(pieces[d], dz=2 * d) for d in range(1, half)]
    (own,) = call(sum_kernel, pieces, (shape(F32, padded, 2 * lane),))
    own, final = lax.optimization_barrier((own, final))
    (result,) = small_call(
        finish_kernel, place, (own, from_partner(own)), (shape(F32, blocks, fine * 4 * lane),)
    )
    return result, final


def shards(
    nodes,
    edges,
    cot_nodes,
    weights,
    edge_src,
    edge_dst,
    halo_rows,
    couple_rows,
    couple_count,
    couple_target,
    couple_weight,
):
    nodes_own = nodes[0]
    edges_own = edges[0]
    cotangent = cot_nodes[0]
    count, width = nodes_own.shape
    edge_count = edges_own.shape[0]
    depth = halo_rows.shape[1] // 2
    patches = lax.axis_size("patch")
    slots = couple_rows.shape[2]
    scale = 1.0 / math.sqrt(2 * patches * edge_count)
    side = jnp.stack([lax.axis_index("mesh"), lax.axis_index("patch")]).astype(I32)
    target, margin = couple_target[0], couple_weight[0]
    unit = 2 * width * width

    def weight(block):
        return Far(weights, block * width, width)

    def weight(block):
        return Far(weights, block * width, width)

    slot_block = shape(BF, slots // TILE, 1, TILE, width)
    outgoing, low_out, high_out, live = stream(
        send_kernel,
        (couple_rows[0], couple_count[0], halo_rows, nodes_own),
        (slot_block, shape(BF, depth, width), shape(BF, depth, width), shape(I32, 1, slots)),
        flops=(slots + 2 * depth) * unit,
    )
    crossed = from_partner(outgoing.reshape(slots, width))
    low, high = shift(high_out, 1), shift(low_out, -1)
    crossed, low, high = lax.optimization_barrier((crossed, low, high))
    received = route(crossed)
    slope, agg, message, half, grad_hidden = stream(
        edge_kernel,
        (
            edge_dst, nodes_own, weight(1), weight(4), cotangent, weight(6), edge_src, low, high,
            weight(0), edges_own, weight(2), weight(3),
        ),
        (shape(BF, edge_count, width), shape(BF, count, width)) + (shape(F32, count, width),) * 3,
        scratch=(pltpu.VMEM((edge_count, width), BF),),
        flops=edge_count * 6 * unit,
    )
    square = shape(BF, count, width)
    grads = shape(BF, 7, 2, RING, width // RING, width // 4)
    rim = shape(BF, depth, width)
    edge_block = shape(BF, edge_count, width)
    returned, grad_pooled, pooled, hidden, grad_node_pre = stream(
        node_kernel,
        (target, margin, received, message, half, weight(5), grad_hidden),
        (slot_block, square, square, square, square),
        flops=count * 8 * unit,
    )
    crossed_back = from_partner(returned.reshape(slots, width))
    couple_back = route(crossed_back)
    grad_pooled, crossed_back = lax.optimization_barrier((grad_pooled, crossed_back))
    send, own, grad_edge_pre, by_source, by_target, grad_low, grad_high = stream(
        lambda *refs: grad_kernel(*refs, patches=patches, scale=scale),
        (
            side, nodes_own, grad_node_pre, grad_pooled, agg, edge_dst, weight(3), slope, edge_src, pooled,
            edges_own, hidden, cotangent, low, high, weight(0),
        ),
        (grads, grads, edge_block, square, square, rim, rim),
        scratch=[pltpu.VMEM((count, width), BF)],
        early=4,
    )
    other = from_partner(send)
    edge_grads, new_nodes, total = stream(
        rest_kernel,
        (
            grad_edge_pre, weight(2), hidden, weight(6), nodes_own, by_source, weight(0), by_target,
            weight(1), grad_node_pre, weight(4), cotangent,
        ),
        (edge_block, square, shape(F32, count, width)),
        flops=edge_count * 300 * unit,
    )

    def last(sums, back_low, back_high, back):
        (final,) = stream(
            last_kernel,
            (live, halo_rows, sums, back_low, back_high, back),
            (square,),
            flops=count * 2 * unit,
        )
        return final

    summed, node_grads = weight_sums(own, other, side, couple_back, total, (grad_low, grad_high), last)
    return (new_nodes[None], node_grads[None], edge_grads[None], summed)


def solution(mesh):
    return jax.shard_map(
        shards,
        mesh=mesh,
        in_specs=(
            P("mesh", "patch", None),
            P("mesh", "patch", None),
            P("mesh", "patch", None),
            P(),
            P("mesh", "patch"),
            P("mesh", "patch"),
            P("mesh", "patch"),
            P("mesh", "patch", None),
            P("mesh", "patch", None),
            P("mesh", "patch", None),
            P("mesh", "patch", None),
        ),
        out_specs=(
            P("mesh", "patch", None),
            P("mesh", "patch", None),
            P("mesh", "patch", None),
            P(None, "patch"),
        ),
        check_vma=False,
    )
```

```python
import math

import jax
import jax.numpy as jnp
from jax import lax
from jax.experimental import pallas as pl
from jax.experimental.pallas import tpu as pltpu
from jax.sharding import PartitionSpec as P

SLOT = 8
PLANE = 16
TILE = 256
LIMIT = 61 * 2**20 - 2**16
BF = jnp.bfloat16
F32 = jnp.float32
I32 = jnp.int32
VMEM = pl.BlockSpec(memory_space=pltpu.VMEM)
SMEM = pl.BlockSpec(memory_space=pltpu.SMEM)


def dot(a, b):
    return jnp.dot(a, b, preferred_element_type=F32)


def dot_nt(a, b):
    return lax.dot_general(a, b, (((1,), (1,)), ((), ())), preferred_element_type=F32)


def column(row):
    return jnp.transpose(jnp.broadcast_to(row.astype(F32), (128, row.shape[1])))


def pick(col, count, value=None):
    base = lax.broadcasted_iota(I32, (col.shape[0], 128), 1).astype(F32)
    one = jnp.ones_like(base) if value is None else value
    parts = [jnp.where(col == base + float(k), one, 0.0).astype(BF) for k in range(0, count, 128)]
    return parts[0] if len(parts) == 1 else jnp.concatenate(parts, axis=1)


def pick_t(row, start, size, value=None):
    base = lax.broadcasted_iota(I32, (size, row.shape[1]), 0) + start
    one = jnp.ones(base.shape, F32) if value is None else jnp.broadcast_to(value, base.shape)
    return jnp.where(base == row, one, 0.0).astype(BF)


def row_order(width, patches):
    fine = width // patches
    depth = patches // PLANE
    row = lax.broadcasted_iota(I32, (width, width), 0)
    col = lax.broadcasted_iota(I32, (width, width), 1)
    plane, z, offset = row // (depth * fine), (row // fine) % depth, row % fine
    return jnp.where(col == (z * PLANE + plane) * fine + offset, 1.0, 0.0).astype(BF)


def tiles(count):
    return [slice(i, i + TILE) for i in range(0, count, TILE)]


class Far:
    def __init__(self, array, start=0, size=None):
        self.array = array
        self.start = start
        self.size = array.shape[0] if size is None else size


class Fetched:
    def __init__(self, copies, buffer, then):
        self.copies, self.buffer, self.then = copies, buffer, then
        self.started, self.waited = False, False
        self.shape = buffer.shape

    def start(self):
        if not self.started:
            self.started = True
            for copy in self.copies:
                copy.start()

    def wait(self):
        if not self.waited:
            self.waited = True
            self.start()
            for copy in self.copies:
                copy.wait()
            for later in self.then:
                later.start()

    def __getitem__(self, index):
        self.wait()
        return self.buffer[index]


def cuts(dims):
    if len(dims) > 3:
        return [(i, 1) for i in range(dims[0])]
    step = TILE if len(dims) == 2 and dims[0] % TILE == 0 else dims[0]
    return [(i, step) for i in range(0, dims[0], step)]


class Staged:
    def __init__(self, copies, buffer):
        self.copies, self.buffer, self.sent = copies, buffer, set()
        self.shape = buffer.shape

    def __getitem__(self, index):
        return self.buffer[index]

    def __setitem__(self, index, value):
        self.buffer[index] = value

    def flush(self, index=None):
        for i in range(len(self.copies)) if index is None else [index]:
            if i not in self.sent:
                self.copies[i].start()
                self.sent.add(i)

    def wait(self):
        for copy in self.copies:
            copy.wait()


def flush(self):
        if not self.sent:
            self.copy.start()
            self.sent = True


def flush(*refs):
    for ref in refs:
        ref.flush()


def cost(arrays, flops):
    size = sum(math.prod(a.shape) * a.dtype.itemsize for a in arrays) if flops else 0
    return pl.CostEstimate(flops=flops, bytes_accessed=size, transcendentals=0)


def call(kernel, args, outs):
    return pl.pallas_call(
        kernel,
        out_shape=tuple(outs),
        in_specs=[VMEM] * len(args),
        out_specs=tuple([VMEM] * len(outs)),
        compiler_params=pltpu.CompilerParams(vmem_limit_bytes=14 * 2**20),
        cost_estimate=cost(list(args) + list(outs), 0),
    )(*args)


def stream(kernel, args, outs, scratch=(), flops=0, early=None, local=False):
    args = [a if isinstance(a, Far) or a.ndim == 1 else Far(a) for a in args]
    far = [i for i, a in enumerate(args) if isinstance(a, Far)]
    arrays = [a.array if isinstance(a, Far) else a for a in args]
    moved = [((args[i].size,) + args[i].array.shape[1:], args[i].array.dtype) for i in far]
    moved += [] if local else [(o.shape, o.dtype) for o in outs]
    hbm = pl.BlockSpec(memory_space=pltpu.HBM)
    ins, made = len(args), len(args) + len(outs)
    early = len(far) if early is None else early

    def body(*refs):
        buffers, sems, rest = refs[made : made + len(moved)], refs[made + len(moved)], refs[made + len(moved) + 1 :]
        used = 0

        def copies(source, target, dims, first=0):
            nonlocal used
            made_here = []
            for start, size in cuts(dims):
                x, y = source.at[pl.ds(first + start, size)], target.at[pl.ds(start, size)]
                if first == 0 and size == dims[0]:
                    x, y = source, target
                made_here.append(pltpu.make_async_copy(x, y, sems.at[used]))
                used += 1
            return made_here

        reads, later = list(refs[:ins]), []
        for k, i in enumerate(far):
            held = copies(reads[i], buffers[k], moved[k][0], args[i].start)
            reads[i] = Fetched(held, buffers[k], later if k == early - 1 else [])
            if k < early:
                reads[i].start()
            else:
                later.append(reads[i])
        writes = list(refs[ins:made])
        if not local:
            for k, out in enumerate(writes):
                buffer = buffers[len(far) + k]
                writes[k] = Staged(copies(buffer, out, out.shape), buffer)
        kernel(*reads, *writes, *rest)
        if not local:
            flush(*writes)
        for i in far:
            reads[i].wait()
        if not local:
            for write in writes:
                write.wait()

    count = sum(len(cuts(dims)) for dims, _ in moved)
    return pl.pallas_call(
        body,
        out_shape=tuple(outs),
        in_specs=[hbm if isinstance(a, Far) else SMEM for a in args],
        out_specs=tuple([VMEM if local else hbm] * len(outs)),
        scratch_shapes=[pltpu.VMEM(*m) for m in moved] + [pltpu.SemaphoreType.DMA((count,))] + list(scratch),
        compiler_params=pltpu.CompilerParams(vmem_limit_bytes=14 * 2**20 if local else LIMIT),
        cost_estimate=cost(arrays + list(outs), flops),
    )(*arrays)


def shape(dtype, *dims):
    return jax.ShapeDtypeStruct(dims, dtype)


def send_kernel(rows_ref, count_ref, halo_ref, nodes_ref, out_ref, low_ref, high_ref, live_ref):
    slots = rows_ref.shape[1]
    patches = count_ref.shape[1]
    width = nodes_ref.shape[0]
    owner = lax.broadcasted_iota(I32, (patches, slots), 0)
    place = lax.broadcasted_iota(I32, (patches, slots), 1)
    repeat = jnp.where(place // SLOT == owner, 1.0, 0.0).astype(BF)
    counts = jnp.broadcast_to(count_ref[...].astype(F32), (8, patches)).astype(BF)
    spread = dot(counts, repeat)[:1].astype(I32)
    slot = lax.broadcasted_iota(I32, (1, slots), 1) % SLOT
    live = jnp.where(slot < spread, rows_ref[...], -1)
    live_ref[...] = live
    nodes = nodes_ref[...]
    depth = low_ref.shape[0]
    halo = dot(pick(column(halo_ref[...]), width), nodes).astype(BF)
    low_ref[...] = halo[:depth]
    high_ref[...] = halo[depth:]
    flush(low_ref, high_ref, live_ref)
    col = column(live)
    for i, r in enumerate(tiles(slots)):
        out_ref[i, 0] = dot(pick(col[r], width), nodes).astype(BF)
        out_ref.flush(i)


def edge_kernel(
    dst_ref, nodes_ref, wb_ref, na_ref, cot_ref, nsec_ref, src_ref, low_ref, high_ref, wa_ref, edges_ref, wc_ref,
    second_ref, slope_ref, agg_ref, msg_ref, half_ref, ghid_ref, hid_ref,
):
    count, width = nodes_ref.shape
    inner = edges_ref.shape[0] - edges_ref.shape[0] // 4
    dst = column(dst_ref[...])
    nodes = nodes_ref[...]
    src = column(src_ref[...])
    halo = jnp.concatenate([low_ref[...], high_ref[...]], axis=0)
    for r in tiles(edges_ref.shape[0]):
        if r.stop <= inner:
            feat = dot(pick(src[r], count), nodes).astype(BF)
        else:
            feat = dot(pick(src[r] - float(count), halo.shape[0]), halo).astype(BF)
        own = dot(pick(dst[r], count), nodes).astype(BF)
        pre = dot(own, wb_ref[...]) + dot(feat, wa_ref[...]) + dot(edges_ref[r], wc_ref[...])
        sigma = jax.nn.sigmoid(pre)
        hid_ref[r] = (pre * sigma).astype(BF)
        slope_ref[r] = (sigma * (1.0 + pre * (1.0 - sigma))).astype(BF)
    flush(slope_ref)
    for r in tiles(count):
        agg = dot(pick_t(dst_ref[...], r.start, TILE), hid_ref[...]).astype(BF)
        agg_ref[r] = agg
        msg_ref[r] = dot(agg, second_ref[...])
        half_ref[r] = dot(nodes_ref[r], na_ref[...])
        ghid_ref[r] = dot_nt(cot_ref[r], nsec_ref[...])


def put(ref, index, value, first):
    half = value.shape[1] // 2
    own = jnp.where(first, value[:, :half], value[:, half:]).astype(BF)
    send = jnp.where(first, value[:, half:], value[:, :half]).astype(BF)
    for buffer, part in ((ref.own, own), (ref.send, send)):
        buffer[index] = part.reshape(buffer.shape[1:])
        buffer.flush(index)


class Blocks:
    def __init__(self, own, send):
        self.own, self.send = own, send


def node_kernel(
    target_ref, margin_ref, recv_ref, msg_ref, half_ref, nb_ref, ghid_ref,
    ret_ref, gpool_ref, pooled_ref, hid_ref, gnode_ref,
):
    count = msg_ref.shape[0]
    target, margin = target_ref[...], margin_ref[...]
    for r in tiles(count):
        coupled = dot(pick_t(target, r.start, TILE, margin), recv_ref[...])
        pooled = (msg_ref[r] + coupled).astype(BF)
        pooled_ref[r] = pooled
        pre = half_ref[r] + dot(pooled, nb_ref[...])
        sigma = jax.nn.sigmoid(pre)
        hid_ref[r] = (pre * sigma).astype(BF)
        gnode = (ghid_ref[r] * (sigma * (1.0 + pre * (1.0 - sigma)))).astype(BF)
        gnode_ref[r] = gnode
        gpool_ref[r] = dot_nt(gnode, nb_ref[...]).astype(BF)
    flush(gpool_ref, gnode_ref, pooled_ref, hid_ref)
    gpool = gpool_ref[...]
    col, weight = column(target), column(margin)
    for i, r in enumerate(tiles(recv_ref.shape[0])):
        ret_ref[i, 0] = dot(pick(col[r], count, weight[r]), gpool).astype(BF)
        ret_ref.flush(i)


def grad_kernel(
    side_ref, nodes_ref, gnode_ref, gpool_ref, agg_ref, dst_ref, esec_ref, slope_ref, src_ref, pooled_ref,
    edges_ref, hid_ref, cot_ref, low_ref, high_ref, wa_ref,
    send_ref, own_ref, gedge_ref, bysrc_ref, bydst_ref, glow_ref, ghigh_ref, turned_ref,
    *, patches, scale
):
    count, width = nodes_ref.shape
    inner = edges_ref.shape[0] - edges_ref.shape[0] // 4
    depth = low_ref.shape[0]
    first = side_ref[0] == 0
    order = row_order(width, patches)
    blocks = Blocks(own_ref, send_ref)
    turned_ref[...] = dot_nt(order, nodes_ref[...]).astype(BF)
    put(blocks, 4, dot(turned_ref[...], gnode_ref[...]) * scale, first)
    put(blocks, 3, dot(dot_nt(order, agg_ref[...]).astype(BF), gpool_ref[...]) * scale, first)
    gpool = gpool_ref[...]
    dst_row, src_row = dst_ref[...], src_ref[...]
    dst = column(dst_row)
    for r in tiles(edges_ref.shape[0]):
        message = dot(pick(dst[r], count), gpool).astype(BF)
        gedge_ref[r] = (dot_nt(message, esec_ref[...]) * slope_ref[r].astype(F32)).astype(BF)
    flush(gedge_ref)
    for r in tiles(count):
        bydst_ref[r] = dot(pick_t(dst_row, r.start, TILE), gedge_ref[...]).astype(BF)
        bysrc_ref[r] = dot(pick_t(src_row[:, :inner], r.start, TILE), gedge_ref[:inner]).astype(BF)
    flush(bysrc_ref, bydst_ref)
    put(blocks, 1, dot(turned_ref[...], bydst_ref[...]) * scale, first)
    halo = dot(pick_t(src_row[:, inner:], count, 2 * depth), gedge_ref[inner:]).astype(BF)
    rim = dot_nt(order, jnp.concatenate([low_ref[...], high_ref[...]], axis=0)).astype(BF)
    put(blocks, 0, (dot(turned_ref[...], bysrc_ref[...]) + dot(rim, halo)) * scale, first)
    back = dot_nt(halo, wa_ref[...]).astype(BF)
    glow_ref[...] = back[:depth]
    ghigh_ref[...] = back[depth:]
    flush(glow_ref, ghigh_ref)
    pairs = ((2, edges_ref, gedge_ref), (5, pooled_ref, gnode_ref), (6, hid_ref, cot_ref))
    for index, left, right in pairs:
        turned = dot_nt(order, left[...]).astype(BF)
        put(blocks, index, dot(turned, right[...]) * scale, first)


def rest_kernel(
    gedge_ref, wc_ref, hid_ref, nsec_ref, nodes_ref, bysrc_ref, wa_ref, bydst_ref, wb_ref, gnode_ref, na_ref,
    cot_ref, edge_ref, new_ref, total_ref,
):
    for r in tiles(gedge_ref.shape[0]):
        edge_ref[r] = dot_nt(gedge_ref[r], wc_ref[...]).astype(BF)
    flush(edge_ref)
    for r in tiles(bysrc_ref.shape[0]):
        new_ref[r] = (nodes_ref[r].astype(F32) + dot(hid_ref[r], nsec_ref[...])).astype(BF)
    flush(new_ref)
    for r in tiles(bysrc_ref.shape[0]):
        total_ref[r] = (
            cot_ref[r].astype(F32)
            + dot_nt(bysrc_ref[r], wa_ref[...])
            + dot_nt(bydst_ref[r], wb_ref[...])
            + dot_nt(gnode_ref[r], na_ref[...])
        )


def last_kernel(live_ref, halo_ref, total_ref, low_ref, high_ref, back_ref, out_ref):
    halo_back = jnp.concatenate([low_ref[...], high_ref[...]], axis=0)
    for r in tiles(total_ref.shape[0]):
        out_ref[r] = (
            total_ref[r]
            + dot(pick_t(halo_ref[...], r.start, TILE), halo_back)
            + dot(pick_t(live_ref[...], r.start, TILE), back_ref[...])
        ).astype(BF)


def from_partner(value):
    return lax.ppermute(value, "mesh", [(0, 1), (1, 0)])


def shift(value, step):
    count = lax.axis_size("patch")
    return lax.ppermute(value, "patch", [(i, (i + step) % count) for i in range(count)])


def route(crossed):
    rows, width = crossed.shape
    patches = lax.axis_size("patch")
    crossed = crossed.reshape(patches, rows // patches, width)
    routed = lax.all_to_all(crossed, "patch", split_axis=0, concat_axis=0, tiled=True)
    return routed.reshape(rows, width)


def hop(value, dz):
    patches = lax.axis_size("patch")
    pairs = [(p, (p + dz * PLANE) % patches) for p in range(patches)]
    return lax.ppermute(value, "patch", pairs)


def join_kernel(own_ref, other_ref, out_ref):
    for block in range(out_ref.shape[1]):
        out_ref[:, block] = (own_ref[block].astype(F32) + other_ref[block].astype(F32)).astype(BF)


def total_of(refs):
    total = refs[0][...].astype(F32)
    for ref in refs[1:]:
        total = total + ref[...].astype(F32)
    return total


def depth_kernel(place_ref, in_ref, keep_ref, send_ref, hold):
    depth = hold.shape[0]
    count, blocks, rows, _ = in_ref.shape
    fine = rows // depth
    hold[...] = jnp.zeros(hold.shape, F32)
    for block in range(blocks):
        total = in_ref[0, block].astype(F32)
        for i in range(1, count):
            total = total + in_ref[i, block].astype(F32)
        for d in range(depth):
            hold[d, block * fine : (block + 1) * fine] = total[d * fine : (d + 1) * fine]
    even = (place_ref[1] // PLANE) % 2 == 0
    for j in range(depth // 2):
        low, high = hold[2 * j], hold[2 * j + 1]
        keep_ref[j] = jnp.where(even, low, high)
        send_ref[j] = jnp.where(even, high, low).astype(BF)


def pair_kernel(place_ref, keep_ref, other_ref, *outs):
    mine = place_ref[1] // PLANE // 2
    for d, out in enumerate(outs):
        j = (mine + d) % len(outs)
        out[...] = keep_ref[j] + other_ref[j].astype(F32)


def sum_kernel(*refs):
    refs[-1][...] = total_of(refs[:-1])


def finish_kernel(place_ref, own_ref, other_ref, out_ref):
    first = place_ref[0] == 0
    lane = own_ref.shape[1]
    left = jnp.where(first, own_ref[...], other_ref[...])
    right = jnp.where(first, other_ref[...], own_ref[...])
    blocks, width = out_ref.shape
    for block in range(blocks):
        for k in range(width // (2 * lane)):
            row = block * (width // (2 * lane)) + k
            start = 2 * k * lane
            out_ref[block : block + 1, start : start + lane] = left[row : row + 1]
            out_ref[block : block + 1, start + lane : start + 2 * lane] = right[row : row + 1]


def small_call(kernel, place, args, outs, scratch=()):
    return pl.pallas_call(
        kernel,
        out_shape=tuple(outs),
        in_specs=[SMEM] + [VMEM] * len(args),
        out_specs=tuple([VMEM] * len(outs)),
        scratch_shapes=list(scratch),
        compiler_params=pltpu.CompilerParams(vmem_limit_bytes=14 * 2**20),
        cost_estimate=cost(list(args) + list(outs), 0),
    )(place, *args)


def weight_sums(own, other, place, couple_back, total, rims, last):
    patches = lax.axis_size("patch")
    depth = patches // PLANE
    blocks, planes, rows, lane = own.shape
    fine = rows // depth
    other, total = lax.optimization_barrier((other, total))
    (paired,) = stream(join_kernel, (own, other), (shape(BF, planes, blocks, rows, lane),), local=True)
    back_low, back_high = shift(rims[1], 1), shift(rims[0], -1)
    paired, couple_back, back_low, back_high = lax.optimization_barrier(
        (paired, couple_back, back_low, back_high)
    )
    groups = [[z * PLANE + i for i in range(PLANE)] for z in range(depth)]
    pieces = lax.all_to_all(
        paired, "patch", split_axis=0, concat_axis=0, axis_index_groups=groups, tiled=True
    )
    padded = (blocks * fine + 15) // 16 * 16
    half = depth // 2
    keep, send = stream(
        depth_kernel,
        (place, pieces),
        (shape(F32, half, padded, lane), shape(BF, half, padded, lane)),
        scratch=(pltpu.VMEM((depth, padded, lane), F32),),
        local=True,
    )
    final = last(total, back_low, back_high, couple_back)
    send, final = lax.optimization_barrier((send, final))
    pairs = [(p, (p // PLANE ^ 1) * PLANE + p % PLANE) for p in range(patches)]
    other = lax.ppermute(send, "patch", pairs)
    pieces = small_call(pair_kernel, place, (keep, other), (shape(F32, padded, lane),) * half)
    pieces = [pieces[0]] + [hop(pieces[d], 2 * d) for d in range(1, half)]
    (own,) = call(sum_kernel, pieces, (shape(F32, padded, lane),))
    (result,) = small_call(
        finish_kernel, place, (own, from_partner(own)), (shape(F32, blocks, fine * 2 * lane),)
    )
    return result, final


def shards(
    nodes,
    edges,
    cot_nodes,
    weights,
    edge_src,
    edge_dst,
    halo_rows,
    couple_rows,
    couple_count,
    couple_target,
    couple_weight,
):
    nodes_own = nodes[0]
    edges_own = edges[0]
    cotangent = cot_nodes[0]
    count, width = nodes_own.shape
    edge_count = edges_own.shape[0]
    depth = halo_rows.shape[1] // 2
    patches = lax.axis_size("patch")
    slots = couple_rows.shape[2]
    scale = 1.0 / math.sqrt(2 * patches * edge_count)
    side = jnp.stack([lax.axis_index("mesh"), lax.axis_index("patch")]).astype(I32)
    target, margin = couple_target[0], couple_weight[0]
    unit = 2 * width * width

    def weight(block):
        return Far(weights, block * width, width)

    def weight(block):
        return Far(weights, block * width, width)

    slot_block = shape(BF, slots // TILE, 1, TILE, width)
    outgoing, low_out, high_out, live = stream(
        send_kernel,
        (couple_rows[0], couple_count[0], halo_rows, nodes_own),
        (slot_block, shape(BF, depth, width), shape(BF, depth, width), shape(I32, 1, slots)),
        flops=(slots + 2 * depth) * unit,
    )
    crossed = from_partner(outgoing.reshape(slots, width))
    low, high = shift(high_out, 1), shift(low_out, -1)
    crossed, low, high = lax.optimization_barrier((crossed, low, high))
    received = route(crossed)
    slope, agg, message, half, grad_hidden = stream(
        edge_kernel,
        (
            edge_dst, nodes_own, weight(1), weight(4), cotangent, weight(6), edge_src, low, high,
            weight(0), edges_own, weight(2), weight(3),
        ),
        (shape(BF, edge_count, width), shape(BF, count, width)) + (shape(F32, count, width),) * 3,
        scratch=(pltpu.VMEM((edge_count, width), BF),),
        flops=edge_count * 6 * unit,
    )
    square = shape(BF, count, width)
    grads = shape(BF, 7, PLANE, width // PLANE, width // 2)
    rim = shape(BF, depth, width)
    edge_block = shape(BF, edge_count, width)
    returned, grad_pooled, pooled, hidden, grad_node_pre = stream(
        node_kernel,
        (target, margin, received, message, half, weight(5), grad_hidden),
        (slot_block, square, square, square, square),
        flops=count * 8 * unit,
    )
    crossed_back = from_partner(returned.reshape(slots, width))
    couple_back = route(crossed_back)
    grad_pooled, crossed_back = lax.optimization_barrier((grad_pooled, crossed_back))
    send, own, grad_edge_pre, by_source, by_target, grad_low, grad_high = stream(
        lambda *refs: grad_kernel(*refs, patches=patches, scale=scale),
        (
            side, nodes_own, grad_node_pre, grad_pooled, agg, edge_dst, weight(3), slope, edge_src, pooled,
            edges_own, hidden, cotangent, low, high, weight(0),
        ),
        (grads, grads, edge_block, square, square, rim, rim),
        scratch=[pltpu.VMEM((count, width), BF)],
        early=4,
    )
    other = from_partner(send)
    edge_grads, new_nodes, total = stream(
        rest_kernel,
        (
            grad_edge_pre, weight(2), hidden, weight(6), nodes_own, by_source, weight(0), by_target,
            weight(1), grad_node_pre, weight(4), cotangent,
        ),
        (edge_block, square, shape(F32, count, width)),
        flops=edge_count * 300 * unit,
    )

    def last(sums, back_low, back_high, back):
        (final,) = stream(
            last_kernel,
            (live, halo_rows, sums, back_low, back_high, back),
            (square,),
            flops=count * 2 * unit,
        )
        return final

    summed, node_grads = weight_sums(own, other, side, couple_back, total, (grad_low, grad_high), last)
    return (new_nodes[None], node_grads[None], edge_grads[None], summed)


def solution(mesh):
    return jax.shard_map(
        shards,
        mesh=mesh,
        in_specs=(
            P("mesh", "patch", None),
            P("mesh", "patch", None),
            P("mesh", "patch", None),
            P(),
            P("mesh", "patch"),
            P("mesh", "patch"),
            P("mesh", "patch"),
            P("mesh", "patch", None),
            P("mesh", "patch", None),
            P("mesh", "patch", None),
            P("mesh", "patch", None),
        ),
        out_specs=(
            P("mesh", "patch", None),
            P("mesh", "patch", None),
            P("mesh", "patch", None),
            P(None, "patch"),
        ),
        check_vma=False,
    )
```

```python
import math

import jax
import jax.numpy as jnp
from jax import lax
from jax.experimental import pallas as pl
from jax.experimental.pallas import tpu as pltpu
from jax.sharding import PartitionSpec as P

SLOT = 8
RING = 4
PLANE = RING * RING
TILE = 256
LIMIT = 61 * 2**20 - 2**16
BF = jnp.bfloat16
F32 = jnp.float32
I32 = jnp.int32
VMEM = pl.BlockSpec(memory_space=pltpu.VMEM)
SMEM = pl.BlockSpec(memory_space=pltpu.SMEM)


def dot(a, b):
    return jnp.dot(a, b, preferred_element_type=F32)


def dot_nt(a, b):
    return lax.dot_general(a, b, (((1,), (1,)), ((), ())), preferred_element_type=F32)


def column(row):
    return jnp.transpose(jnp.broadcast_to(row.astype(F32), (128, row.shape[1])))


def pick(col, count, value=None):
    base = lax.broadcasted_iota(I32, (col.shape[0], 128), 1).astype(F32)
    one = jnp.ones_like(base) if value is None else value
    parts = [jnp.where(col == base + float(k), one, 0.0).astype(BF) for k in range(0, count, 128)]
    return parts[0] if len(parts) == 1 else jnp.concatenate(parts, axis=1)


def pick_t(row, start, size, value=None):
    base = lax.broadcasted_iota(I32, (size, row.shape[1]), 0) + start
    one = jnp.ones(base.shape, F32) if value is None else jnp.broadcast_to(value, base.shape)
    return jnp.where(base == row, one, 0.0).astype(BF)


def row_order(place, width, patches):
    fine = width // patches
    depth = patches // PLANE
    row = lax.broadcasted_iota(I32, (width, width), 0)
    col = lax.broadcasted_iota(I32, (width, width), 1)
    dx, dy = row // (width // RING), (row // (width // PLANE)) % RING
    dz, offset = (row // fine) % depth, row % fine
    x, y = place % RING, (place // RING) % RING
    patch = dz * PLANE + (y + dy) % RING * RING + (x + dx) % RING
    return jnp.where(col == patch * fine + offset, 1.0, 0.0).astype(BF)


def tiles(count):
    return [slice(i, i + TILE) for i in range(0, count, TILE)]


class Far:
    def __init__(self, array, start=0, size=None):
        self.array = array
        self.start = start
        self.size = array.shape[0] if size is None else size


class Fetched:
    def __init__(self, copies, buffer, then):
        self.copies, self.buffer, self.then = copies, buffer, then
        self.started, self.waited = False, False
        self.shape = buffer.shape

    def start(self):
        if not self.started:
            self.started = True
            for copy in self.copies:
                copy.start()

    def wait(self):
        if not self.waited:
            self.waited = True
            self.start()
            for copy in self.copies:
                copy.wait()
            for later in self.then:
                later.start()

    def __getitem__(self, index):
        self.wait()
        return self.buffer[index]


def cuts(dims):
    if len(dims) > 3:
        return [(i, 1) for i in range(dims[0])]
    step = TILE if len(dims) == 2 and dims[0] % TILE == 0 else dims[0]
    return [(i, step) for i in range(0, dims[0], step)]


class Staged:
    def __init__(self, copies, buffer):
        self.copies, self.buffer, self.sent = copies, buffer, set()
        self.shape = buffer.shape

    def __getitem__(self, index):
        return self.buffer[index]

    def __setitem__(self, index, value):
        self.buffer[index] = value

    def flush(self, index=None):
        for i in range(len(self.copies)) if index is None else [index]:
            if i not in self.sent:
                self.copies[i].start()
                self.sent.add(i)

    def wait(self):
        for copy in self.copies:
            copy.wait()


def flush(self):
        if not self.sent:
            self.copy.start()
            self.sent = True


def flush(*refs):
    for ref in refs:
        ref.flush()


def cost(arrays, flops):
    size = sum(math.prod(a.shape) * a.dtype.itemsize for a in arrays) if flops else 0
    return pl.CostEstimate(flops=flops, bytes_accessed=size, transcendentals=0)


def call(kernel, args, outs):
    return pl.pallas_call(
        kernel,
        out_shape=tuple(outs),
        in_specs=[VMEM] * len(args),
        out_specs=tuple([VMEM] * len(outs)),
        compiler_params=pltpu.CompilerParams(vmem_limit_bytes=14 * 2**20),
        cost_estimate=cost(list(args) + list(outs), 0),
    )(*args)


def stream(kernel, args, outs, scratch=(), flops=0, early=None, local=False):
    args = [a if isinstance(a, Far) or a.ndim == 1 else Far(a) for a in args]
    far = [i for i, a in enumerate(args) if isinstance(a, Far)]
    arrays = [a.array if isinstance(a, Far) else a for a in args]
    moved = [((args[i].size,) + args[i].array.shape[1:], args[i].array.dtype) for i in far]
    moved += [] if local else [(o.shape, o.dtype) for o in outs]
    hbm = pl.BlockSpec(memory_space=pltpu.HBM)
    ins, made = len(args), len(args) + len(outs)
    early = len(far) if early is None else early

    def body(*refs):
        buffers, sems, rest = refs[made : made + len(moved)], refs[made + len(moved)], refs[made + len(moved) + 1 :]
        used = 0

        def copies(source, target, dims, first=0):
            nonlocal used
            made_here = []
            for start, size in cuts(dims):
                x, y = source.at[pl.ds(first + start, size)], target.at[pl.ds(start, size)]
                if first == 0 and size == dims[0]:
                    x, y = source, target
                made_here.append(pltpu.make_async_copy(x, y, sems.at[used]))
                used += 1
            return made_here

        reads, later = list(refs[:ins]), []
        for k, i in enumerate(far):
            held = copies(reads[i], buffers[k], moved[k][0], args[i].start)
            reads[i] = Fetched(held, buffers[k], later if k == early - 1 else [])
            if k < early:
                reads[i].start()
            else:
                later.append(reads[i])
        writes = list(refs[ins:made])
        if not local:
            for k, out in enumerate(writes):
                buffer = buffers[len(far) + k]
                writes[k] = Staged(copies(buffer, out, out.shape), buffer)
        kernel(*reads, *writes, *rest)
        if not local:
            flush(*writes)
        for i in far:
            reads[i].wait()
        if not local:
            for write in writes:
                write.wait()

    count = sum(len(cuts(dims)) for dims, _ in moved)
    return pl.pallas_call(
        body,
        out_shape=tuple(outs),
        in_specs=[hbm if isinstance(a, Far) else SMEM for a in args],
        out_specs=tuple([VMEM if local else hbm] * len(outs)),
        scratch_shapes=[pltpu.VMEM(*m) for m in moved] + [pltpu.SemaphoreType.DMA((count,))] + list(scratch),
        compiler_params=pltpu.CompilerParams(vmem_limit_bytes=14 * 2**20 if local else LIMIT),
        cost_estimate=cost(arrays + list(outs), flops),
    )(*arrays)


def shape(dtype, *dims):
    return jax.ShapeDtypeStruct(dims, dtype)


def send_kernel(rows_ref, count_ref, halo_ref, nodes_ref, out_ref, low_ref, high_ref, live_ref):
    slots = rows_ref.shape[1]
    patches = count_ref.shape[1]
    width = nodes_ref.shape[0]
    owner = lax.broadcasted_iota(I32, (patches, slots), 0)
    place = lax.broadcasted_iota(I32, (patches, slots), 1)
    repeat = jnp.where(place // SLOT == owner, 1.0, 0.0).astype(BF)
    counts = jnp.broadcast_to(count_ref[...].astype(F32), (8, patches)).astype(BF)
    spread = dot(counts, repeat)[:1].astype(I32)
    slot = lax.broadcasted_iota(I32, (1, slots), 1) % SLOT
    live = jnp.where(slot < spread, rows_ref[...], -1)
    live_ref[...] = live
    nodes = nodes_ref[...]
    depth = low_ref.shape[0]
    halo = dot(pick(column(halo_ref[...]), width), nodes).astype(BF)
    low_ref[...] = halo[:depth]
    high_ref[...] = halo[depth:]
    flush(low_ref, high_ref, live_ref)
    col = column(live)
    for i, r in enumerate(tiles(slots)):
        out_ref[i, 0] = dot(pick(col[r], width), nodes).astype(BF)
        out_ref.flush(i)


def edge_kernel(
    dst_ref, nodes_ref, wb_ref, na_ref, cot_ref, nsec_ref, src_ref, low_ref, high_ref, wa_ref, edges_ref, wc_ref,
    second_ref, slope_ref, agg_ref, msg_ref, half_ref, ghid_ref, hid_ref,
):
    count, width = nodes_ref.shape
    inner = edges_ref.shape[0] - edges_ref.shape[0] // 4
    dst = column(dst_ref[...])
    nodes = nodes_ref[...]
    src = column(src_ref[...])
    halo = jnp.concatenate([low_ref[...], high_ref[...]], axis=0)
    for r in tiles(edges_ref.shape[0]):
        if r.stop <= inner:
            feat = dot(pick(src[r], count), nodes).astype(BF)
        else:
            feat = dot(pick(src[r] - float(count), halo.shape[0]), halo).astype(BF)
        own = dot(pick(dst[r], count), nodes).astype(BF)
        pre = dot(own, wb_ref[...]) + dot(feat, wa_ref[...]) + dot(edges_ref[r], wc_ref[...])
        sigma = jax.nn.sigmoid(pre)
        hid_ref[r] = (pre * sigma).astype(BF)
        slope_ref[r] = (sigma * (1.0 + pre * (1.0 - sigma))).astype(BF)
    flush(slope_ref)
    for r in tiles(count):
        agg = dot(pick_t(dst_ref[...], r.start, TILE), hid_ref[...]).astype(BF)
        agg_ref[r] = agg
        msg_ref[r] = dot(agg, second_ref[...])
        half_ref[r] = dot(nodes_ref[r], na_ref[...])
        ghid_ref[r] = dot_nt(cot_ref[r], nsec_ref[...])


def put(ref, index, value, first):
    half = value.shape[1] // 2
    lane = half // 2
    step = value.shape[0] // RING
    fine = step // RING
    own = jnp.where(first, value[:, :half], value[:, half:]).astype(BF)
    send = jnp.where(first, value[:, half:], value[:, :half]).astype(BF)
    for buffer, part in ((ref.own, own), (ref.send, send)):
        for i in range(RING):
            buffer[index, 0, i] = part[i * step : (i + 1) * step, :lane]
            for j in range(RING):
                start = i * step + j * fine
                buffer[index, 1, j, i * fine : (i + 1) * fine] = part[start : start + fine, lane:]
        buffer.flush(index)


class Blocks:
    def __init__(self, own, send):
        self.own, self.send = own, send


def node_kernel(
    target_ref, margin_ref, recv_ref, msg_ref, half_ref, nb_ref, ghid_ref,
    ret_ref, gpool_ref, pooled_ref, hid_ref, gnode_ref,
):
    count = msg_ref.shape[0]
    target, margin = target_ref[...], margin_ref[...]
    for r in tiles(count):
        coupled = dot(pick_t(target, r.start, TILE, margin), recv_ref[...])
        pooled = (msg_ref[r] + coupled).astype(BF)
        pooled_ref[r] = pooled
        pre = half_ref[r] + dot(pooled, nb_ref[...])
        sigma = jax.nn.sigmoid(pre)
        hid_ref[r] = (pre * sigma).astype(BF)
        gnode = (ghid_ref[r] * (sigma * (1.0 + pre * (1.0 - sigma)))).astype(BF)
        gnode_ref[r] = gnode
        gpool_ref[r] = dot_nt(gnode, nb_ref[...]).astype(BF)
    flush(gpool_ref, gnode_ref, pooled_ref, hid_ref)
    gpool = gpool_ref[...]
    col, weight = column(target), column(margin)
    for i, r in enumerate(tiles(recv_ref.shape[0])):
        ret_ref[i, 0] = dot(pick(col[r], count, weight[r]), gpool).astype(BF)
        ret_ref.flush(i)


def grad_kernel(
    side_ref, nodes_ref, gnode_ref, gpool_ref, agg_ref, dst_ref, esec_ref, slope_ref, src_ref, pooled_ref,
    edges_ref, hid_ref, cot_ref, low_ref, high_ref, wa_ref,
    send_ref, own_ref, gedge_ref, bysrc_ref, bydst_ref, glow_ref, ghigh_ref, turned_ref,
    *, patches, scale
):
    count, width = nodes_ref.shape
    inner = edges_ref.shape[0] - edges_ref.shape[0] // 4
    depth = low_ref.shape[0]
    first = side_ref[0] == 0
    order = row_order(side_ref[1], width, patches)
    blocks = Blocks(own_ref, send_ref)
    turned_ref[...] = dot_nt(order, nodes_ref[...]).astype(BF)
    put(blocks, 4, dot(turned_ref[...], gnode_ref[...]) * scale, first)
    put(blocks, 3, dot(dot_nt(order, agg_ref[...]).astype(BF), gpool_ref[...]) * scale, first)
    gpool = gpool_ref[...]
    dst_row, src_row = dst_ref[...], src_ref[...]
    dst = column(dst_row)
    for r in tiles(edges_ref.shape[0]):
        message = dot(pick(dst[r], count), gpool).astype(BF)
        gedge_ref[r] = (dot_nt(message, esec_ref[...]) * slope_ref[r].astype(F32)).astype(BF)
    flush(gedge_ref)
    for r in tiles(count):
        bydst_ref[r] = dot(pick_t(dst_row, r.start, TILE), gedge_ref[...]).astype(BF)
        bysrc_ref[r] = dot(pick_t(src_row[:, :inner], r.start, TILE), gedge_ref[:inner]).astype(BF)
    flush(bysrc_ref, bydst_ref)
    put(blocks, 1, dot(turned_ref[...], bydst_ref[...]) * scale, first)
    halo = dot(pick_t(src_row[:, inner:], count, 2 * depth), gedge_ref[inner:]).astype(BF)
    rim = dot_nt(order, jnp.concatenate([low_ref[...], high_ref[...]], axis=0)).astype(BF)
    put(blocks, 0, (dot(turned_ref[...], bysrc_ref[...]) + dot(rim, halo)) * scale, first)
    back = dot_nt(halo, wa_ref[...]).astype(BF)
    glow_ref[...] = back[:depth]
    ghigh_ref[...] = back[depth:]
    flush(glow_ref, ghigh_ref)
    pairs = ((2, edges_ref, gedge_ref), (5, pooled_ref, gnode_ref), (6, hid_ref, cot_ref))
    for index, left, right in pairs:
        turned = dot_nt(order, left[...]).astype(BF)
        put(blocks, index, dot(turned, right[...]) * scale, first)


def rest_kernel(
    gedge_ref, wc_ref, hid_ref, nsec_ref, nodes_ref, bysrc_ref, wa_ref, bydst_ref, wb_ref, gnode_ref, na_ref,
    cot_ref, edge_ref, new_ref, total_ref,
):
    for r in tiles(gedge_ref.shape[0]):
        edge_ref[r] = dot_nt(gedge_ref[r], wc_ref[...]).astype(BF)
    flush(edge_ref)
    for r in tiles(bysrc_ref.shape[0]):
        new_ref[r] = (nodes_ref[r].astype(F32) + dot(hid_ref[r], nsec_ref[...])).astype(BF)
    flush(new_ref)
    for r in tiles(bysrc_ref.shape[0]):
        total_ref[r] = (
            cot_ref[r].astype(F32)
            + dot_nt(bysrc_ref[r], wa_ref[...])
            + dot_nt(bydst_ref[r], wb_ref[...])
            + dot_nt(gnode_ref[r], na_ref[...])
        )


def last_kernel(live_ref, halo_ref, total_ref, low_ref, high_ref, back_ref, out_ref):
    halo_back = jnp.concatenate([low_ref[...], high_ref[...]], axis=0)
    for r in tiles(total_ref.shape[0]):
        out_ref[r] = (
            total_ref[r]
            + dot(pick_t(halo_ref[...], r.start, TILE), halo_back)
            + dot(pick_t(live_ref[...], r.start, TILE), back_ref[...])
        ).astype(BF)


def from_partner(value):
    return lax.ppermute(value, "mesh", [(0, 1), (1, 0)])


def shift(value, step):
    count = lax.axis_size("patch")
    return lax.ppermute(value, "patch", [(i, (i + step) % count) for i in range(count)])


def route(crossed):
    rows, width = crossed.shape
    patches = lax.axis_size("patch")
    crossed = crossed.reshape(patches, rows // patches, width)
    routed = lax.all_to_all(crossed, "patch", split_axis=0, concat_axis=0, tiled=True)
    return routed.reshape(rows, width)


def hop(value, dz=0, dy=0, dx=0):
    depth = lax.axis_size("patch") // PLANE
    pairs = []
    for p in range(depth * PLANE):
        z, y, x = p // PLANE, p // RING % RING, p % RING
        pairs.append((p, (z + dz) % depth * PLANE + (y + dy) % RING * RING + (x + dx) % RING))
    return lax.ppermute(value, "patch", pairs)


def join_kernel(own_ref, other_ref, *outs):
    for index, out in enumerate(outs):
        c, d = index // RING, index % RING
        out[...] = (own_ref[:, c, d].astype(F32) + other_ref[:, c, d].astype(F32)).astype(BF)


def total_of(refs):
    total = refs[0][...].astype(F32)
    for ref in refs[1:]:
        total = total + ref[...].astype(F32)
    return total


def plane_kernel(*refs):
    for c in range(2):
        total = total_of(refs[c * RING : (c + 1) * RING])
        fine = total.shape[1] // RING
        for d in range(RING):
            refs[(2 + c) * RING + d][...] = total[:, d * fine : (d + 1) * fine].astype(BF)


def depth_kernel(place_ref, *refs):
    ins, (keep_ref, send_ref, hold) = refs[: 2 * RING], refs[2 * RING :]
    depth = hold.shape[0]
    hold[...] = jnp.zeros(hold.shape, F32)
    for c in range(2):
        total = total_of(ins[c * RING : (c + 1) * RING])
        blocks, rows, lane = total.shape
        fine = rows // depth
        for block in range(blocks):
            for d in range(depth):
                hold[d, block * fine : (block + 1) * fine, c * lane : (c + 1) * lane] = total[
                    block, d * fine : (d + 1) * fine
                ]
    even = (place_ref[1] // PLANE) % 2 == 0
    for j in range(depth // 2):
        low, high = hold[2 * j], hold[2 * j + 1]
        keep_ref[j] = jnp.where(even, low, high)
        send_ref[j] = jnp.where(even, high, low).astype(BF)


def pair_kernel(place_ref, keep_ref, other_ref, *outs):
    mine = place_ref[1] // PLANE // 2
    for d, out in enumerate(outs):
        j = (mine + d) % len(outs)
        out[...] = keep_ref[j] + other_ref[j].astype(F32)


def sum_kernel(*refs):
    refs[-1][...] = total_of(refs[:-1])


def finish_kernel(place_ref, own_ref, other_ref, out_ref):
    first = place_ref[0] == 0
    lane = own_ref.shape[1]
    left = jnp.where(first, own_ref[...], other_ref[...])
    right = jnp.where(first, other_ref[...], own_ref[...])
    blocks, width = out_ref.shape
    for block in range(blocks):
        for k in range(width // (2 * lane)):
            row = block * (width // (2 * lane)) + k
            start = 2 * k * lane
            out_ref[block : block + 1, start : start + lane] = left[row : row + 1]
            out_ref[block : block + 1, start + lane : start + 2 * lane] = right[row : row + 1]


def small_call(kernel, place, args, outs, scratch=()):
    return pl.pallas_call(
        kernel,
        out_shape=tuple(outs),
        in_specs=[SMEM] + [VMEM] * len(args),
        out_specs=tuple([VMEM] * len(outs)),
        scratch_shapes=list(scratch),
        compiler_params=pltpu.CompilerParams(vmem_limit_bytes=14 * 2**20),
        cost_estimate=cost(list(args) + list(outs), 0),
    )(place, *args)


def spread(pieces, axes):
    return [
        pieces[c * RING + d] if d == 0 else hop(pieces[c * RING + d], **{axis: d})
        for c, axis in enumerate(axes)
        for d in range(RING)
    ]


def weight_sums(own, other, place, couple_back, total, rims, last):
    patches = lax.axis_size("patch")
    depth = patches // PLANE
    blocks, _, _, rows, lane = own.shape
    fine = rows // RING // depth
    other, total = lax.optimization_barrier((other, total))
    pieces = stream(join_kernel, (own, other), (shape(BF, blocks, rows, lane),) * (2 * RING), local=True)
    back_low, back_high = shift(rims[1], 1), shift(rims[0], -1)
    pieces, back_low, back_high = lax.optimization_barrier((pieces, back_low, back_high))
    pieces = spread(pieces, ("dx", "dy"))
    pieces, couple_back, total = lax.optimization_barrier((pieces, couple_back, total))
    pieces = call(plane_kernel, pieces, (shape(BF, blocks, rows // RING, lane),) * (2 * RING))
    final = last(total, back_low, back_high, couple_back)
    pieces = spread(pieces, ("dy", "dx"))
    pieces, final = lax.optimization_barrier((pieces, final))
    padded = (blocks * fine + 15) // 16 * 16
    half = depth // 2
    keep, send = small_call(
        depth_kernel,
        place,
        pieces,
        (shape(F32, half, padded, 2 * lane), shape(BF, half, padded, 2 * lane)),
        scratch=(pltpu.VMEM((depth, padded, 2 * lane), F32),),
    )
    pairs = [(p, (p // PLANE ^ 1) * PLANE + p % PLANE) for p in range(patches)]
    other = lax.ppermute(send, "patch", pairs)
    pieces = small_call(pair_kernel, place, (keep, other), (shape(F32, padded, 2 * lane),) * half)
    pieces = [pieces[0]] + [hop(pieces[d], dz=2 * d) for d in range(1, half)]
    (own,) = call(sum_kernel, pieces, (shape(F32, padded, 2 * lane),))
    (result,) = small_call(
        finish_kernel, place, (own, from_partner(own)), (shape(F32, blocks, fine * 4 * lane),)
    )
    return result, final


def shards(
    nodes,
    edges,
    cot_nodes,
    weights,
    edge_src,
    edge_dst,
    halo_rows,
    couple_rows,
    couple_count,
    couple_target,
    couple_weight,
):
    nodes_own = nodes[0]
    edges_own = edges[0]
    cotangent = cot_nodes[0]
    count, width = nodes_own.shape
    edge_count = edges_own.shape[0]
    depth = halo_rows.shape[1] // 2
    patches = lax.axis_size("patch")
    slots = couple_rows.shape[2]
    scale = 1.0 / math.sqrt(2 * patches * edge_count)
    side = jnp.stack([lax.axis_index("mesh"), lax.axis_index("patch")]).astype(I32)
    target, margin = couple_target[0], couple_weight[0]
    unit = 2 * width * width

    def weight(block):
        return Far(weights, block * width, width)

    def weight(block):
        return Far(weights, block * width, width)

    slot_block = shape(BF, slots // TILE, 1, TILE, width)
    outgoing, low_out, high_out, live = stream(
        send_kernel,
        (couple_rows[0], couple_count[0], halo_rows, nodes_own),
        (slot_block, shape(BF, depth, width), shape(BF, depth, width), shape(I32, 1, slots)),
        flops=(slots + 2 * depth) * unit,
    )
    crossed = from_partner(outgoing.reshape(slots, width))
    low, high = shift(high_out, 1), shift(low_out, -1)
    crossed, low, high = lax.optimization_barrier((crossed, low, high))
    received = route(crossed)
    slope, agg, message, half, grad_hidden = stream(
        edge_kernel,
        (
            edge_dst, nodes_own, weight(1), weight(4), cotangent, weight(6), edge_src, low, high,
            weight(0), edges_own, weight(2), weight(3),
        ),
        (shape(BF, edge_count, width), shape(BF, count, width)) + (shape(F32, count, width),) * 3,
        scratch=(pltpu.VMEM((edge_count, width), BF),),
        flops=edge_count * 6 * unit,
    )
    square = shape(BF, count, width)
    grads = shape(BF, 7, 2, RING, width // RING, width // 4)
    rim = shape(BF, depth, width)
    edge_block = shape(BF, edge_count, width)
    returned, grad_pooled, pooled, hidden, grad_node_pre = stream(
        node_kernel,
        (target, margin, received, message, half, weight(5), grad_hidden),
        (slot_block, square, square, square, square),
        flops=count * 8 * unit,
    )
    crossed_back = from_partner(returned.reshape(slots, width))
    couple_back = route(crossed_back)
    grad_pooled, crossed_back = lax.optimization_barrier((grad_pooled, crossed_back))
    send, own, grad_edge_pre, by_source, by_target, grad_low, grad_high = stream(
        lambda *refs: grad_kernel(*refs, patches=patches, scale=scale),
        (
            side, nodes_own, grad_node_pre, grad_pooled, agg, edge_dst, weight(3), slope, edge_src, pooled,
            edges_own, hidden, cotangent, low, high, weight(0),
        ),
        (grads, grads, edge_block, square, square, rim, rim),
        scratch=[pltpu.VMEM((count, width), BF)],
        early=4,
    )
    other = from_partner(send)
    edge_grads, new_nodes, total = stream(
        rest_kernel,
        (
            grad_edge_pre, weight(2), hidden, weight(6), nodes_own, by_source, weight(0), by_target,
            weight(1), grad_node_pre, weight(4), cotangent,
        ),
        (edge_block, square, shape(F32, count, width)),
        flops=edge_count * 300 * unit,
    )

    def last(sums, back_low, back_high, back):
        (final,) = stream(
            last_kernel,
            (live, halo_rows, sums, back_low, back_high, back),
            (square,),
            flops=count * 2 * unit,
        )
        return final

    summed, node_grads = weight_sums(own, other, side, couple_back, total, (grad_low, grad_high), last)
    return (new_nodes[None], node_grads[None], edge_grads[None], summed)


def solution(mesh):
    return jax.shard_map(
        shards,
        mesh=mesh,
        in_specs=(
            P("mesh", "patch", None),
            P("mesh", "patch", None),
            P("mesh", "patch", None),
            P(),
            P("mesh", "patch"),
            P("mesh", "patch"),
            P("mesh", "patch"),
            P("mesh", "patch", None),
            P("mesh", "patch", None),
            P("mesh", "patch", None),
            P("mesh", "patch", None),
        ),
        out_specs=(
            P("mesh", "patch", None),
            P("mesh", "patch", None),
            P("mesh", "patch", None),
            P(None, "patch"),
        ),
        check_vma=False,
    )
```

```python
import math

import jax
import jax.numpy as jnp
from jax import lax
from jax.experimental import pallas as pl
from jax.experimental.pallas import tpu as pltpu
from jax.sharding import PartitionSpec as P

SLOT = 8
RING = 4
PLANE = RING * RING
TILE = 256
LIMIT = 61 * 2**20 - 2**16
BF = jnp.bfloat16
F32 = jnp.float32
I32 = jnp.int32
VMEM = pl.BlockSpec(memory_space=pltpu.VMEM)
SMEM = pl.BlockSpec(memory_space=pltpu.SMEM)


def dot(a, b):
    return jnp.dot(a, b, preferred_element_type=F32)


def dot_nt(a, b):
    return lax.dot_general(a, b, (((1,), (1,)), ((), ())), preferred_element_type=F32)


def column(row):
    return jnp.transpose(jnp.broadcast_to(row.astype(F32), (128, row.shape[1])))


def pick(col, count, value=None):
    base = lax.broadcasted_iota(I32, (col.shape[0], 128), 1).astype(F32)
    one = jnp.ones_like(base) if value is None else value
    parts = [jnp.where(col == base + float(k), one, 0.0).astype(BF) for k in range(0, count, 128)]
    return parts[0] if len(parts) == 1 else jnp.concatenate(parts, axis=1)


def pick_t(row, start, size, value=None):
    base = lax.broadcasted_iota(I32, (size, row.shape[1]), 0) + start
    one = jnp.ones(base.shape, F32) if value is None else jnp.broadcast_to(value, base.shape)
    return jnp.where(base == row, one, 0.0).astype(BF)


def row_order(place, width, patches):
    fine = width // patches
    depth = patches // PLANE
    row = lax.broadcasted_iota(I32, (width, width), 0)
    col = lax.broadcasted_iota(I32, (width, width), 1)
    dx, dy = row // (width // RING), (row // (width // PLANE)) % RING
    dz, offset = (row // fine) % depth, row % fine
    x, y = place % RING, (place // RING) % RING
    patch = dz * PLANE + (y + dy) % RING * RING + (x + dx) % RING
    return jnp.where(col == patch * fine + offset, 1.0, 0.0).astype(BF)


def tiles(count):
    return [slice(i, i + TILE) for i in range(0, count, TILE)]


class Far:
    def __init__(self, array, start=0, size=None):
        self.array = array
        self.start = start
        self.size = array.shape[0] if size is None else size


class Fetched:
    def __init__(self, copies, buffer, then):
        self.copies, self.buffer, self.then = copies, buffer, then
        self.started, self.waited = False, False
        self.shape = buffer.shape

    def start(self):
        if not self.started:
            self.started = True
            for copy in self.copies:
                copy.start()

    def wait(self):
        if not self.waited:
            self.waited = True
            self.start()
            for copy in self.copies:
                copy.wait()
            for later in self.then:
                later.start()

    def __getitem__(self, index):
        self.wait()
        return self.buffer[index]


def cuts(dims):
    if len(dims) > 3:
        return [(i, 1) for i in range(dims[0])]
    step = TILE if len(dims) == 2 and dims[0] % TILE == 0 else dims[0]
    return [(i, step) for i in range(0, dims[0], step)]


class Staged:
    def __init__(self, copies, buffer):
        self.copies, self.buffer, self.sent = copies, buffer, set()
        self.shape = buffer.shape

    def __getitem__(self, index):
        return self.buffer[index]

    def __setitem__(self, index, value):
        self.buffer[index] = value

    def flush(self, index=None):
        for i in range(len(self.copies)) if index is None else [index]:
            if i not in self.sent:
                self.copies[i].start()
                self.sent.add(i)

    def wait(self):
        for copy in self.copies:
            copy.wait()


def flush(self):
        if not self.sent:
            self.copy.start()
            self.sent = True


def flush(*refs):
    for ref in refs:
        ref.flush()


def cost(arrays, flops):
    size = sum(math.prod(a.shape) * a.dtype.itemsize for a in arrays)
    return pl.CostEstimate(flops=flops, bytes_accessed=size, transcendentals=0)


def call(kernel, args, outs):
    return pl.pallas_call(
        kernel,
        out_shape=tuple(outs),
        in_specs=[VMEM] * len(args),
        out_specs=tuple([VMEM] * len(outs)),
        compiler_params=pltpu.CompilerParams(vmem_limit_bytes=14 * 2**20),
        cost_estimate=cost(list(args) + list(outs), 0),
    )(*args)


def stream(kernel, args, outs, scratch=(), flops=0, early=None, local=False):
    args = [a if isinstance(a, Far) or a.ndim == 1 else Far(a) for a in args]
    far = [i for i, a in enumerate(args) if isinstance(a, Far)]
    arrays = [a.array if isinstance(a, Far) else a for a in args]
    moved = [((args[i].size,) + args[i].array.shape[1:], args[i].array.dtype) for i in far]
    moved += [] if local else [(o.shape, o.dtype) for o in outs]
    hbm = pl.BlockSpec(memory_space=pltpu.HBM)
    ins, made = len(args), len(args) + len(outs)
    early = len(far) if early is None else early

    def body(*refs):
        buffers, sems, rest = refs[made : made + len(moved)], refs[made + len(moved)], refs[made + len(moved) + 1 :]
        used = 0

        def copies(source, target, dims, first=0):
            nonlocal used
            made_here = []
            for start, size in cuts(dims):
                x, y = source.at[pl.ds(first + start, size)], target.at[pl.ds(start, size)]
                if first == 0 and size == dims[0]:
                    x, y = source, target
                made_here.append(pltpu.make_async_copy(x, y, sems.at[used]))
                used += 1
            return made_here

        reads, later = list(refs[:ins]), []
        for k, i in enumerate(far):
            held = copies(reads[i], buffers[k], moved[k][0], args[i].start)
            reads[i] = Fetched(held, buffers[k], later if k == early - 1 else [])
            if k < early:
                reads[i].start()
            else:
                later.append(reads[i])
        writes = list(refs[ins:made])
        if not local:
            for k, out in enumerate(writes):
                buffer = buffers[len(far) + k]
                writes[k] = Staged(copies(buffer, out, out.shape), buffer)
        kernel(*reads, *writes, *rest)
        if not local:
            flush(*writes)
        for i in far:
            reads[i].wait()
        if not local:
            for write in writes:
                write.wait()

    count = sum(len(cuts(dims)) for dims, _ in moved)
    return pl.pallas_call(
        body,
        out_shape=tuple(outs),
        in_specs=[hbm if isinstance(a, Far) else SMEM for a in args],
        out_specs=tuple([VMEM if local else hbm] * len(outs)),
        scratch_shapes=[pltpu.VMEM(*m) for m in moved] + [pltpu.SemaphoreType.DMA((count,))] + list(scratch),
        compiler_params=pltpu.CompilerParams(vmem_limit_bytes=14 * 2**20 if local else LIMIT),
        cost_estimate=cost(arrays + list(outs), flops),
    )(*arrays)


def shape(dtype, *dims):
    return jax.ShapeDtypeStruct(dims, dtype)


def send_kernel(rows_ref, count_ref, halo_ref, nodes_ref, out_ref, low_ref, high_ref, live_ref):
    slots = rows_ref.shape[1]
    patches = count_ref.shape[1]
    width = nodes_ref.shape[0]
    owner = lax.broadcasted_iota(I32, (patches, slots), 0)
    place = lax.broadcasted_iota(I32, (patches, slots), 1)
    repeat = jnp.where(place // SLOT == owner, 1.0, 0.0).astype(BF)
    counts = jnp.broadcast_to(count_ref[...].astype(F32), (8, patches)).astype(BF)
    spread = dot(counts, repeat)[:1].astype(I32)
    slot = lax.broadcasted_iota(I32, (1, slots), 1) % SLOT
    live = jnp.where(slot < spread, rows_ref[...], -1)
    live_ref[...] = live
    nodes = nodes_ref[...]
    depth = low_ref.shape[0]
    halo = dot(pick(column(halo_ref[...]), width), nodes).astype(BF)
    low_ref[...] = halo[:depth]
    high_ref[...] = halo[depth:]
    flush(low_ref, high_ref, live_ref)
    col = column(live)
    for i, r in enumerate(tiles(slots)):
        out_ref[i, 0] = dot(pick(col[r], width), nodes).astype(BF)
        out_ref.flush(i)


def edge_kernel(
    dst_ref, nodes_ref, wb_ref, na_ref, cot_ref, nsec_ref, src_ref, low_ref, high_ref, wa_ref, edges_ref, wc_ref,
    second_ref, slope_ref, agg_ref, msg_ref, half_ref, ghid_ref, hid_ref,
):
    count, width = nodes_ref.shape
    inner = edges_ref.shape[0] - edges_ref.shape[0] // 4
    dst = column(dst_ref[...])
    nodes = nodes_ref[...]
    src = column(src_ref[...])
    halo = jnp.concatenate([low_ref[...], high_ref[...]], axis=0)
    for r in tiles(edges_ref.shape[0]):
        if r.stop <= inner:
            feat = dot(pick(src[r], count), nodes).astype(BF)
        else:
            feat = dot(pick(src[r] - float(count), halo.shape[0]), halo).astype(BF)
        own = dot(pick(dst[r], count), nodes).astype(BF)
        pre = dot(own, wb_ref[...]) + dot(feat, wa_ref[...]) + dot(edges_ref[r], wc_ref[...])
        sigma = jax.nn.sigmoid(pre)
        hid_ref[r] = (pre * sigma).astype(BF)
        slope_ref[r] = (sigma * (1.0 + pre * (1.0 - sigma))).astype(BF)
    flush(slope_ref)
    for r in tiles(count):
        agg = dot(pick_t(dst_ref[...], r.start, TILE), hid_ref[...]).astype(BF)
        agg_ref[r] = agg
        msg_ref[r] = dot(agg, second_ref[...])
        half_ref[r] = dot(nodes_ref[r], na_ref[...])
        ghid_ref[r] = dot_nt(cot_ref[r], nsec_ref[...])


def put(ref, index, value, first):
    half = value.shape[1] // 2
    lane = half // 2
    step = value.shape[0] // RING
    fine = step // RING
    own = jnp.where(first, value[:, :half], value[:, half:]).astype(BF)
    send = jnp.where(first, value[:, half:], value[:, :half]).astype(BF)
    for buffer, part in ((ref.own, own), (ref.send, send)):
        for i in range(RING):
            buffer[index, 0, i] = part[i * step : (i + 1) * step, :lane]
            for j in range(RING):
                start = i * step + j * fine
                buffer[index, 1, j, i * fine : (i + 1) * fine] = part[start : start + fine, lane:]
        buffer.flush(index)


class Blocks:
    def __init__(self, own, send):
        self.own, self.send = own, send


def core_kernel(
    side_ref, target_ref, margin_ref, recv_ref, msg_ref, half_ref, nb_ref, ghid_ref, dst_ref, nodes_ref, agg_ref,
    esec_ref, slope_ref, src_ref, edges_ref, cot_ref, low_ref, high_ref, wa_ref,
    ret_ref, send_ref, own_ref, gedge_ref, bysrc_ref, bydst_ref, glow_ref, ghigh_ref, hid_ref, gnode_ref,
    turned_ref, pooled_ref, gpool_ref, *, patches, scale
):
    count, width = nodes_ref.shape
    inner = edges_ref.shape[0] - edges_ref.shape[0] // 4
    depth = low_ref.shape[0]
    first = side_ref[0] == 0
    target, margin = target_ref[...], margin_ref[...]
    for r in tiles(count):
        coupled = dot(pick_t(target, r.start, TILE, margin), recv_ref[...])
        pooled = (msg_ref[r] + coupled).astype(BF)
        pooled_ref[r] = pooled
        pre = half_ref[r] + dot(pooled, nb_ref[...])
        sigma = jax.nn.sigmoid(pre)
        hid_ref[r] = (pre * sigma).astype(BF)
        gnode = (ghid_ref[r] * (sigma * (1.0 + pre * (1.0 - sigma)))).astype(BF)
        gnode_ref[r] = gnode
        gpool_ref[r] = dot_nt(gnode, nb_ref[...]).astype(BF)
    flush(hid_ref, gnode_ref)
    gpool = gpool_ref[...]
    col, weight = column(target), column(margin)
    for i, r in enumerate(tiles(recv_ref.shape[0])):
        ret_ref[i, 0] = dot(pick(col[r], count, weight[r]), gpool).astype(BF)
        ret_ref.flush(i)
    dst_row, src_row = dst_ref[...], src_ref[...]
    dst = column(dst_row)
    for r in tiles(edges_ref.shape[0]):
        message = dot(pick(dst[r], count), gpool).astype(BF)
        gedge_ref[r] = (dot_nt(message, esec_ref[...]) * slope_ref[r].astype(F32)).astype(BF)
    flush(gedge_ref)
    for r in tiles(count):
        bydst_ref[r] = dot(pick_t(dst_row, r.start, TILE), gedge_ref[...]).astype(BF)
        bysrc_ref[r] = dot(pick_t(src_row[:, :inner], r.start, TILE), gedge_ref[:inner]).astype(BF)
    flush(bysrc_ref, bydst_ref)
    halo = dot(pick_t(src_row[:, inner:], count, 2 * depth), gedge_ref[inner:]).astype(BF)
    back = dot_nt(halo, wa_ref[...]).astype(BF)
    glow_ref[...] = back[:depth]
    ghigh_ref[...] = back[depth:]
    flush(glow_ref, ghigh_ref)
    order = row_order(side_ref[1], width, patches)
    blocks = Blocks(own_ref, send_ref)
    turned_ref[...] = dot_nt(order, nodes_ref[...]).astype(BF)
    put(blocks, 1, dot(turned_ref[...], bydst_ref[...]) * scale, first)
    rim = dot_nt(order, jnp.concatenate([low_ref[...], high_ref[...]], axis=0)).astype(BF)
    put(blocks, 0, (dot(turned_ref[...], bysrc_ref[...]) + dot(rim, halo)) * scale, first)
    put(blocks, 4, dot(turned_ref[...], gnode_ref[...]) * scale, first)
    pairs = ((2, edges_ref, gedge_ref), (3, agg_ref, gpool_ref), (5, pooled_ref, gnode_ref), (6, hid_ref, cot_ref))
    for index, left, right in pairs:
        turned = dot_nt(order, left[...]).astype(BF)
        put(blocks, index, dot(turned, right[...]) * scale, first)


def rest_kernel(
    gedge_ref, wc_ref, hid_ref, nsec_ref, nodes_ref, bysrc_ref, wa_ref, bydst_ref, wb_ref, gnode_ref, na_ref,
    cot_ref, edge_ref, new_ref, total_ref,
):
    for r in tiles(gedge_ref.shape[0]):
        edge_ref[r] = dot_nt(gedge_ref[r], wc_ref[...]).astype(BF)
    flush(edge_ref)
    for r in tiles(bysrc_ref.shape[0]):
        new_ref[r] = (nodes_ref[r].astype(F32) + dot(hid_ref[r], nsec_ref[...])).astype(BF)
    flush(new_ref)
    for r in tiles(bysrc_ref.shape[0]):
        total_ref[r] = (
            cot_ref[r].astype(F32)
            + dot_nt(bysrc_ref[r], wa_ref[...])
            + dot_nt(bydst_ref[r], wb_ref[...])
            + dot_nt(gnode_ref[r], na_ref[...])
        )


def last_kernel(live_ref, halo_ref, total_ref, low_ref, high_ref, back_ref, out_ref):
    halo_back = jnp.concatenate([low_ref[...], high_ref[...]], axis=0)
    for r in tiles(total_ref.shape[0]):
        out_ref[r] = (
            total_ref[r]
            + dot(pick_t(halo_ref[...], r.start, TILE), halo_back)
            + dot(pick_t(live_ref[...], r.start, TILE), back_ref[...])
        ).astype(BF)


def from_partner(value):
    return lax.ppermute(value, "mesh", [(0, 1), (1, 0)])


def shift(value, step):
    count = lax.axis_size("patch")
    return lax.ppermute(value, "patch", [(i, (i + step) % count) for i in range(count)])


def route(crossed):
    rows, width = crossed.shape
    patches = lax.axis_size("patch")
    crossed = crossed.reshape(patches, rows // patches, width)
    routed = lax.all_to_all(crossed, "patch", split_axis=0, concat_axis=0, tiled=True)
    return routed.reshape(rows, width)


def hop(value, dz=0, dy=0, dx=0):
    depth = lax.axis_size("patch") // PLANE
    pairs = []
    for p in range(depth * PLANE):
        z, y, x = p // PLANE, p // RING % RING, p % RING
        pairs.append((p, (z + dz) % depth * PLANE + (y + dy) % RING * RING + (x + dx) % RING))
    return lax.ppermute(value, "patch", pairs)


def join_kernel(own_ref, other_ref, *outs):
    for index, out in enumerate(outs):
        c, d = index // RING, index % RING
        out[...] = (own_ref[:, c, d].astype(F32) + other_ref[:, c, d].astype(F32)).astype(BF)


def total_of(refs):
    total = refs[0][...].astype(F32)
    for ref in refs[1:]:
        total = total + ref[...].astype(F32)
    return total


def plane_kernel(*refs):
    for c in range(2):
        total = total_of(refs[c * RING : (c + 1) * RING])
        fine = total.shape[1] // RING
        for d in range(RING):
            refs[(2 + c) * RING + d][...] = total[:, d * fine : (d + 1) * fine].astype(BF)


def depth_kernel(place_ref, *refs):
    ins, (keep_ref, send_ref, hold) = refs[: 2 * RING], refs[2 * RING :]
    depth = hold.shape[0]
    hold[...] = jnp.zeros(hold.shape, F32)
    for c in range(2):
        total = total_of(ins[c * RING : (c + 1) * RING])
        blocks, rows, lane = total.shape
        fine = rows // depth
        for block in range(blocks):
            for d in range(depth):
                hold[d, block * fine : (block + 1) * fine, c * lane : (c + 1) * lane] = total[
                    block, d * fine : (d + 1) * fine
                ]
    even = (place_ref[1] // PLANE) % 2 == 0
    for j in range(depth // 2):
        low, high = hold[2 * j], hold[2 * j + 1]
        keep_ref[j] = jnp.where(even, low, high)
        send_ref[j] = jnp.where(even, high, low).astype(BF)


def pair_kernel(place_ref, keep_ref, other_ref, *outs):
    mine = place_ref[1] // PLANE // 2
    for d, out in enumerate(outs):
        j = (mine + d) % len(outs)
        out[...] = keep_ref[j] + other_ref[j].astype(F32)


def sum_kernel(*refs):
    refs[-1][...] = total_of(refs[:-1])


def finish_kernel(place_ref, own_ref, other_ref, out_ref):
    first = place_ref[0] == 0
    lane = own_ref.shape[1]
    left = jnp.where(first, own_ref[...], other_ref[...])
    right = jnp.where(first, other_ref[...], own_ref[...])
    blocks, width = out_ref.shape
    for block in range(blocks):
        for k in range(width // (2 * lane)):
            row = block * (width // (2 * lane)) + k
            start = 2 * k * lane
            out_ref[block : block + 1, start : start + lane] = left[row : row + 1]
            out_ref[block : block + 1, start + lane : start + 2 * lane] = right[row : row + 1]


def small_call(kernel, place, args, outs, scratch=()):
    return pl.pallas_call(
        kernel,
        out_shape=tuple(outs),
        in_specs=[SMEM] + [VMEM] * len(args),
        out_specs=tuple([VMEM] * len(outs)),
        scratch_shapes=list(scratch),
        compiler_params=pltpu.CompilerParams(vmem_limit_bytes=14 * 2**20),
        cost_estimate=cost(list(args) + list(outs), 0),
    )(place, *args)


def spread(pieces, axes):
    return [
        pieces[c * RING + d] if d == 0 else hop(pieces[c * RING + d], **{axis: d})
        for c, axis in enumerate(axes)
        for d in range(RING)
    ]


def weight_sums(own, other, place, couple_back, total, rims, last):
    patches = lax.axis_size("patch")
    depth = patches // PLANE
    blocks, _, _, rows, lane = own.shape
    fine = rows // RING // depth
    pieces = stream(join_kernel, (own, other), (shape(BF, blocks, rows, lane),) * (2 * RING), local=True)
    pieces = spread(pieces, ("dx", "dy"))
    pieces[1], rims, total = lax.optimization_barrier((pieces[1], rims, total))
    back_low, back_high = shift(rims[1], 1), shift(rims[0], -1)
    pieces, couple_back, total, back_low, back_high = lax.optimization_barrier(
        (pieces, couple_back, total, back_low, back_high)
    )
    pieces = call(plane_kernel, pieces, (shape(BF, blocks, rows // RING, lane),) * (2 * RING))
    final = last(total, back_low, back_high, couple_back)
    pieces = spread(pieces, ("dy", "dx"))
    pieces, final = lax.optimization_barrier((pieces, final))
    padded = (blocks * fine + 15) // 16 * 16
    half = depth // 2
    keep, send = small_call(
        depth_kernel,
        place,
        pieces,
        (shape(F32, half, padded, 2 * lane), shape(BF, half, padded, 2 * lane)),
        scratch=(pltpu.VMEM((depth, padded, 2 * lane), F32),),
    )
    pairs = [(p, (p // PLANE ^ 1) * PLANE + p % PLANE) for p in range(patches)]
    other = lax.ppermute(send, "patch", pairs)
    pieces = small_call(pair_kernel, place, (keep, other), (shape(F32, padded, 2 * lane),) * half)
    pieces = [pieces[0]] + [hop(pieces[d], dz=2 * d) for d in range(1, half)]
    (own,) = call(sum_kernel, pieces, (shape(F32, padded, 2 * lane),))
    (result,) = small_call(
        finish_kernel, place, (own, from_partner(own)), (shape(F32, blocks, fine * 4 * lane),)
    )
    return result, final


def shards(
    nodes,
    edges,
    cot_nodes,
    weights,
    edge_src,
    edge_dst,
    halo_rows,
    couple_rows,
    couple_count,
    couple_target,
    couple_weight,
):
    nodes_own = nodes[0]
    edges_own = edges[0]
    cotangent = cot_nodes[0]
    count, width = nodes_own.shape
    edge_count = edges_own.shape[0]
    depth = halo_rows.shape[1] // 2
    patches = lax.axis_size("patch")
    slots = couple_rows.shape[2]
    scale = 1.0 / math.sqrt(2 * patches * edge_count)
    side = jnp.stack([lax.axis_index("mesh"), lax.axis_index("patch")]).astype(I32)
    target, margin = couple_target[0], couple_weight[0]
    unit = 2 * width * width

    def weight(block):
        return Far(weights, block * width, width)

    def weight(block):
        return Far(weights, block * width, width)

    slot_block = shape(BF, slots // TILE, 1, TILE, width)
    outgoing, low_out, high_out, live = stream(
        send_kernel,
        (couple_rows[0], couple_count[0], halo_rows, nodes_own),
        (slot_block, shape(BF, depth, width), shape(BF, depth, width), shape(I32, 1, slots)),
        flops=(slots + 2 * depth) * unit,
    )
    crossed = from_partner(outgoing.reshape(slots, width))
    low, high = shift(high_out, 1), shift(low_out, -1)
    crossed, low, high = lax.optimization_barrier((crossed, low, high))
    received = route(crossed)
    slope, agg, message, half, grad_hidden = stream(
        edge_kernel,
        (
            edge_dst, nodes_own, weight(1), weight(4), cotangent, weight(6), edge_src, low, high,
            weight(0), edges_own, weight(2), weight(3),
        ),
        (shape(BF, edge_count, width), shape(BF, count, width)) + (shape(F32, count, width),) * 3,
        scratch=(pltpu.VMEM((edge_count, width), BF),),
        flops=edge_count * 6 * unit,
    )
    square = shape(BF, count, width)
    grads = shape(BF, 7, 2, RING, width // RING, width // 4)
    rim = shape(BF, depth, width)
    edge_block = shape(BF, edge_count, width)
    (
        returned, send, own, grad_edge_pre, by_source, by_target, grad_low, grad_high, hidden, grad_node_pre
    ) = stream(
        lambda *refs: core_kernel(*refs, patches=patches, scale=scale),
        (
            side, target, margin, received, message, half, weight(5), grad_hidden, edge_dst, nodes_own, agg,
            weight(3), slope, edge_src, edges_own, cotangent, low, high, weight(0),
        ),
        (slot_block, grads, grads, edge_block, square, square, rim, rim, square, square),
        scratch=[pltpu.VMEM((count, width), BF)] * 3,
        flops=edge_count * 18 * unit,
        early=7,
    )
    crossed_back = from_partner(returned.reshape(slots, width))
    couple_back = route(crossed_back)
    other = from_partner(send)
    edge_grads, new_nodes, total = stream(
        rest_kernel,
        (
            grad_edge_pre, weight(2), hidden, weight(6), nodes_own, by_source, weight(0), by_target,
            weight(1), grad_node_pre, weight(4), cotangent,
        ),
        (edge_block, square, shape(F32, count, width)),
        flops=edge_count * 3 * unit,
    )

    def last(sums, back_low, back_high, back):
        (final,) = stream(
            last_kernel,
            (live, halo_rows, sums, back_low, back_high, back),
            (square,),
            flops=count * 2 * unit,
        )
        return final

    summed, node_grads = weight_sums(own, other, side, couple_back, total, (grad_low, grad_high), last)
    return (new_nodes[None], node_grads[None], edge_grads[None], summed)


def solution(mesh):
    return jax.shard_map(
        shards,
        mesh=mesh,
        in_specs=(
            P("mesh", "patch", None),
            P("mesh", "patch", None),
            P("mesh", "patch", None),
            P(),
            P("mesh", "patch"),
            P("mesh", "patch"),
            P("mesh", "patch"),
            P("mesh", "patch", None),
            P("mesh", "patch", None),
            P("mesh", "patch", None),
            P("mesh", "patch", None),
        ),
        out_specs=(
            P("mesh", "patch", None),
            P("mesh", "patch", None),
            P("mesh", "patch", None),
            P(None, "patch"),
        ),
        check_vma=False,
    )
```

```python
import math

import jax
import jax.numpy as jnp
from jax import lax
from jax.experimental import pallas as pl
from jax.experimental.pallas import tpu as pltpu
from jax.sharding import PartitionSpec as P

SLOT = 8
RING = 4
PLANE = RING * RING
TILE = 256
LIMIT = 61 * 2**20 - 2**16
BF = jnp.bfloat16
F32 = jnp.float32
I32 = jnp.int32
VMEM = pl.BlockSpec(memory_space=pltpu.VMEM)
SMEM = pl.BlockSpec(memory_space=pltpu.SMEM)


def dot(a, b):
    return jnp.dot(a, b, preferred_element_type=F32)


def dot_nt(a, b):
    return lax.dot_general(a, b, (((1,), (1,)), ((), ())), preferred_element_type=F32)


def column(row):
    return jnp.transpose(jnp.broadcast_to(row.astype(F32), (128, row.shape[1])))


def pick(col, count, value=None):
    base = lax.broadcasted_iota(I32, (col.shape[0], 128), 1).astype(F32)
    one = jnp.ones_like(base) if value is None else value
    parts = [jnp.where(col == base + float(k), one, 0.0).astype(BF) for k in range(0, count, 128)]
    return parts[0] if len(parts) == 1 else jnp.concatenate(parts, axis=1)


def pick_t(row, start, size, value=None):
    base = lax.broadcasted_iota(I32, (size, row.shape[1]), 0) + start
    one = jnp.ones(base.shape, F32) if value is None else jnp.broadcast_to(value, base.shape)
    return jnp.where(base == row, one, 0.0).astype(BF)


def row_order(place, width, patches):
    fine = width // patches
    depth = patches // PLANE
    row = lax.broadcasted_iota(I32, (width, width), 0)
    col = lax.broadcasted_iota(I32, (width, width), 1)
    dx, dy = row // (width // RING), (row // (width // PLANE)) % RING
    dz, offset = (row // fine) % depth, row % fine
    x, y = place % RING, (place // RING) % RING
    patch = dz * PLANE + (y + dy) % RING * RING + (x + dx) % RING
    return jnp.where(col == patch * fine + offset, 1.0, 0.0).astype(BF)


def tiles(count):
    return [slice(i, i + TILE) for i in range(0, count, TILE)]


class Far:
    def __init__(self, array, start=0, size=None):
        self.array = array
        self.start = start
        self.size = array.shape[0] if size is None else size


class Fetched:
    def __init__(self, copies, buffer, then):
        self.copies, self.buffer, self.then = copies, buffer, then
        self.started, self.waited = False, False
        self.shape = buffer.shape

    def start(self):
        if not self.started:
            self.started = True
            for copy in self.copies:
                copy.start()

    def wait(self):
        if not self.waited:
            self.waited = True
            self.start()
            for copy in self.copies:
                copy.wait()
            for later in self.then:
                later.start()

    def __getitem__(self, index):
        self.wait()
        return self.buffer[index]


def cuts(dims):
    if len(dims) > 3:
        return [(i, 1) for i in range(dims[0])]
    step = TILE if len(dims) == 2 and dims[0] % TILE == 0 else dims[0]
    return [(i, step) for i in range(0, dims[0], step)]


class Staged:
    def __init__(self, copies, buffer):
        self.copies, self.buffer, self.sent = copies, buffer, set()
        self.shape = buffer.shape

    def __getitem__(self, index):
        return self.buffer[index]

    def __setitem__(self, index, value):
        self.buffer[index] = value

    def flush(self, index=None):
        for i in range(len(self.copies)) if index is None else [index]:
            if i not in self.sent:
                self.copies[i].start()
                self.sent.add(i)

    def wait(self):
        for copy in self.copies:
            copy.wait()


def flush(self):
        if not self.sent:
            self.copy.start()
            self.sent = True


def flush(*refs):
    for ref in refs:
        ref.flush()


def cost(arrays, flops):
    size = sum(math.prod(a.shape) * a.dtype.itemsize for a in arrays)
    return pl.CostEstimate(flops=flops, bytes_accessed=size, transcendentals=0)


def call(kernel, args, outs):
    return pl.pallas_call(
        kernel,
        out_shape=tuple(outs),
        in_specs=[VMEM] * len(args),
        out_specs=tuple([VMEM] * len(outs)),
        compiler_params=pltpu.CompilerParams(vmem_limit_bytes=14 * 2**20),
        cost_estimate=cost(list(args) + list(outs), 0),
    )(*args)


def stream(kernel, args, outs, scratch=(), flops=0, early=None, local=False):
    args = [a if isinstance(a, Far) or a.ndim == 1 else Far(a) for a in args]
    far = [i for i, a in enumerate(args) if isinstance(a, Far)]
    arrays = [a.array if isinstance(a, Far) else a for a in args]
    moved = [((args[i].size,) + args[i].array.shape[1:], args[i].array.dtype) for i in far]
    moved += [] if local else [(o.shape, o.dtype) for o in outs]
    hbm = pl.BlockSpec(memory_space=pltpu.HBM)
    ins, made = len(args), len(args) + len(outs)
    early = len(far) if early is None else early

    def body(*refs):
        buffers, sems, rest = refs[made : made + len(moved)], refs[made + len(moved)], refs[made + len(moved) + 1 :]
        used = 0

        def copies(source, target, dims, first=0):
            nonlocal used
            made_here = []
            for start, size in cuts(dims):
                x, y = source.at[pl.ds(first + start, size)], target.at[pl.ds(start, size)]
                if first == 0 and size == dims[0]:
                    x, y = source, target
                made_here.append(pltpu.make_async_copy(x, y, sems.at[used]))
                used += 1
            return made_here

        reads, later = list(refs[:ins]), []
        for k, i in enumerate(far):
            held = copies(reads[i], buffers[k], moved[k][0], args[i].start)
            reads[i] = Fetched(held, buffers[k], later if k == early - 1 else [])
            if k < early:
                reads[i].start()
            else:
                later.append(reads[i])
        writes = list(refs[ins:made])
        if not local:
            for k, out in enumerate(writes):
                buffer = buffers[len(far) + k]
                writes[k] = Staged(copies(buffer, out, out.shape), buffer)
        kernel(*reads, *writes, *rest)
        if not local:
            flush(*writes)
        for i in far:
            reads[i].wait()
        if not local:
            for write in writes:
                write.wait()

    count = sum(len(cuts(dims)) for dims, _ in moved)
    return pl.pallas_call(
        body,
        out_shape=tuple(outs),
        in_specs=[hbm if isinstance(a, Far) else SMEM for a in args],
        out_specs=tuple([VMEM if local else hbm] * len(outs)),
        scratch_shapes=[pltpu.VMEM(*m) for m in moved] + [pltpu.SemaphoreType.DMA((count,))] + list(scratch),
        compiler_params=pltpu.CompilerParams(vmem_limit_bytes=14 * 2**20 if local else LIMIT),
        cost_estimate=cost(arrays + list(outs), flops),
    )(*arrays)


def shape(dtype, *dims):
    return jax.ShapeDtypeStruct(dims, dtype)


def send_kernel(rows_ref, count_ref, halo_ref, nodes_ref, out_ref, low_ref, high_ref, live_ref):
    slots = rows_ref.shape[1]
    patches = count_ref.shape[1]
    width = nodes_ref.shape[0]
    owner = lax.broadcasted_iota(I32, (patches, slots), 0)
    place = lax.broadcasted_iota(I32, (patches, slots), 1)
    repeat = jnp.where(place // SLOT == owner, 1.0, 0.0).astype(BF)
    counts = jnp.broadcast_to(count_ref[...].astype(F32), (8, patches)).astype(BF)
    spread = dot(counts, repeat)[:1].astype(I32)
    slot = lax.broadcasted_iota(I32, (1, slots), 1) % SLOT
    live = jnp.where(slot < spread, rows_ref[...], -1)
    live_ref[...] = live
    nodes = nodes_ref[...]
    depth = low_ref.shape[0]
    halo = dot(pick(column(halo_ref[...]), width), nodes).astype(BF)
    low_ref[...] = halo[:depth]
    high_ref[...] = halo[depth:]
    flush(low_ref, high_ref, live_ref)
    col = column(live)
    for i, r in enumerate(tiles(slots)):
        out_ref[i, 0] = dot(pick(col[r], width), nodes).astype(BF)
        out_ref.flush(i)


def edge_kernel(
    dst_ref, nodes_ref, wb_ref, na_ref, cot_ref, nsec_ref, src_ref, low_ref, high_ref, wa_ref, edges_ref, wc_ref,
    second_ref, slope_ref, agg_ref, msg_ref, half_ref, ghid_ref, hid_ref,
):
    count, width = nodes_ref.shape
    inner = edges_ref.shape[0] - edges_ref.shape[0] // 4
    dst = column(dst_ref[...])
    nodes = nodes_ref[...]
    src = column(src_ref[...])
    halo = jnp.concatenate([low_ref[...], high_ref[...]], axis=0)
    for r in tiles(edges_ref.shape[0]):
        if r.stop <= inner:
            feat = dot(pick(src[r], count), nodes).astype(BF)
        else:
            feat = dot(pick(src[r] - float(count), halo.shape[0]), halo).astype(BF)
        own = dot(pick(dst[r], count), nodes).astype(BF)
        pre = dot(own, wb_ref[...]) + dot(feat, wa_ref[...]) + dot(edges_ref[r], wc_ref[...])
        sigma = jax.nn.sigmoid(pre)
        hid_ref[r] = (pre * sigma).astype(BF)
        slope_ref[r] = (sigma * (1.0 + pre * (1.0 - sigma))).astype(BF)
    flush(slope_ref)
    for r in tiles(count):
        agg = dot(pick_t(dst_ref[...], r.start, TILE), hid_ref[...]).astype(BF)
        agg_ref[r] = agg
        msg_ref[r] = dot(agg, second_ref[...])
        half_ref[r] = dot(nodes_ref[r], na_ref[...])
        ghid_ref[r] = dot_nt(cot_ref[r], nsec_ref[...])


def put(ref, index, value, first):
    half = value.shape[1] // 2
    lane = half // 2
    step = value.shape[0] // RING
    fine = step // RING
    own = jnp.where(first, value[:, :half], value[:, half:]).astype(BF)
    send = jnp.where(first, value[:, half:], value[:, :half]).astype(BF)
    for buffer, part in ((ref.own, own), (ref.send, send)):
        for i in range(RING):
            buffer[index, 0, i] = part[i * step : (i + 1) * step, :lane]
            for j in range(RING):
                start = i * step + j * fine
                buffer[index, 1, j, i * fine : (i + 1) * fine] = part[start : start + fine, lane:]
        buffer.flush(index)


class Blocks:
    def __init__(self, own, send):
        self.own, self.send = own, send


def core_kernel(
    side_ref, target_ref, margin_ref, recv_ref, msg_ref, half_ref, nb_ref, ghid_ref, dst_ref, nodes_ref, agg_ref,
    esec_ref, slope_ref, src_ref, edges_ref, cot_ref, low_ref, high_ref, wa_ref,
    ret_ref, send_ref, own_ref, gedge_ref, bysrc_ref, bydst_ref, glow_ref, ghigh_ref, hid_ref, gnode_ref,
    turned_ref, pooled_ref, gpool_ref, *, patches, scale
):
    count, width = nodes_ref.shape
    inner = edges_ref.shape[0] - edges_ref.shape[0] // 4
    depth = low_ref.shape[0]
    first = side_ref[0] == 0
    target, margin = target_ref[...], margin_ref[...]
    for r in tiles(count):
        coupled = dot(pick_t(target, r.start, TILE, margin), recv_ref[...])
        pooled = (msg_ref[r] + coupled).astype(BF)
        pooled_ref[r] = pooled
        pre = half_ref[r] + dot(pooled, nb_ref[...])
        sigma = jax.nn.sigmoid(pre)
        hid_ref[r] = (pre * sigma).astype(BF)
        gnode = (ghid_ref[r] * (sigma * (1.0 + pre * (1.0 - sigma)))).astype(BF)
        gnode_ref[r] = gnode
        gpool_ref[r] = dot_nt(gnode, nb_ref[...]).astype(BF)
    flush(hid_ref, gnode_ref)
    gpool = gpool_ref[...]
    col, weight = column(target), column(margin)
    for i, r in enumerate(tiles(recv_ref.shape[0])):
        ret_ref[i, 0] = dot(pick(col[r], count, weight[r]), gpool).astype(BF)
        ret_ref.flush(i)
    dst_row, src_row = dst_ref[...], src_ref[...]
    dst = column(dst_row)
    for r in tiles(edges_ref.shape[0]):
        message = dot(pick(dst[r], count), gpool).astype(BF)
        gedge_ref[r] = (dot_nt(message, esec_ref[...]) * slope_ref[r].astype(F32)).astype(BF)
    flush(gedge_ref)
    for r in tiles(count):
        bydst_ref[r] = dot(pick_t(dst_row, r.start, TILE), gedge_ref[...]).astype(BF)
        bysrc_ref[r] = dot(pick_t(src_row[:, :inner], r.start, TILE), gedge_ref[:inner]).astype(BF)
    flush(bysrc_ref, bydst_ref)
    halo = dot(pick_t(src_row[:, inner:], count, 2 * depth), gedge_ref[inner:]).astype(BF)
    back = dot_nt(halo, wa_ref[...]).astype(BF)
    glow_ref[...] = back[:depth]
    ghigh_ref[...] = back[depth:]
    flush(glow_ref, ghigh_ref)
    order = row_order(side_ref[1], width, patches)
    blocks = Blocks(own_ref, send_ref)
    turned_ref[...] = dot_nt(order, nodes_ref[...]).astype(BF)
    put(blocks, 1, dot(turned_ref[...], bydst_ref[...]) * scale, first)
    rim = dot_nt(order, jnp.concatenate([low_ref[...], high_ref[...]], axis=0)).astype(BF)
    put(blocks, 0, (dot(turned_ref[...], bysrc_ref[...]) + dot(rim, halo)) * scale, first)
    put(blocks, 4, dot(turned_ref[...], gnode_ref[...]) * scale, first)
    pairs = ((2, edges_ref, gedge_ref), (3, agg_ref, gpool_ref), (5, pooled_ref, gnode_ref), (6, hid_ref, cot_ref))
    for index, left, right in pairs:
        turned = dot_nt(order, left[...]).astype(BF)
        put(blocks, index, dot(turned, right[...]) * scale, first)


def rest_kernel(
    gedge_ref, wc_ref, hid_ref, nsec_ref, nodes_ref, bysrc_ref, wa_ref, bydst_ref, wb_ref, gnode_ref, na_ref,
    cot_ref, edge_ref, new_ref, total_ref,
):
    for r in tiles(gedge_ref.shape[0]):
        edge_ref[r] = dot_nt(gedge_ref[r], wc_ref[...]).astype(BF)
    flush(edge_ref)
    for r in tiles(bysrc_ref.shape[0]):
        new_ref[r] = (nodes_ref[r].astype(F32) + dot(hid_ref[r], nsec_ref[...])).astype(BF)
    flush(new_ref)
    for r in tiles(bysrc_ref.shape[0]):
        total_ref[r] = (
            cot_ref[r].astype(F32)
            + dot_nt(bysrc_ref[r], wa_ref[...])
            + dot_nt(bydst_ref[r], wb_ref[...])
            + dot_nt(gnode_ref[r], na_ref[...])
        )


def last_kernel(live_ref, halo_ref, total_ref, low_ref, high_ref, back_ref, out_ref):
    halo_back = jnp.concatenate([low_ref[...], high_ref[...]], axis=0)
    for r in tiles(total_ref.shape[0]):
        out_ref[r] = (
            total_ref[r]
            + dot(pick_t(halo_ref[...], r.start, TILE), halo_back)
            + dot(pick_t(live_ref[...], r.start, TILE), back_ref[...])
        ).astype(BF)


def from_partner(value):
    return lax.ppermute(value, "mesh", [(0, 1), (1, 0)])


def shift(value, step):
    count = lax.axis_size("patch")
    return lax.ppermute(value, "patch", [(i, (i + step) % count) for i in range(count)])


def route(crossed):
    rows, width = crossed.shape
    patches = lax.axis_size("patch")
    crossed = crossed.reshape(patches, rows // patches, width)
    routed = lax.all_to_all(crossed, "patch", split_axis=0, concat_axis=0, tiled=True)
    return routed.reshape(rows, width)


def hop(value, dz=0, dy=0, dx=0):
    depth = lax.axis_size("patch") // PLANE
    pairs = []
    for p in range(depth * PLANE):
        z, y, x = p // PLANE, p // RING % RING, p % RING
        pairs.append((p, (z + dz) % depth * PLANE + (y + dy) % RING * RING + (x + dx) % RING))
    return lax.ppermute(value, "patch", pairs)


def join_kernel(own_ref, other_ref, *outs):
    for index, out in enumerate(outs):
        c, d = index // RING, index % RING
        out[...] = (own_ref[:, c, d].astype(F32) + other_ref[:, c, d].astype(F32)).astype(BF)


def total_of(refs):
    total = refs[0][...].astype(F32)
    for ref in refs[1:]:
        total = total + ref[...].astype(F32)
    return total


def plane_kernel(*refs):
    for c in range(2):
        total = total_of(refs[c * RING : (c + 1) * RING])
        fine = total.shape[1] // RING
        for d in range(RING):
            refs[(2 + c) * RING + d][...] = total[:, d * fine : (d + 1) * fine].astype(BF)


def depth_kernel(place_ref, *refs):
    ins, (keep_ref, send_ref, hold) = refs[: 2 * RING], refs[2 * RING :]
    depth = hold.shape[0]
    hold[...] = jnp.zeros(hold.shape, F32)
    for c in range(2):
        total = total_of(ins[c * RING : (c + 1) * RING])
        blocks, rows, lane = total.shape
        fine = rows // depth
        for block in range(blocks):
            for d in range(depth):
                hold[d, block * fine : (block + 1) * fine, c * lane : (c + 1) * lane] = total[
                    block, d * fine : (d + 1) * fine
                ]
    even = (place_ref[1] // PLANE) % 2 == 0
    for j in range(depth // 2):
        low, high = hold[2 * j], hold[2 * j + 1]
        keep_ref[j] = jnp.where(even, low, high)
        send_ref[j] = jnp.where(even, high, low).astype(BF)


def pair_kernel(place_ref, keep_ref, other_ref, *outs):
    mine = place_ref[1] // PLANE // 2
    for d, out in enumerate(outs):
        j = (mine + d) % len(outs)
        out[...] = keep_ref[j] + other_ref[j].astype(F32)


def sum_kernel(*refs):
    refs[-1][...] = total_of(refs[:-1])


def finish_kernel(place_ref, own_ref, other_ref, out_ref):
    first = place_ref[0] == 0
    lane = own_ref.shape[1]
    left = jnp.where(first, own_ref[...], other_ref[...])
    right = jnp.where(first, other_ref[...], own_ref[...])
    blocks, width = out_ref.shape
    for block in range(blocks):
        for k in range(width // (2 * lane)):
            row = block * (width // (2 * lane)) + k
            start = 2 * k * lane
            out_ref[block : block + 1, start : start + lane] = left[row : row + 1]
            out_ref[block : block + 1, start + lane : start + 2 * lane] = right[row : row + 1]


def small_call(kernel, place, args, outs, scratch=()):
    return pl.pallas_call(
        kernel,
        out_shape=tuple(outs),
        in_specs=[SMEM] + [VMEM] * len(args),
        out_specs=tuple([VMEM] * len(outs)),
        scratch_shapes=list(scratch),
        compiler_params=pltpu.CompilerParams(vmem_limit_bytes=14 * 2**20),
        cost_estimate=cost(list(args) + list(outs), 0),
    )(place, *args)


def spread(pieces, axes):
    return [
        pieces[c * RING + d] if d == 0 else hop(pieces[c * RING + d], **{axis: d})
        for c, axis in enumerate(axes)
        for d in range(RING)
    ]


def weight_sums(own, other, place, couple_back, total, last):
    patches = lax.axis_size("patch")
    depth = patches // PLANE
    blocks, _, _, rows, lane = own.shape
    fine = rows // RING // depth
    pieces = stream(join_kernel, (own, other), (shape(BF, blocks, rows, lane),) * (2 * RING), local=True)
    pieces = spread(pieces, ("dx", "dy"))
    pieces, couple_back, total = lax.optimization_barrier((pieces, couple_back, total))
    pieces = call(plane_kernel, pieces, (shape(BF, blocks, rows // RING, lane),) * (2 * RING))
    final = last(total, couple_back)
    pieces = spread(pieces, ("dy", "dx"))
    pieces, final = lax.optimization_barrier((pieces, final))
    padded = (blocks * fine + 15) // 16 * 16
    half = depth // 2
    keep, send = small_call(
        depth_kernel,
        place,
        pieces,
        (shape(F32, half, padded, 2 * lane), shape(BF, half, padded, 2 * lane)),
        scratch=(pltpu.VMEM((depth, padded, 2 * lane), F32),),
    )
    pairs = [(p, (p // PLANE ^ 1) * PLANE + p % PLANE) for p in range(patches)]
    other = lax.ppermute(send, "patch", pairs)
    pieces = small_call(pair_kernel, place, (keep, other), (shape(F32, padded, 2 * lane),) * half)
    pieces = [pieces[0]] + [hop(pieces[d], dz=2 * d) for d in range(1, half)]
    (own,) = call(sum_kernel, pieces, (shape(F32, padded, 2 * lane),))
    (result,) = small_call(
        finish_kernel, place, (own, from_partner(own)), (shape(F32, blocks, fine * 4 * lane),)
    )
    return result, final


def shards(
    nodes,
    edges,
    cot_nodes,
    weights,
    edge_src,
    edge_dst,
    halo_rows,
    couple_rows,
    couple_count,
    couple_target,
    couple_weight,
):
    nodes_own = nodes[0]
    edges_own = edges[0]
    cotangent = cot_nodes[0]
    count, width = nodes_own.shape
    edge_count = edges_own.shape[0]
    depth = halo_rows.shape[1] // 2
    patches = lax.axis_size("patch")
    slots = couple_rows.shape[2]
    scale = 1.0 / math.sqrt(2 * patches * edge_count)
    side = jnp.stack([lax.axis_index("mesh"), lax.axis_index("patch")]).astype(I32)
    target, margin = couple_target[0], couple_weight[0]
    unit = 2 * width * width

    def weight(block):
        return Far(weights, block * width, width)

    def weight(block):
        return Far(weights, block * width, width)

    slot_block = shape(BF, slots // TILE, 1, TILE, width)
    outgoing, low_out, high_out, live = stream(
        send_kernel,
        (couple_rows[0], couple_count[0], halo_rows, nodes_own),
        (slot_block, shape(BF, depth, width), shape(BF, depth, width), shape(I32, 1, slots)),
        flops=(slots + 2 * depth) * unit,
    )
    crossed = from_partner(outgoing.reshape(slots, width))
    low, high = shift(high_out, 1), shift(low_out, -1)
    crossed, low, high = lax.optimization_barrier((crossed, low, high))
    received = route(crossed)
    slope, agg, message, half, grad_hidden = stream(
        edge_kernel,
        (
            edge_dst, nodes_own, weight(1), weight(4), cotangent, weight(6), edge_src, low, high,
            weight(0), edges_own, weight(2), weight(3),
        ),
        (shape(BF, edge_count, width), shape(BF, count, width)) + (shape(F32, count, width),) * 3,
        scratch=(pltpu.VMEM((edge_count, width), BF),),
        flops=edge_count * 6 * unit,
    )
    square = shape(BF, count, width)
    grads = shape(BF, 7, 2, RING, width // RING, width // 4)
    rim = shape(BF, depth, width)
    edge_block = shape(BF, edge_count, width)
    (
        returned, send, own, grad_edge_pre, by_source, by_target, grad_low, grad_high, hidden, grad_node_pre
    ) = stream(
        lambda *refs: core_kernel(*refs, patches=patches, scale=scale),
        (
            side, target, margin, received, message, half, weight(5), grad_hidden, edge_dst, nodes_own, agg,
            weight(3), slope, edge_src, edges_own, cotangent, low, high, weight(0),
        ),
        (slot_block, grads, grads, edge_block, square, square, rim, rim, square, square),
        scratch=[pltpu.VMEM((count, width), BF)] * 3,
        flops=edge_count * 18 * unit,
        early=7,
    )
    crossed_back = from_partner(returned.reshape(slots, width))
    back_low, back_high = shift(grad_high, 1), shift(grad_low, -1)
    crossed_back, back_low, back_high = lax.optimization_barrier((crossed_back, back_low, back_high))
    couple_back = route(crossed_back)
    other = from_partner(send)
    edge_grads, new_nodes, total = stream(
        rest_kernel,
        (
            grad_edge_pre, weight(2), hidden, weight(6), nodes_own, by_source, weight(0), by_target,
            weight(1), grad_node_pre, weight(4), cotangent,
        ),
        (edge_block, square, shape(F32, count, width)),
        flops=edge_count * 3 * unit,
    )

    def last(sums, back):
        (final,) = stream(
            last_kernel,
            (live, halo_rows, sums, back_low, back_high, back),
            (square,),
            flops=count * 2 * unit,
        )
        return final

    summed, node_grads = weight_sums(own, other, side, couple_back, total, last)
    return (new_nodes[None], node_grads[None], edge_grads[None], summed)


def solution(mesh):
    return jax.shard_map(
        shards,
        mesh=mesh,
        in_specs=(
            P("mesh", "patch", None),
            P("mesh", "patch", None),
            P("mesh", "patch", None),
            P(),
            P("mesh", "patch"),
            P("mesh", "patch"),
            P("mesh", "patch"),
            P("mesh", "patch", None),
            P("mesh", "patch", None),
            P("mesh", "patch", None),
            P("mesh", "patch", None),
        ),
        out_specs=(
            P("mesh", "patch", None),
            P("mesh", "patch", None),
            P("mesh", "patch", None),
            P(None, "patch"),
        ),
        check_vma=False,
    )
```

```python
import math

import jax
import jax.numpy as jnp
from jax import lax
from jax.experimental import pallas as pl
from jax.experimental.pallas import tpu as pltpu
from jax.sharding import PartitionSpec as P

SLOT = 8
RING = 4
PLANE = RING * RING
TILE = 256
LIMIT = 61 * 2**20 - 2**16
BF = jnp.bfloat16
F32 = jnp.float32
I32 = jnp.int32
VMEM = pl.BlockSpec(memory_space=pltpu.VMEM)
SMEM = pl.BlockSpec(memory_space=pltpu.SMEM)


def dot(a, b):
    return jnp.dot(a, b, preferred_element_type=F32)


def dot_nt(a, b):
    return lax.dot_general(a, b, (((1,), (1,)), ((), ())), preferred_element_type=F32)


def column(row):
    return jnp.transpose(jnp.broadcast_to(row.astype(F32), (128, row.shape[1])))


def pick(col, count, value=None):
    base = lax.broadcasted_iota(I32, (col.shape[0], 128), 1).astype(F32)
    one = jnp.ones_like(base) if value is None else value
    parts = [jnp.where(col == base + float(k), one, 0.0).astype(BF) for k in range(0, count, 128)]
    return parts[0] if len(parts) == 1 else jnp.concatenate(parts, axis=1)


def pick_t(row, start, size, value=None):
    base = lax.broadcasted_iota(I32, (size, row.shape[1]), 0) + start
    one = jnp.ones(base.shape, F32) if value is None else jnp.broadcast_to(value, base.shape)
    return jnp.where(base == row, one, 0.0).astype(BF)


def row_order(place, width, patches):
    fine = width // patches
    depth = patches // PLANE
    row = lax.broadcasted_iota(I32, (width, width), 0)
    col = lax.broadcasted_iota(I32, (width, width), 1)
    dx, dy = row // (width // RING), (row // (width // PLANE)) % RING
    dz, offset = (row // fine) % depth, row % fine
    x, y = place % RING, (place // RING) % RING
    patch = dz * PLANE + (y + dy) % RING * RING + (x + dx) % RING
    return jnp.where(col == patch * fine + offset, 1.0, 0.0).astype(BF)


def tiles(count):
    return [slice(i, i + TILE) for i in range(0, count, TILE)]


class Far:
    def __init__(self, array, start=0, size=None):
        self.array = array
        self.start = start
        self.size = array.shape[0] if size is None else size


class Fetched:
    def __init__(self, copies, buffer, then):
        self.copies, self.buffer, self.then = copies, buffer, then
        self.started, self.waited = False, False
        self.shape = buffer.shape

    def start(self):
        if not self.started:
            self.started = True
            for copy in self.copies:
                copy.start()

    def wait(self):
        if not self.waited:
            self.waited = True
            self.start()
            for copy in self.copies:
                copy.wait()
            for later in self.then:
                later.start()

    def __getitem__(self, index):
        self.wait()
        return self.buffer[index]


def cuts(dims):
    if len(dims) > 3:
        return [(i, 1) for i in range(dims[0])]
    step = TILE if len(dims) == 2 and dims[0] % TILE == 0 else dims[0]
    return [(i, step) for i in range(0, dims[0], step)]


class Staged:
    def __init__(self, copies, buffer):
        self.copies, self.buffer, self.sent = copies, buffer, set()
        self.shape = buffer.shape

    def __getitem__(self, index):
        return self.buffer[index]

    def __setitem__(self, index, value):
        self.buffer[index] = value

    def flush(self, index=None):
        for i in range(len(self.copies)) if index is None else [index]:
            if i not in self.sent:
                self.copies[i].start()
                self.sent.add(i)

    def wait(self):
        for copy in self.copies:
            copy.wait()


def flush(self):
        if not self.sent:
            self.copy.start()
            self.sent = True


def flush(*refs):
    for ref in refs:
        ref.flush()


def cost(arrays, flops):
    size = sum(math.prod(a.shape) * a.dtype.itemsize for a in arrays)
    return pl.CostEstimate(flops=flops, bytes_accessed=size, transcendentals=0)


def call(kernel, args, outs):
    return pl.pallas_call(
        kernel,
        out_shape=tuple(outs),
        in_specs=[VMEM] * len(args),
        out_specs=tuple([VMEM] * len(outs)),
        compiler_params=pltpu.CompilerParams(vmem_limit_bytes=14 * 2**20),
        cost_estimate=cost(list(args) + list(outs), 0),
    )(*args)


def stream(kernel, args, outs, scratch=(), flops=0, early=None, local=False):
    args = [a if isinstance(a, Far) or a.ndim == 1 else Far(a) for a in args]
    far = [i for i, a in enumerate(args) if isinstance(a, Far)]
    arrays = [a.array if isinstance(a, Far) else a for a in args]
    moved = [((args[i].size,) + args[i].array.shape[1:], args[i].array.dtype) for i in far]
    moved += [] if local else [(o.shape, o.dtype) for o in outs]
    hbm = pl.BlockSpec(memory_space=pltpu.HBM)
    ins, made = len(args), len(args) + len(outs)
    early = len(far) if early is None else early

    def body(*refs):
        buffers, sems, rest = refs[made : made + len(moved)], refs[made + len(moved)], refs[made + len(moved) + 1 :]
        used = 0

        def copies(source, target, dims, first=0):
            nonlocal used
            made_here = []
            for start, size in cuts(dims):
                x, y = source.at[pl.ds(first + start, size)], target.at[pl.ds(start, size)]
                if first == 0 and size == dims[0]:
                    x, y = source, target
                made_here.append(pltpu.make_async_copy(x, y, sems.at[used]))
                used += 1
            return made_here

        reads, later = list(refs[:ins]), []
        for k, i in enumerate(far):
            held = copies(reads[i], buffers[k], moved[k][0], args[i].start)
            reads[i] = Fetched(held, buffers[k], later if k == early - 1 else [])
            if k < early:
                reads[i].start()
            else:
                later.append(reads[i])
        writes = list(refs[ins:made])
        if not local:
            for k, out in enumerate(writes):
                buffer = buffers[len(far) + k]
                writes[k] = Staged(copies(buffer, out, out.shape), buffer)
        kernel(*reads, *writes, *rest)
        if not local:
            flush(*writes)
        for i in far:
            reads[i].wait()
        if not local:
            for write in writes:
                write.wait()

    count = sum(len(cuts(dims)) for dims, _ in moved)
    return pl.pallas_call(
        body,
        out_shape=tuple(outs),
        in_specs=[hbm if isinstance(a, Far) else SMEM for a in args],
        out_specs=tuple([VMEM if local else hbm] * len(outs)),
        scratch_shapes=[pltpu.VMEM(*m) for m in moved] + [pltpu.SemaphoreType.DMA((count,))] + list(scratch),
        compiler_params=pltpu.CompilerParams(vmem_limit_bytes=14 * 2**20 if local else LIMIT),
        cost_estimate=cost(arrays + list(outs), flops),
    )(*arrays)


def shape(dtype, *dims):
    return jax.ShapeDtypeStruct(dims, dtype)


def send_kernel(rows_ref, count_ref, halo_ref, nodes_ref, out_ref, low_ref, high_ref, live_ref):
    slots = rows_ref.shape[1]
    patches = count_ref.shape[1]
    width = nodes_ref.shape[0]
    owner = lax.broadcasted_iota(I32, (patches, slots), 0)
    place = lax.broadcasted_iota(I32, (patches, slots), 1)
    repeat = jnp.where(place // SLOT == owner, 1.0, 0.0).astype(BF)
    counts = jnp.broadcast_to(count_ref[...].astype(F32), (8, patches)).astype(BF)
    spread = dot(counts, repeat)[:1].astype(I32)
    slot = lax.broadcasted_iota(I32, (1, slots), 1) % SLOT
    live = jnp.where(slot < spread, rows_ref[...], -1)
    live_ref[...] = live
    nodes = nodes_ref[...]
    depth = low_ref.shape[0]
    halo = dot(pick(column(halo_ref[...]), width), nodes).astype(BF)
    low_ref[...] = halo[:depth]
    high_ref[...] = halo[depth:]
    flush(low_ref, high_ref, live_ref)
    col = column(live)
    for i, r in enumerate(tiles(slots)):
        out_ref[i, 0] = dot(pick(col[r], width), nodes).astype(BF)
        out_ref.flush(i)


def edge_kernel(
    dst_ref, nodes_ref, wb_ref, na_ref, cot_ref, nsec_ref, src_ref, low_ref, high_ref, wa_ref, edges_ref, wc_ref,
    second_ref, slope_ref, agg_ref, msg_ref, half_ref, ghid_ref, hid_ref,
):
    count, width = nodes_ref.shape
    inner = edges_ref.shape[0] - edges_ref.shape[0] // 4
    dst = column(dst_ref[...])
    nodes = nodes_ref[...]
    src = column(src_ref[...])
    halo = jnp.concatenate([low_ref[...], high_ref[...]], axis=0)
    for r in tiles(edges_ref.shape[0]):
        if r.stop <= inner:
            feat = dot(pick(src[r], count), nodes).astype(BF)
        else:
            feat = dot(pick(src[r] - float(count), halo.shape[0]), halo).astype(BF)
        own = dot(pick(dst[r], count), nodes).astype(BF)
        pre = dot(own, wb_ref[...]) + dot(feat, wa_ref[...]) + dot(edges_ref[r], wc_ref[...])
        sigma = jax.nn.sigmoid(pre)
        hid_ref[r] = (pre * sigma).astype(BF)
        slope_ref[r] = (sigma * (1.0 + pre * (1.0 - sigma))).astype(BF)
    flush(slope_ref)
    for r in tiles(count):
        agg = dot(pick_t(dst_ref[...], r.start, TILE), hid_ref[...]).astype(BF)
        agg_ref[r] = agg
        msg_ref[r] = dot(agg, second_ref[...])
        half_ref[r] = dot(nodes_ref[r], na_ref[...])
        ghid_ref[r] = dot_nt(cot_ref[r], nsec_ref[...])


def put(ref, index, value, first):
    half = value.shape[1] // 2
    lane = half // 2
    step = value.shape[0] // RING
    fine = step // RING
    own = jnp.where(first, value[:, :half], value[:, half:]).astype(BF)
    send = jnp.where(first, value[:, half:], value[:, :half]).astype(BF)
    for buffer, part in ((ref.own, own), (ref.send, send)):
        for i in range(RING):
            buffer[index, 0, i] = part[i * step : (i + 1) * step, :lane]
            for j in range(RING):
                start = i * step + j * fine
                buffer[index, 1, j, i * fine : (i + 1) * fine] = part[start : start + fine, lane:]
        buffer.flush(index)


class Blocks:
    def __init__(self, own, send):
        self.own, self.send = own, send


def core_kernel(
    side_ref, target_ref, margin_ref, recv_ref, msg_ref, half_ref, nb_ref, ghid_ref, dst_ref, nodes_ref, agg_ref,
    esec_ref, slope_ref, src_ref, edges_ref, cot_ref, low_ref, high_ref, wa_ref,
    ret_ref, send_ref, own_ref, gedge_ref, bysrc_ref, bydst_ref, glow_ref, ghigh_ref, hid_ref, gnode_ref,
    turned_ref, pooled_ref, gpool_ref, *, patches, scale
):
    count, width = nodes_ref.shape
    inner = edges_ref.shape[0] - edges_ref.shape[0] // 4
    depth = low_ref.shape[0]
    first = side_ref[0] == 0
    target, margin = target_ref[...], margin_ref[...]
    for r in tiles(count):
        coupled = dot(pick_t(target, r.start, TILE, margin), recv_ref[...])
        pooled = (msg_ref[r] + coupled).astype(BF)
        pooled_ref[r] = pooled
        pre = half_ref[r] + dot(pooled, nb_ref[...])
        sigma = jax.nn.sigmoid(pre)
        hid_ref[r] = (pre * sigma).astype(BF)
        gnode = (ghid_ref[r] * (sigma * (1.0 + pre * (1.0 - sigma)))).astype(BF)
        gnode_ref[r] = gnode
        gpool_ref[r] = dot_nt(gnode, nb_ref[...]).astype(BF)
    flush(hid_ref, gnode_ref)
    gpool = gpool_ref[...]
    col, weight = column(target), column(margin)
    for i, r in enumerate(tiles(recv_ref.shape[0])):
        ret_ref[i, 0] = dot(pick(col[r], count, weight[r]), gpool).astype(BF)
        ret_ref.flush(i)
    dst_row, src_row = dst_ref[...], src_ref[...]
    dst = column(dst_row)
    for r in tiles(edges_ref.shape[0]):
        message = dot(pick(dst[r], count), gpool).astype(BF)
        gedge_ref[r] = (dot_nt(message, esec_ref[...]) * slope_ref[r].astype(F32)).astype(BF)
    flush(gedge_ref)
    for r in tiles(count):
        bydst_ref[r] = dot(pick_t(dst_row, r.start, TILE), gedge_ref[...]).astype(BF)
        bysrc_ref[r] = dot(pick_t(src_row[:, :inner], r.start, TILE), gedge_ref[:inner]).astype(BF)
    flush(bysrc_ref, bydst_ref)
    halo = dot(pick_t(src_row[:, inner:], count, 2 * depth), gedge_ref[inner:]).astype(BF)
    back = dot_nt(halo, wa_ref[...]).astype(BF)
    glow_ref[...] = back[:depth]
    ghigh_ref[...] = back[depth:]
    flush(glow_ref, ghigh_ref)
    order = row_order(side_ref[1], width, patches)
    blocks = Blocks(own_ref, send_ref)
    turned_ref[...] = dot_nt(order, nodes_ref[...]).astype(BF)
    put(blocks, 1, dot(turned_ref[...], bydst_ref[...]) * scale, first)
    rim = dot_nt(order, jnp.concatenate([low_ref[...], high_ref[...]], axis=0)).astype(BF)
    put(blocks, 0, (dot(turned_ref[...], bysrc_ref[...]) + dot(rim, halo)) * scale, first)
    put(blocks, 4, dot(turned_ref[...], gnode_ref[...]) * scale, first)
    pairs = ((2, edges_ref, gedge_ref), (3, agg_ref, gpool_ref), (5, pooled_ref, gnode_ref), (6, hid_ref, cot_ref))
    for index, left, right in pairs:
        turned = dot_nt(order, left[...]).astype(BF)
        put(blocks, index, dot(turned, right[...]) * scale, first)


def rest_kernel(
    gedge_ref, wc_ref, hid_ref, nsec_ref, nodes_ref, bysrc_ref, wa_ref, bydst_ref, wb_ref, gnode_ref, na_ref,
    cot_ref, edge_ref, new_ref, total_ref,
):
    for r in tiles(gedge_ref.shape[0]):
        edge_ref[r] = dot_nt(gedge_ref[r], wc_ref[...]).astype(BF)
    flush(edge_ref)
    for r in tiles(bysrc_ref.shape[0]):
        new_ref[r] = (nodes_ref[r].astype(F32) + dot(hid_ref[r], nsec_ref[...])).astype(BF)
    flush(new_ref)
    for r in tiles(bysrc_ref.shape[0]):
        total_ref[r] = (
            cot_ref[r].astype(F32)
            + dot_nt(bysrc_ref[r], wa_ref[...])
            + dot_nt(bydst_ref[r], wb_ref[...])
            + dot_nt(gnode_ref[r], na_ref[...])
        )


def last_kernel(live_ref, halo_ref, total_ref, low_ref, high_ref, back_ref, out_ref):
    halo_back = jnp.concatenate([low_ref[...], high_ref[...]], axis=0)
    for r in tiles(total_ref.shape[0]):
        out_ref[r] = (
            total_ref[r]
            + dot(pick_t(halo_ref[...], r.start, TILE), halo_back)
            + dot(pick_t(live_ref[...], r.start, TILE), back_ref[...])
        ).astype(BF)


def from_partner(value):
    return lax.ppermute(value, "mesh", [(0, 1), (1, 0)])


def shift(value, step):
    count = lax.axis_size("patch")
    return lax.ppermute(value, "patch", [(i, (i + step) % count) for i in range(count)])


def route(crossed):
    rows, width = crossed.shape
    patches = lax.axis_size("patch")
    crossed = crossed.reshape(patches, rows // patches, width)
    routed = lax.all_to_all(crossed, "patch", split_axis=0, concat_axis=0, tiled=True)
    return routed.reshape(rows, width)


def hop(value, dz=0, dy=0, dx=0):
    depth = lax.axis_size("patch") // PLANE
    pairs = []
    for p in range(depth * PLANE):
        z, y, x = p // PLANE, p // RING % RING, p % RING
        pairs.append((p, (z + dz) % depth * PLANE + (y + dy) % RING * RING + (x + dx) % RING))
    return lax.ppermute(value, "patch", pairs)


def join_kernel(own_ref, other_ref, *outs):
    for index, out in enumerate(outs):
        c, d = index // RING, index % RING
        out[...] = (own_ref[:, c, d].astype(F32) + other_ref[:, c, d].astype(F32)).astype(BF)


def total_of(refs):
    total = refs[0][...].astype(F32)
    for ref in refs[1:]:
        total = total + ref[...].astype(F32)
    return total


def relay_kernel(a_ref, b_ref, c_ref, d_ref, x_ref, y_ref):
    x_ref[...] = total_of((a_ref, b_ref)).astype(BF)
    y_ref[...] = total_of((c_ref, d_ref)).astype(BF)


def plane_kernel(*refs):
    ins = len(refs) - 2 * RING
    for c in range(2):
        total = total_of(refs[c * ins // 2 : (c + 1) * ins // 2])
        fine = total.shape[1] // RING
        for d in range(RING):
            refs[ins + c * RING + d][...] = total[:, d * fine : (d + 1) * fine].astype(BF)


def depth_kernel(place_ref, *refs):
    ins, (keep_ref, send_ref, hold) = refs[: 2 * RING], refs[2 * RING :]
    depth = hold.shape[0]
    hold[...] = jnp.zeros(hold.shape, F32)
    for c in range(2):
        total = total_of(ins[c * RING : (c + 1) * RING])
        blocks, rows, lane = total.shape
        fine = rows // depth
        for block in range(blocks):
            for d in range(depth):
                hold[d, block * fine : (block + 1) * fine, c * lane : (c + 1) * lane] = total[
                    block, d * fine : (d + 1) * fine
                ]
    even = (place_ref[1] // PLANE) % 2 == 0
    for j in range(depth // 2):
        low, high = hold[2 * j], hold[2 * j + 1]
        keep_ref[j] = jnp.where(even, low, high)
        send_ref[j] = jnp.where(even, high, low).astype(BF)


def pair_kernel(place_ref, keep_ref, other_ref, *outs):
    mine = place_ref[1] // PLANE // 2
    for d, out in enumerate(outs):
        j = (mine + d) % len(outs)
        out[...] = keep_ref[j] + other_ref[j].astype(F32)


def sum_kernel(*refs):
    refs[-1][...] = total_of(refs[:-1])


def finish_kernel(place_ref, own_ref, other_ref, out_ref):
    first = place_ref[0] == 0
    lane = own_ref.shape[1]
    left = jnp.where(first, own_ref[...], other_ref[...])
    right = jnp.where(first, other_ref[...], own_ref[...])
    blocks, width = out_ref.shape
    for block in range(blocks):
        for k in range(width // (2 * lane)):
            row = block * (width // (2 * lane)) + k
            start = 2 * k * lane
            out_ref[block : block + 1, start : start + lane] = left[row : row + 1]
            out_ref[block : block + 1, start + lane : start + 2 * lane] = right[row : row + 1]


def small_call(kernel, place, args, outs, scratch=()):
    return pl.pallas_call(
        kernel,
        out_shape=tuple(outs),
        in_specs=[SMEM] + [VMEM] * len(args),
        out_specs=tuple([VMEM] * len(outs)),
        scratch_shapes=list(scratch),
        compiler_params=pltpu.CompilerParams(vmem_limit_bytes=14 * 2**20),
        cost_estimate=cost(list(args) + list(outs), 0),
    )(place, *args)


def spread(pieces, axes):
    return [
        pieces[c * RING + d] if d == 0 else hop(pieces[c * RING + d], **{axis: d})
        for c, axis in enumerate(axes)
        for d in range(RING)
    ]


def weight_sums(own, other, place, couple_back, total, rims, last):
    patches = lax.axis_size("patch")
    depth = patches // PLANE
    blocks, _, _, rows, lane = own.shape
    fine = rows // RING // depth
    pieces = stream(join_kernel, (own, other), (shape(BF, blocks, rows, lane),) * (2 * RING), local=True)
    relay_x, relay_y = hop(pieces[2], dx=3), hop(pieces[RING + 2], dy=3)
    near_x, near_y = hop(pieces[1], dx=1), hop(pieces[RING + 1], dy=1)
    piece = shape(BF, blocks, rows, lane)
    mid_x, mid_y = call(relay_kernel, (pieces[3], relay_x, pieces[RING + 3], relay_y), (piece, piece))
    far_x, far_y = hop(mid_x, dx=3), hop(mid_y, dy=3)
    near_x, rims, total = lax.optimization_barrier((near_x, rims, total))
    back_low, back_high = shift(rims[1], 1), shift(rims[0], -1)
    pieces = [pieces[0], near_x, far_x, pieces[RING], near_y, far_y]
    pieces, couple_back, total, back_low, back_high = lax.optimization_barrier((pieces, couple_back, total, back_low, back_high))
    pieces = call(plane_kernel, pieces, (shape(BF, blocks, rows // RING, lane),) * (2 * RING))
    final = last(total, back_low, back_high, couple_back)
    pieces = spread(pieces, ("dy", "dx"))
    pieces, final = lax.optimization_barrier((pieces, final))
    padded = (blocks * fine + 15) // 16 * 16
    half = depth // 2
    keep, send = small_call(
        depth_kernel,
        place,
        pieces,
        (shape(F32, half, padded, 2 * lane), shape(BF, half, padded, 2 * lane)),
        scratch=(pltpu.VMEM((depth, padded, 2 * lane), F32),),
    )
    pairs = [(p, (p // PLANE ^ 1) * PLANE + p % PLANE) for p in range(patches)]
    other = lax.ppermute(send, "patch", pairs)
    pieces = small_call(pair_kernel, place, (keep, other), (shape(F32, padded, 2 * lane),) * half)
    pieces = [pieces[0]] + [hop(pieces[d], dz=2 * d) for d in range(1, half)]
    (own,) = call(sum_kernel, pieces, (shape(F32, padded, 2 * lane),))
    (result,) = small_call(
        finish_kernel, place, (own, from_partner(own)), (shape(F32, blocks, fine * 4 * lane),)
    )
    return result, final


def shards(
    nodes,
    edges,
    cot_nodes,
    weights,
    edge_src,
    edge_dst,
    halo_rows,
    couple_rows,
    couple_count,
    couple_target,
    couple_weight,
):
    nodes_own = nodes[0]
    edges_own = edges[0]
    cotangent = cot_nodes[0]
    count, width = nodes_own.shape
    edge_count = edges_own.shape[0]
    depth = halo_rows.shape[1] // 2
    patches = lax.axis_size("patch")
    slots = couple_rows.shape[2]
    scale = 1.0 / math.sqrt(2 * patches * edge_count)
    side = jnp.stack([lax.axis_index("mesh"), lax.axis_index("patch")]).astype(I32)
    target, margin = couple_target[0], couple_weight[0]
    unit = 2 * width * width

    def weight(block):
        return Far(weights, block * width, width)

    def weight(block):
        return Far(weights, block * width, width)

    slot_block = shape(BF, slots // TILE, 1, TILE, width)
    outgoing, low_out, high_out, live = stream(
        send_kernel,
        (couple_rows[0], couple_count[0], halo_rows, nodes_own),
        (slot_block, shape(BF, depth, width), shape(BF, depth, width), shape(I32, 1, slots)),
        flops=(slots + 2 * depth) * unit,
    )
    crossed = from_partner(outgoing.reshape(slots, width))
    low, high = shift(high_out, 1), shift(low_out, -1)
    crossed, low, high = lax.optimization_barrier((crossed, low, high))
    received = route(crossed)
    slope, agg, message, half, grad_hidden = stream(
        edge_kernel,
        (
            edge_dst, nodes_own, weight(1), weight(4), cotangent, weight(6), edge_src, low, high,
            weight(0), edges_own, weight(2), weight(3),
        ),
        (shape(BF, edge_count, width), shape(BF, count, width)) + (shape(F32, count, width),) * 3,
        scratch=(pltpu.VMEM((edge_count, width), BF),),
        flops=edge_count * 6 * unit,
    )
    square = shape(BF, count, width)
    grads = shape(BF, 7, 2, RING, width // RING, width // 4)
    rim = shape(BF, depth, width)
    edge_block = shape(BF, edge_count, width)
    (
        returned, send, own, grad_edge_pre, by_source, by_target, grad_low, grad_high, hidden, grad_node_pre
    ) = stream(
        lambda *refs: core_kernel(*refs, patches=patches, scale=scale),
        (
            side, target, margin, received, message, half, weight(5), grad_hidden, edge_dst, nodes_own, agg,
            weight(3), slope, edge_src, edges_own, cotangent, low, high, weight(0),
        ),
        (slot_block, grads, grads, edge_block, square, square, rim, rim, square, square),
        scratch=[pltpu.VMEM((count, width), BF)] * 3,
        flops=edge_count * 18 * unit,
        early=7,
    )
    crossed_back = from_partner(returned.reshape(slots, width))
    couple_back = route(crossed_back)
    other = from_partner(send)
    edge_grads, new_nodes, total = stream(
        rest_kernel,
        (
            grad_edge_pre, weight(2), hidden, weight(6), nodes_own, by_source, weight(0), by_target,
            weight(1), grad_node_pre, weight(4), cotangent,
        ),
        (edge_block, square, shape(F32, count, width)),
        flops=edge_count * 3 * unit,
    )

    def last(sums, back_low, back_high, back):
        (final,) = stream(
            last_kernel,
            (live, halo_rows, sums, back_low, back_high, back),
            (square,),
            flops=count * 2 * unit,
        )
        return final

    summed, node_grads = weight_sums(own, other, side, couple_back, total, (grad_low, grad_high), last)
    return (new_nodes[None], node_grads[None], edge_grads[None], summed)


def solution(mesh):
    return jax.shard_map(
        shards,
        mesh=mesh,
        in_specs=(
            P("mesh", "patch", None),
            P("mesh", "patch", None),
            P("mesh", "patch", None),
            P(),
            P("mesh", "patch"),
            P("mesh", "patch"),
            P("mesh", "patch"),
            P("mesh", "patch", None),
            P("mesh", "patch", None),
            P("mesh", "patch", None),
            P("mesh", "patch", None),
        ),
        out_specs=(
            P("mesh", "patch", None),
            P("mesh", "patch", None),
            P("mesh", "patch", None),
            P(None, "patch"),
        ),
        check_vma=False,
    )
```
